512 devices in a mesh: heads: 8 (over x, z_hi), tokens: 64 (over y, z_lo, core).
Axes of the slice: x: 4, y: 4, z: 16 (z_hi: 2, z_lo: 8; z = z_hi * 8 + z_lo), core: 2. Of those that a mesh axis runs over, the one named last changes fastest.
Arguments:
- queries: bfloat16 [128, 64, 576], P('heads', 'tokens'), may hold values from -40 to 40
- latent_keys: bfloat16 [65536, 576], P('tokens'), may hold values from -4 to 4
- index_queries: bfloat16 [64, 64, 128], P(None, 'heads'), may hold values from -4 to 4
- index_keys: bfloat16 [65536, 128], P('tokens'), may hold values from -8 to 8
- index_weights: float32 [64, 64], P(None, 'heads'), may hold values from 0 to 1.2
- positions: int32 [64], replicated, may hold values from 32768 to 65535
Outputs:
- index_query_grad: float32 [64, 64, 128], P(None, 'heads')
- index_weight_grad: float32 [64, 64], P(None, 'heads')
- index_key_grad: float32 [65536, 128], P('tokens')
The draws below stay inside these ranges and needn't reach their ends.
All inputs are finite; a program needn't handle non-finite values.
Results may differ from the reference program's by a relative error of at most 0.0026.
Values may be sent and summed in bfloat16 or wider, within the bound.
No kernel may reach another device: no remote copies, remote signals or barrier semaphores. Data moves between devices by JAX's collectives and lax.ppermute only.
A program may use at most 64 MiB of HBM per device.

```python
import jax
import jax.numpy as jnp
from jax import lax

H = 128
DL = 512
DR = 64
HI = 64
DI = 128
Q = 64
KEYS = 65536
GRAD_SCALE = 8192


def main_pair(key):
    folded = jax.random.fold_in(key, 11)
    first_key, second_key = jax.random.split(folded, 2)
    width = DL + DR
    query_spread = 2.5 * (192.0 / width) ** 0.5
    key_rows = jnp.clip(jax.random.normal(first_key, (KEYS, width), jnp.float32), -4.0, 4.0)
    query_rows = query_spread * jnp.clip(jax.random.normal(second_key, (H, Q, width), jnp.float32), -4.0, 4.0)
    return (query_rows, key_rows)


def index_pair(key):
    folded = jax.random.fold_in(key, 23)
    first_key, second_key = jax.random.split(folded, 2)
    key_rows = jnp.clip(jax.random.normal(first_key, (KEYS, DI), jnp.float32), -4.0, 4.0)
    query_rows = jnp.clip(jax.random.normal(second_key, (Q, HI, DI), jnp.float32), -4.0, 4.0)
    key_rows = 0.7 * key_rows
    return (query_rows, key_rows)


def draw_queries(key, part):
    return main_pair(key)[0].astype(jnp.bfloat16)


def draw_latent_keys(key, part):
    return main_pair(key)[1].astype(jnp.bfloat16)


def draw_index_queries(key, part):
    return index_pair(key)[0].astype(jnp.bfloat16)


def draw_index_keys(key, part):
    return index_pair(key)[1].astype(jnp.bfloat16)


def touch_ends(drawn, key, smallest, high):
    longest = drawn.shape.index(max(drawn.shape))
    spots = []
    for shift in (0, 1):
        where = [jax.random.randint(jax.random.fold_in(key, axis), (), 0, length) for axis, length in enumerate(drawn.shape)]
        where[longest] = (where[longest] + shift) % drawn.shape[longest]
        spots.append(tuple(where))
    return drawn.at[spots[0]].set(smallest).at[spots[1]].set(high)


def block_scale(stream_key, extent, shards, smallest, high):
    def one(dim, blocks):
        heights = jax.random.uniform(jax.random.fold_in(jax.random.fold_in(stream_key, 6), dim), (blocks,), jnp.float32, smallest / len(shards), high / len(shards))
        return jnp.repeat(jnp.exp(heights), extent[dim] // blocks).reshape((-1,) + (1,) * (len(extent) - dim - 1))

    level = one(*shards[0])
    for cut in shards[1:]:
        level = level * one(*cut)
    return level


def setup_inputs(seed: int = 0) -> dict:
    key_of = jax.random.split(jax.random.key(seed), 7)
    queries = draw_queries(jax.random.fold_in(key_of[6], 71), 0)
    latent_keys = draw_latent_keys(jax.random.fold_in(key_of[6], 71), 0)
    index_queries = draw_index_queries(jax.random.fold_in(key_of[6], 71), 0)
    index_keys = draw_index_keys(jax.random.fold_in(key_of[6], 71), 0)
    index_weights = jnp.clip(1.2 * jax.random.uniform(key_of[4], (Q, HI), jnp.float32) ** block_scale(key_of[4], (Q, HI), ((1, 8),), -0.2, 0.2), 0.0, 1.2)
    positions = touch_ends(jax.random.randint(key_of[5], (Q,), KEYS // 2, KEYS), jax.random.fold_in(key_of[5], 1), KEYS // 2, KEYS - 1).astype(jnp.int32)
    return {"queries": queries, "latent_keys": latent_keys, "index_queries": index_queries, "index_keys": index_keys, "index_weights": index_weights, "positions": positions}


softmax_scale = 192.0 ** -0.5
masked_value = -1.0e30


def reference(queries, latent_keys, index_queries, index_keys, index_weights, positions):
    key_index = jnp.arange(KEYS, dtype=jnp.int32)
    visible = key_index[None, :] <= positions[:, None]

    def head_step(running, head_query):
        scores = jnp.dot(head_query, latent_keys.T, preferred_element_type=jnp.float32) * softmax_scale
        scores = jnp.where(visible, scores, masked_value)
        row_max = jnp.max(scores, axis=1, keepdims=True)
        exponent = jnp.exp(scores - row_max)
        row_sum = jnp.sum(exponent, axis=1, keepdims=True)
        return running + exponent / row_sum, None

    summed, _ = lax.scan(head_step, jnp.zeros((Q, KEYS), jnp.float32), queries)
    target = summed / H

    index_scale = DI ** -0.5
    head_queries = jnp.transpose(index_queries, (1, 0, 2))
    head_weights = index_weights.T

    def index_step(running, head_pair):
        head_query, head_weight = head_pair
        active = jnp.dot(head_query, index_keys.T, preferred_element_type=jnp.float32) * index_scale
        return running + head_weight[:, None] * jnp.maximum(active, 0.0), None

    logits, _ = lax.scan(index_step, jnp.zeros((Q, KEYS), jnp.float32), (head_queries, head_weights))
    logits = jnp.where(visible, logits, masked_value)
    row_max = jnp.max(logits, axis=1, keepdims=True)
    exponent = jnp.exp(logits - row_max)
    index_probs = exponent / jnp.sum(exponent, axis=1, keepdims=True)
    dlogit = GRAD_SCALE * (index_probs - target)

    def grad_step(running, head_pair):
        head_query, head_weight = head_pair
        active = jnp.dot(head_query, index_keys.T, preferred_element_type=jnp.float32) * index_scale
        gate_grad = (dlogit * head_weight[:, None] * (active > 0.0)).astype(jnp.bfloat16)
        query_grad = jnp.dot(gate_grad, index_keys, preferred_element_type=jnp.float32) * index_scale
        weight_grad = jnp.sum(dlogit * jnp.maximum(active, 0.0), axis=1)
        key_grad = running + jnp.dot(gate_grad.T, head_query, preferred_element_type=jnp.float32) * index_scale
        return key_grad, (query_grad, weight_grad)

    key_grad, (query_grads, weight_grads) = lax.scan(grad_step, jnp.zeros((KEYS, DI), jnp.float32), (head_queries, head_weights))
    return jnp.transpose(query_grads, (1, 0, 2)), weight_grads.T, key_grad
```

```python
import jax
import jax.numpy as jnp
from jax import lax
from jax.sharding import PartitionSpec as P

H = 128
NX, NZH = 4, 2
NY, NZ, NC = 4, 8, 2

softmax_scale = 192.0 ** (-0.5)
masked_value = -1e30


def token_at(y, z, c):
    return (y * NZ + z) * NC + c


def head_at(x, z):
    return x * NZH + z


groups_z = [[token_at(y, z, c) for z in range(NZ)] for y in range(NY) for c in range(NC)]
groups_yc = [[token_at(y, z, c) for y in range(NY) for c in range(NC)] for z in range(NZ)]
groups_x = [[head_at(x, z) for x in range(NX)] for z in range(NZH)]
pairs_zh = [(head_at(x, z), head_at(x, 1 - z)) for x in range(NX) for z in range(NZH)]


def pairs_x(flip):
    return [(head_at(x, z), head_at(x ^ flip, z)) for x in range(NX) for z in range(NZH)]


def exchanged(parts, axis, groups):
    return lax.all_to_all(parts, axis, 0, 0, tiled=True, axis_index_groups=groups)


def gathered(value, axis, groups):
    copies = jnp.broadcast_to(value[None], (len(groups[0]), *value.shape))
    return exchanged(copies, axis, groups)


def x_scatter_sum(parts, x):
    total = lax.dynamic_index_in_dim(parts, x, 0, keepdims=False)
    for flip in range(1, NX):
        piece = lax.dynamic_index_in_dim(parts, x ^ flip, 0, keepdims=False)
        total = total + lax.ppermute(piece, "heads", pairs_x(flip))
    return total


def x_gather(piece, x):
    whole = jnp.broadcast_to(piece[None], (NX, *piece.shape))
    for flip in range(1, NX):
        other = lax.ppermute(piece, "heads", pairs_x(flip))
        whole = lax.dynamic_update_index_in_dim(whole, other, x ^ flip, 0)
    return whole


def both_zh(value):
    return value + lax.ppermute(value, "heads", pairs_zh)


def joined(stats):
    maximum = jnp.max(stats[:, 0], axis=0)
    total = jnp.sum(stats[:, 1] * jnp.exp(stats[:, 0] - maximum), axis=0)
    return jnp.stack([maximum, total])


def local(queries, latent_keys, index_queries, index_keys, index_weights, positions):
    heads_here, width = queries.shape[0], queries.shape[2]
    key_count = latent_keys.shape[0]
    query_count, index_heads, index_width = index_queries.shape
    loss_scale = key_count * lax.axis_size("tokens") // 8
    x = lax.axis_index("heads") // NZH
    key_index = lax.axis_index("tokens") * key_count + jnp.arange(key_count, dtype=jnp.int32)
    share_rows = query_count // NX

    along_z = gathered(queries.reshape(heads_here, width), "tokens", groups_z)
    rows = gathered(along_z, "tokens", groups_yc).reshape(-1, width)

    index_scale = index_width ** (-0.5)
    active = (
        jnp.einsum("qjd,kd->qjk", index_queries, index_keys, preferred_element_type=jnp.float32)
        * index_scale
    )
    rectified = jnp.maximum(active, 0.0)
    partial_logits = jnp.sum(index_weights[:, :, None] * rectified, axis=1)
    logits = both_zh(x_scatter_sum(partial_logits.reshape(NX, share_rows, key_count), x))
    share_positions = lax.dynamic_slice_in_dim(positions, x * share_rows, share_rows, 0)
    logits = jnp.where(key_index[None, :] <= share_positions[:, None], logits, masked_value)
    index_max = jnp.max(logits, axis=1)
    index_total = jnp.sum(jnp.exp(logits - index_max[:, None]), axis=1)

    row_positions = positions.reshape(NY, NZ, NC).transpose(0, 2, 1).reshape(query_count)
    visible = key_index[None, :] <= row_positions[:, None]
    scores = (
        jnp.einsum("rd,kd->rk", rows, latent_keys, preferred_element_type=jnp.float32)
        * softmax_scale
    ).reshape(query_count, heads_here, key_count)
    scores = jnp.where(visible[:, None, :], scores, masked_value)
    local_max = jnp.max(scores, axis=2)
    exponent = jnp.exp(scores - local_max[..., None])
    local_total = jnp.sum(exponent, axis=2)

    def lines(main, index):
        return jnp.concatenate([main.reshape(-1, 128), jnp.pad(index, (0, 128 - share_rows))[None]])

    stats = jnp.stack([lines(local_max, index_max), lines(local_total, index_total)])
    stats = joined(gathered(stats, "tokens", groups_z))
    stats = joined(gathered(stats, "tokens", groups_yc))
    maximum = stats[0, :-1].reshape(query_count, heads_here)
    total = stats[1, :-1].reshape(query_count, heads_here)
    index_max, index_total = stats[0, -1, :share_rows], stats[1, -1, :share_rows]

    weight = jnp.exp(local_max - maximum) / total
    partial_target = jnp.sum(exponent * weight[..., None], axis=1)
    partial_target = partial_target.reshape(NY, NC, NZ, key_count).transpose(0, 2, 1, 3)
    partial_target = partial_target.reshape(NX, share_rows, key_count)
    target = both_zh(exchanged(partial_target, "heads", groups_x).sum(axis=0)) / H
    index_probs = jnp.exp(logits - index_max[:, None]) / index_total[:, None]
    share_grad = loss_scale * (index_probs - target)
    dlogit = gathered(share_grad, "heads", groups_x).reshape(query_count, key_count)

    gate = (dlogit[:, None, :] * index_weights[:, :, None] * (active > 0.0)).astype(jnp.bfloat16)
    query_local = (
        jnp.einsum("qjk,kd->qjd", gate, index_keys, preferred_element_type=jnp.float32)
        * index_scale
    ).reshape(-1, 128)
    weight_local = jnp.sum(dlogit[:, None, :] * rectified, axis=2).reshape(-1, 128)
    key_local = (
        jnp.einsum("qjk,qjd->kd", gate, index_queries, preferred_element_type=jnp.float32)
        * index_scale
    )

    both = jnp.concatenate([query_local, weight_local])
    piece_rows = -(-len(both) // (NY * NC * 8)) * 8
    both = jnp.pad(both, ((0, piece_rows * NY * NC - len(both)), (0, 0)))
    piece = exchanged(both.reshape(NY * NC, piece_rows, 128), "tokens", groups_yc).sum(axis=0)
    piece = gathered(piece, "tokens", groups_z).sum(axis=0)
    both = gathered(piece, "tokens", groups_yc).reshape(-1, 128)
    query_lines = query_count * index_heads * index_width // 128
    query_grad = both[:query_lines].reshape(query_count, index_heads, index_width)
    weight_grad = both[query_lines : query_lines + query_count * index_heads // 128]
    weight_grad = weight_grad.reshape(query_count, index_heads)

    key_piece = both_zh(x_scatter_sum(key_local.reshape(NX, key_count // NX, index_width), x))
    key_grad = x_gather(key_piece, x).reshape(key_count, index_width)
    return (query_grad, weight_grad, key_grad)


def solution(mesh):
    placed = (
        P("heads", "tokens", None),
        P("tokens", None),
        P(None, "heads", None),
        P("tokens", None),
        P(None, "heads"),
        P(),
    )
    return jax.shard_map(
        local,
        mesh=mesh,
        in_specs=placed,
        out_specs=(P(None, "heads", None), P(None, "heads"), P("tokens", None)),
        check_vma=False,
    )
```

```python
import jax
import jax.numpy as jnp
from jax import lax
from jax.experimental import pallas as pl
from jax.experimental.pallas import tpu as pltpu
from jax.sharding import PartitionSpec as P

H = 128
NX, NZH = 4, 2
NY, NZ, NC = 4, 8, 2
NYC = NY * NC
GRAD_SCALE = 8192.0

softmax_scale = 192.0 ** (-0.5)
masked_value = -1e30
f32, bf16 = jnp.float32, jnp.bfloat16


def token_at(y, z, c):
    return (y * NZ + z) * NC + c


def head_at(x, z):
    return x * NZH + z


groups_z = [[token_at(y, z, c) for z in range(NZ)] for y in range(NY) for c in range(NC)]
groups_yc = [[token_at(y, z, c) for y in range(NY) for c in range(NC)] for z in range(NZ)]
groups_x = [[head_at(x, z) for x in range(NX)] for z in range(NZH)]
pairs_zh = [(head_at(x, z), head_at(x, 1 - z)) for x in range(NX) for z in range(NZH)]


def pairs_x(flip):
    return [(head_at(x, z), head_at(x ^ flip, z)) for x in range(NX) for z in range(NZH)]


def exchanged(parts, axis, groups):
    return lax.all_to_all(parts, axis, 0, 0, tiled=True, axis_index_groups=groups)


def gathered(value, axis, groups):
    copies = jnp.broadcast_to(value[None], (len(groups[0]), *value.shape))
    return exchanged(copies, axis, groups)


def diagonal(rows, lanes):
    return lax.broadcasted_iota(jnp.int32, (rows, lanes), 0) == lax.broadcasted_iota(
        jnp.int32, (rows, lanes), 1
    )


def as_row(column, lanes=128):
    return jnp.sum(jnp.where(diagonal(column.shape[0], lanes), column, 0.0), axis=0, keepdims=True)


def as_column(row, rows):
    return jnp.sum(jnp.where(diagonal(rows, row.shape[1]), row, 0.0), axis=1, keepdims=True)


def call(kernel, out_shape, grid=None, in_specs=None, out_specs=None, flops=0, moved=0):
    whole = {}
    if grid is not None:
        whole = dict(grid=grid, in_specs=in_specs, out_specs=out_specs)
    return pl.pallas_call(
        kernel,
        out_shape=out_shape,
        compiler_params=pltpu.CompilerParams(vmem_limit_bytes=48 << 20),
        cost_estimate=pl.CostEstimate(flops=flops, bytes_accessed=moved, transcendentals=0),
        **whole,
    )


def score_kernel(limit_ref, q_ref, k_ref, e_ref, m_ref, l_ref):
    b = pl.program_id(0)
    rows, keys = e_ref.shape
    heads = rows // NZ
    s = jnp.dot(q_ref[...], k_ref[...], preferred_element_type=f32) * softmax_scale
    row = lax.broadcasted_iota(jnp.int32, (rows, 1), 0)
    limit = jnp.zeros((rows, 1), jnp.int32)
    for z in range(NZ):
        here = (row >= z * heads) & (row < (z + 1) * heads)
        limit = jnp.where(here, limit_ref[b * NZ + z], limit)
    key = lax.broadcasted_iota(jnp.int32, (1, keys), 1)
    s = jnp.where(key <= limit, s, masked_value)
    m = jnp.max(s, axis=1, keepdims=True)
    e = jnp.exp(s - m)
    e_ref[...] = e
    m_ref[pl.ds(b, 1), :] = as_row(m)
    l_ref[pl.ds(b, 1), :] = as_row(jnp.sum(e, axis=1, keepdims=True))


def message_parts(ref, tokens, heads):
    block = ref[tokens * heads :, :].astype(f32)
    w = block[:, :heads] + block[:, heads : 2 * heads] + block[:, 2 * heads : 3 * heads]
    return ref[: tokens * heads, :], w


def index_dot(iq, ik):
    return lax.dot_general(iq, ik, (((1,), (1,)), ((), ())), preferred_element_type=f32)


def logits_kernel(heads, scale, limit_ref, ik_ref, *refs):
    messages, (logits_ref, stat_ref) = refs[:-2], refs[-2:]
    tokens, keys = logits_ref.shape
    ik = ik_ref[...]
    logits = jnp.zeros((tokens, keys), f32)
    for message in messages:
        for part in range(message.shape[0]):
            iq, w = message_parts(message.at[part], tokens, heads)
            active = index_dot(iq, ik)
            for j in range(heads):
                here = active[j * tokens : (j + 1) * tokens] * scale
                logits = logits + w[:, j : j + 1] * jnp.maximum(here, 0.0)
    key = lax.broadcasted_iota(jnp.int32, (1, keys), 1)
    logits = jnp.where(key <= limit_ref[...], logits, masked_value)
    m = jnp.max(logits, axis=1, keepdims=True)
    l = jnp.sum(jnp.exp(logits - m), axis=1, keepdims=True)
    logits_ref[...] = logits
    stat_ref[...] = jnp.concatenate([as_row(m), as_row(l), jnp.zeros((6, 128), f32)], axis=0)


def joined(stats):
    def one(m, l):
        top = jnp.max(m, axis=0)
        return top, jnp.sum(l * jnp.exp(m - top), axis=0)

    return (*one(stats[:, 0:8], stats[:, 8:16]), *one(stats[:, 16:17], stats[:, 17:18]))


def join_kernel(stats_ref, out_ref):
    lines = jnp.concatenate([*joined(stats_ref[...]), jnp.zeros((6, 128), f32)], axis=0)
    out_ref[...] = jnp.broadcast_to(lines[None], out_ref.shape)


def target_kernel(stats_ref, m_ref, e_ref, out_ref):
    b = pl.program_id(0)
    rows, keys = e_ref.shape
    m = stats_ref[:, pl.ds(b, 1), :]
    l = stats_ref[:, pl.ds(b + 8, 1), :]
    top = jnp.max(m, axis=0)
    total = jnp.sum(l * jnp.exp(m - top), axis=0)
    weight = as_column(jnp.exp(m_ref[pl.ds(b, 1), :] - top) / total, rows)
    part = jnp.sum((e_ref[...] * weight).reshape(NZ, rows // NZ, keys), axis=1)
    out_ref[...] = jnp.broadcast_to(part[None], out_ref.shape)


def grad_kernel(heads, scale, one_ref, two_ref, logits_ref, stats_ref, message_ref, ik_ref, d_ref, out_ref):
    tokens, keys = logits_ref.shape
    stats = stats_ref[...]
    _, _, top, total = joined(stats)
    probs = jnp.exp(logits_ref[...] - as_column(top, tokens)) / as_column(total, tokens)
    dlogit = GRAD_SCALE * (probs - (one_ref[...] + two_ref[...]) / H)
    d_ref[...] = dlogit
    iq, w = message_parts(message_ref, tokens, heads)
    ik = ik_ref[...]
    active = index_dot(iq, ik)
    row = lax.broadcasted_iota(jnp.int32, (tokens, 128), 0)
    place = row // (NC * NZ) * (NC * NZ) + row % NZ * NC + row // NZ % NC
    places = place == lax.broadcasted_iota(jnp.int32, (tokens, 128), 1)
    out_ref[tokens * heads :, :] = jnp.zeros((out_ref.shape[0] - tokens * heads, 128), f32)
    for j in range(heads):
        here = active[j * tokens : (j + 1) * tokens]
        gate = jnp.where(here > 0.0, dlogit * w[:, j : j + 1], 0.0).astype(bf16)
        grad = jnp.dot(gate, ik, preferred_element_type=f32) * scale
        for b in range(NYC):
            first = (b // NC) * (NZ * NC) + b % NC
            lines = pl.ds(first * heads + j, NZ, stride=NC * heads)
            out_ref[lines, :] = grad[b * NZ : (b + 1) * NZ]
        weight_grad = jnp.sum(dlogit * jnp.maximum(here * scale, 0.0), axis=1, keepdims=True)
        out_ref[tokens * heads + j : tokens * heads + j + 1, :] = jnp.sum(
            jnp.where(places, weight_grad, 0.0), axis=0, keepdims=True
        )


def key_kernel(heads, scale, d_ref, ik_ref, *refs):
    messages, out_ref = refs[:-1], refs[-1]
    tokens, keys = d_ref.shape
    dlogit, ik = d_ref[...], ik_ref[...]
    total = jnp.zeros((ik.shape[1], keys), f32)
    for message in messages:
        for part in range(message.shape[0]):
            iq, w = message_parts(message.at[part], tokens, heads)
            active = index_dot(iq, ik)
            gates = []
            for j in range(heads):
                here = active[j * tokens : (j + 1) * tokens]
                gates.append(jnp.where(here > 0.0, dlogit * w[:, j : j + 1], 0.0).astype(bf16))
            gate = jnp.concatenate(gates, axis=0)
            total = total + jnp.dot(iq.T, gate, preferred_element_type=f32)
    out_ref[...] = total.T * scale


def sum_kernel(parts_ref, out_ref):
    out_ref[...] = jnp.broadcast_to(jnp.sum(parts_ref[...], axis=0)[None], out_ref.shape)


def in_order(value):
    return jnp.swapaxes(value.reshape(NY, NZ, NC, *value.shape[1:]), 1, 2).reshape(value.shape)


def local(queries, latent_keys, index_queries, index_keys, index_weights, positions):
    heads_here, width = queries.shape[0], queries.shape[2]
    key_count = latent_keys.shape[0]
    query_count, index_heads, index_width = index_queries.shape
    index_scale = index_width ** (-0.5)
    shape = jax.ShapeDtypeStruct
    limit = in_order(positions - lax.axis_index("tokens") * key_count)

    along_z = gathered(queries.reshape(heads_here, width), "tokens", groups_z)

    high = lax.reduce_precision(index_weights, 8, 7)
    middle = lax.reduce_precision(index_weights - high, 8, 7)
    low = index_weights - high - middle
    lines = jnp.pad(in_order(jnp.concatenate([high, middle, low], axis=1)), ((0, 0), (0, 128 - 3 * index_heads)))
    by_head = in_order(index_queries).transpose(1, 0, 2)
    by_head = by_head.reshape(index_heads * query_count, index_width)
    mine = jnp.concatenate([by_head, lines.astype(bf16)])
    pair = jnp.stack([mine, lax.ppermute(mine, "heads", pairs_zh)])
    messages = [pair] + [lax.ppermute(pair, "heads", pairs_x(flip)) for flip in range(1, NX)]

    rows = gathered(along_z, "tokens", groups_yc).reshape(-1, width)
    row_count = rows.shape[0]
    block = row_count // NYC

    index_flops = 2 * query_count * index_heads * NX * NZH * key_count * index_width
    logits, index_stats = call(
        lambda *refs: logits_kernel(index_heads, index_scale, *refs),
        (shape((query_count, key_count), f32), shape((8, 128), f32)),
        flops=index_flops,
        moved=2 << 20,
    )(limit[:, None], index_keys, *messages)

    score_flops = 2 * row_count * key_count * width
    exponent, local_max, local_total = call(
        score_kernel,
        (shape((row_count, key_count), f32), shape((NYC, block), f32), shape((NYC, block), f32)),
        grid=(NYC,),
        in_specs=[
            pl.BlockSpec(memory_space=pltpu.SMEM),
            pl.BlockSpec((block, width), lambda b: (b, 0)),
            pl.BlockSpec((width, key_count), lambda b: (0, 0)),
        ],
        out_specs=[
            pl.BlockSpec((block, key_count), lambda b: (b, 0)),
            pl.BlockSpec((NYC, block), lambda b: (0, 0)),
            pl.BlockSpec((NYC, block), lambda b: (0, 0)),
        ],
        flops=score_flops,
        moved=7 << 20,
    )(limit, rows, latent_keys.T)

    stats = jnp.concatenate([local_max, local_total, index_stats])
    stats = gathered(stats, "tokens", groups_z)
    stats = call(join_kernel, shape((NYC, *stats.shape[1:]), f32))(stats)
    stats = exchanged(stats, "tokens", groups_yc)

    partial = call(
        target_kernel,
        shape((NX, query_count, key_count), f32),
        grid=(NYC,),
        in_specs=[
            pl.BlockSpec(stats.shape, lambda b: (0, 0, 0)),
            pl.BlockSpec((NYC, block), lambda b: (0, 0)),
            pl.BlockSpec((block, key_count), lambda b: (b, 0)),
        ],
        out_specs=pl.BlockSpec((NX, NZ, key_count), lambda b: (0, b, 0)),
        moved=5 << 20,
    )(stats, local_max, exponent)
    over_x = exchanged(partial, "heads", groups_x).sum(axis=0)
    other = lax.ppermute(over_x, "heads", pairs_zh)

    query_lines = query_count * index_heads
    piece_rows = -(-(query_lines + index_heads) // (NYC * 8)) * 8
    dlogit, both = call(
        lambda *refs: grad_kernel(index_heads, index_scale, *refs),
        (shape((query_count, key_count), f32), shape((piece_rows * NYC, 128), f32)),
        flops=index_flops // 4,
        moved=2 << 20,
    )(over_x, other, logits, stats, mine, index_keys)

    piece = exchanged(both.reshape(NYC, piece_rows, 128), "tokens", groups_yc)
    piece = call(sum_kernel, shape((NZ, piece_rows, 128), f32))(piece)
    piece = exchanged(piece, "tokens", groups_z)
    piece = call(sum_kernel, shape((NYC, piece_rows, 128), f32))(piece)
    both = exchanged(piece, "tokens", groups_yc).reshape(-1, 128)
    query_grad = both[:query_lines].reshape(query_count, index_heads, index_width)
    weight_grad = both[query_lines : query_lines + index_heads, :query_count].T

    key_grad = call(
        lambda *refs: key_kernel(index_heads, index_scale, *refs),
        shape((key_count, index_width), f32),
        flops=2 * index_flops,
        moved=3 << 20,
    )(dlogit, index_keys, *messages)
    return (query_grad, weight_grad, key_grad)


def solution(mesh):
    placed = (
        P("heads", "tokens", None),
        P("tokens", None),
        P(None, "heads", None),
        P("tokens", None),
        P(None, "heads"),
        P(),
    )
    return jax.shard_map(
        local,
        mesh=mesh,
        in_specs=placed,
        out_specs=(P(None, "heads", None), P(None, "heads"), P("tokens", None)),
        check_vma=False,
    )
```

```python
import jax
import jax.numpy as jnp
from jax import lax
from jax.experimental import pallas as pl
from jax.experimental.pallas import tpu as pltpu
from jax.sharding import PartitionSpec as P

H = 128
NX, NZH = 4, 2
NY, NZ, NC = 4, 8, 2
NYC = NY * NC
GRAD_SCALE = 8192.0
VMEM = 32 << 20

softmax_scale = 192.0 ** (-0.5)
masked_value = -1e30
f32, bf16 = jnp.float32, jnp.bfloat16


def token_at(y, z, c):
    return (y * NZ + z) * NC + c


def head_at(x, z):
    return x * NZH + z


all_y, all_z, all_c = range(NY), range(NZ), range(NC)
groups_z = [[token_at(y, z, c) for z in all_z] for y in all_y for c in all_c]
groups_z4 = [
    [token_at(y, half + z, c) for z in range(4)] for half in (0, 4) for y in all_y for c in all_c
]
groups_y = [[token_at(y, z, c) for y in all_y] for z in all_z for c in all_c]
groups_yc = [[token_at(y, z, c) for c in all_c for y in all_y] for z in all_z]
pairs_c = [(token_at(y, z, c), token_at(y, z, 1 - c)) for y in all_y for z in all_z for c in all_c]
pairs_z4 = [(token_at(y, z, c), token_at(y, z ^ 4, c)) for y in all_y for z in all_z for c in all_c]
groups_x = [[head_at(x, z) for x in range(NX)] for z in range(NZH)]
pairs_zh = [(head_at(x, z), head_at(x, 1 - z)) for x in range(NX) for z in range(NZH)]


def pairs_x(flip):
    return [(head_at(x, z), head_at(x ^ flip, z)) for x in range(NX) for z in range(NZH)]


def exchanged(parts, axis, groups):
    return lax.all_to_all(parts, axis, 0, 0, tiled=True, axis_index_groups=groups)


def gathered(value, axis, groups):
    copies = jnp.broadcast_to(value[None], (len(groups[0]), *value.shape))
    return exchanged(copies, axis, groups)


def diagonal(rows, lanes):
    return lax.broadcasted_iota(jnp.int32, (rows, lanes), 0) == lax.broadcasted_iota(
        jnp.int32, (rows, lanes), 1
    )


def as_row(column, lanes=128):
    return jnp.sum(jnp.where(diagonal(column.shape[0], lanes), column, 0.0), axis=0, keepdims=True)


def as_column(row, rows):
    return jnp.sum(jnp.where(diagonal(rows, row.shape[1]), row, 0.0), axis=1, keepdims=True)


def call(kernel, out_shape, flops=0, moved=0):
    return pl.pallas_call(
        kernel,
        out_shape=out_shape,
        compiler_params=pltpu.CompilerParams(vmem_limit_bytes=VMEM),
        cost_estimate=pl.CostEstimate(flops=flops, bytes_accessed=moved, transcendentals=0),
    )


def score_kernel(heads, limit_ref, q_ref, k_ref, e_ref, m_ref, l_ref):
    rows, keys = e_ref.shape
    block = rows // NY
    key = lax.broadcasted_iota(jnp.int32, (1, keys), 1)
    k = k_ref[...]
    for y in range(NY):
        lines = slice(y * block, (y + 1) * block)
        s = jnp.dot(q_ref[lines], k, preferred_element_type=f32) * softmax_scale
        s = jnp.where(key <= limit_ref[lines], s, masked_value)
        m = jnp.max(s, axis=1, keepdims=True)
        e = jnp.exp(s - m)
        e_ref[lines] = e
        m_ref[y : y + 1] = as_row(m)
        l_ref[y : y + 1] = as_row(jnp.sum(e, axis=1, keepdims=True))


def message_parts(ref, tokens, heads):
    block = ref[tokens * heads :, :].astype(f32)
    w = block[:, :heads] + block[:, heads : 2 * heads] + block[:, 2 * heads : 3 * heads]
    return ref[: tokens * heads, :], w


def index_dot(iq, ik):
    return lax.dot_general(iq, ik, (((1,), (1,)), ((), ())), preferred_element_type=f32)


def logits_kernel(heads, scale, message_ref, ik_ref, out_ref):
    tokens = out_ref.shape[0]
    iq, w = message_parts(message_ref, tokens, heads)
    active = index_dot(iq, ik_ref[...])
    logits = jnp.zeros(out_ref.shape, f32)
    for j in range(heads):
        here = active[j * tokens : (j + 1) * tokens] * scale
        logits = logits + w[:, j : j + 1] * jnp.maximum(here, 0.0)
    out_ref[...] = logits


def index_stats_kernel(limit_ref, one_ref, two_ref, logits_ref, stat_ref):
    key = lax.broadcasted_iota(jnp.int32, (1, logits_ref.shape[1]), 1)
    logits = jnp.where(key <= limit_ref[...], one_ref[...] + two_ref[...], masked_value)
    m = jnp.max(logits, axis=1, keepdims=True)
    l = jnp.sum(jnp.exp(logits - m), axis=1, keepdims=True)
    logits_ref[...] = logits
    stat_ref[...] = jnp.concatenate([as_row(m), as_row(l), jnp.zeros((6, 128), f32)], axis=0)


def joined(stats):
    def one(m, l):
        top = jnp.max(m, axis=0)
        return top, jnp.sum(l * jnp.exp(m - top), axis=0)

    return (*one(stats[:, 0:8], stats[:, 8:16]), *one(stats[:, 16:17], stats[:, 17:18]))


def join_kernel(stats_ref, out_ref):
    lines = jnp.concatenate([*joined(stats_ref[...]), jnp.zeros((6, 128), f32)], axis=0)
    out_ref[...] = jnp.broadcast_to(lines[None], out_ref.shape)


def target_kernel(core_ref, stats_ref, m_ref, own_ref, other_ref, out_ref):
    stats = stats_ref[...]
    top, total, _, _ = joined(stats)
    weights = jnp.exp(m_ref[...] - top) / total
    keys = out_ref.shape[1]
    half = out_ref.shape[0] // NC
    block = own_ref.shape[0] // NY
    own = core_ref[0]
    for y in range(NY):
        for core, e_ref in ((own, own_ref), (1 - own, other_ref)):
            row = jnp.where(core == 0, weights[y : y + 1], weights[NY + y : NY + y + 1])
            e = e_ref[y * block : (y + 1) * block] * as_column(row, block)
            part = jnp.sum(e.reshape(NZ, block // NZ, keys), axis=1)
            out_ref[pl.ds(pl.multiple_of(core * half + y * NZ, NZ), NZ), :] = part


def dlogit_kernel(one_ref, two_ref, logits_ref, stats_ref, out_ref):
    rows = logits_ref.shape[0]
    _, _, top, total = joined(stats_ref[...])
    probs = jnp.exp(logits_ref[...] - as_column(top, rows)) / as_column(total, rows)
    dlogit = GRAD_SCALE * (probs - (one_ref[...] + two_ref[...]) / H)
    out_ref[...] = jnp.broadcast_to(dlogit[None], out_ref.shape)


def grad_kernel(heads, scale, d_ref, message_ref, ik_ref, out_ref):
    dlogit = d_ref[...]
    tokens = dlogit.shape[0]
    iq, w = message_parts(message_ref, tokens, heads)
    ik = ik_ref[...]
    active = index_dot(iq, ik)
    row = lax.broadcasted_iota(jnp.int32, (tokens, 128), 0)
    place = row // NZ % NY * (NC * NZ) + row % NZ * NC + row // (NY * NZ)
    places = place == lax.broadcasted_iota(jnp.int32, (tokens, 128), 1)
    out_ref[tokens * heads :, :] = jnp.zeros((out_ref.shape[0] - tokens * heads, 128), f32)
    for j in range(heads):
        here = active[j * tokens : (j + 1) * tokens]
        gate = jnp.where(here > 0.0, dlogit * w[:, j : j + 1], 0.0).astype(bf16)
        grad = jnp.dot(gate, ik, preferred_element_type=f32) * scale
        for b in range(NYC):
            first = b % NY * (NZ * NC) + b // NY
            lines = pl.ds(first * heads + j, NZ, stride=NC * heads)
            out_ref[lines, :] = grad[b * NZ : (b + 1) * NZ]
        weight_grad = jnp.sum(dlogit * jnp.maximum(here * scale, 0.0), axis=1, keepdims=True)
        out_ref[tokens * heads + j : tokens * heads + j + 1, :] = jnp.sum(
            jnp.where(places, weight_grad, 0.0), axis=0, keepdims=True
        )


def key_kernel(heads, scale, d_ref, ik_ref, *refs):
    messages, out_ref = refs[:-1], refs[-1]
    dlogit, ik = d_ref[...], ik_ref[...]
    tokens, keys = dlogit.shape
    total = jnp.zeros((ik.shape[1], keys), f32)
    for message in messages:
        for part in range(message.shape[0]):
            iq, w = message_parts(message.at[part], tokens, heads)
            active = index_dot(iq, ik)
            gates = []
            for j in range(heads):
                here = active[j * tokens : (j + 1) * tokens]
                gates.append(jnp.where(here > 0.0, dlogit * w[:, j : j + 1], 0.0).astype(bf16))
            gate = jnp.concatenate(gates, axis=0)
            total = total + jnp.dot(iq.T, gate, preferred_element_type=f32)
    out_ref[...] = total.T * scale


def sum_kernel(parts_ref, out_ref):
    out_ref[...] = jnp.broadcast_to(jnp.sum(parts_ref[...], axis=0)[None], out_ref.shape)


def pair_kernel(one_ref, two_ref, out_ref):
    out_ref[...] = jnp.broadcast_to((one_ref[...] + two_ref[...])[None], out_ref.shape)


def in_order(value):
    return jnp.moveaxis(value.reshape(NY, NZ, NC, *value.shape[1:]), 2, 0).reshape(value.shape)


def x_scatter_sum(parts, x):
    total = lax.dynamic_index_in_dim(parts, x, 0, keepdims=False)
    for flip in range(1, NX):
        piece = lax.dynamic_index_in_dim(parts, x ^ flip, 0, keepdims=False)
        total = total + lax.ppermute(piece, "heads", pairs_x(flip))
    return total


def local(queries, latent_keys, index_queries, index_keys, index_weights, positions):
    heads_here, width = queries.shape[0], queries.shape[2]
    key_count = latent_keys.shape[0]
    query_count, index_heads, index_width = index_queries.shape
    index_scale = index_width ** (-0.5)
    share_rows = query_count // NX
    shape = jax.ShapeDtypeStruct
    x = lax.axis_index("heads") // NZH
    core = lax.axis_index("tokens") % NC
    limit = in_order(positions - lax.axis_index("tokens") * key_count)

    along_z = gathered(queries.reshape(heads_here, width), "tokens", groups_z)

    high = lax.reduce_precision(index_weights, 8, 7)
    middle = lax.reduce_precision(index_weights - high, 8, 7)
    low = index_weights - high - middle
    lines = in_order(jnp.concatenate([high, middle, low], axis=1))
    lines = jnp.pad(lines, ((0, 0), (0, 128 - 3 * index_heads)))
    by_head = in_order(index_queries).transpose(1, 0, 2)
    by_head = by_head.reshape(index_heads * query_count, index_width)
    mine = jnp.concatenate([by_head, lines.astype(bf16)])

    index_flops = 2 * query_count * index_heads * key_count * index_width
    partial = call(
        lambda *refs: logits_kernel(index_heads, index_scale, *refs),
        shape((query_count, key_count), f32),
        flops=index_flops,
        moved=1 << 20,
    )(mine, index_keys)
    along_z, partial = lax.optimization_barrier((along_z, partial))
    over_x = x_scatter_sum(partial.reshape(NX, share_rows, key_count), x)
    other = lax.ppermute(over_x, "heads", pairs_zh)
    share_limit = lax.dynamic_slice_in_dim(limit, x * share_rows, share_rows, 0)
    logits, index_stats = call(
        index_stats_kernel,
        (shape((share_rows, key_count), f32), shape((8, 128), f32)),
    )(share_limit[:, None], over_x, other)

    own_rows = gathered(along_z, "tokens", groups_y)
    other_rows = lax.ppermute(own_rows, "tokens", pairs_c)
    row_limit = jnp.repeat(limit.reshape(NC, -1), heads_here, axis=1)[:, :, None]
    row_count = row_limit.shape[1]
    score = call(
        lambda *refs: score_kernel(heads_here, *refs),
        (
            shape((row_count, key_count), f32),
            shape((NY, row_count // NY), f32),
            shape((NY, row_count // NY), f32),
        ),
        flops=2 * row_count * key_count * width,
        moved=4 << 20,
    )
    keys_t = latent_keys.T
    first_limit = jnp.where(core == 0, row_limit[0], row_limit[1])
    second_limit = jnp.where(core == 0, row_limit[1], row_limit[0])
    own_e, own_max, own_total = score(first_limit, own_rows.reshape(-1, width), keys_t)
    other_e, other_max, other_total = score(second_limit, other_rows.reshape(-1, width), keys_t)

    def by_core(own, other):
        return jnp.where(core == 0, jnp.concatenate([own, other]), jnp.concatenate([other, own]))

    local_max = by_core(own_max, other_max)
    stats = jnp.concatenate([local_max, by_core(own_total, other_total), index_stats])
    stats, mine = lax.optimization_barrier((stats, mine))
    pair = jnp.stack([mine, lax.ppermute(mine, "heads", pairs_zh)])
    stats = gathered(stats, "tokens", groups_z)
    stats = call(join_kernel, shape((NYC, *stats.shape[1:]), f32))(stats)
    stats = exchanged(stats, "tokens", groups_yc)

    partial = call(target_kernel, shape((query_count, key_count), f32), moved=5 << 20)(
        core.reshape(1), stats, local_max, own_e, other_e
    )
    partial, pair = lax.optimization_barrier((partial, pair))
    messages = [pair] + [lax.ppermute(pair, "heads", pairs_x(flip)) for flip in range(1, NX)]
    over_x = exchanged(partial.reshape(NX, share_rows, key_count), "heads", groups_x).sum(axis=0)
    other = lax.ppermute(over_x, "heads", pairs_zh)
    dlogit = call(dlogit_kernel, shape((NX, share_rows, key_count), f32))(
        over_x, other, logits, stats
    )
    dlogit = exchanged(dlogit, "heads", groups_x).reshape(query_count, key_count)

    query_lines = query_count * index_heads
    piece_rows = -(-(query_lines + index_heads) // (NYC * 8)) * 8
    both = call(
        lambda *refs: grad_kernel(index_heads, index_scale, *refs),
        shape((piece_rows * NYC, 128), f32),
        flops=2 * index_flops,
        moved=2 << 20,
    )(dlogit, mine, index_keys)

    piece = exchanged(both.reshape(NYC, piece_rows, 128), "tokens", groups_yc)
    piece = call(sum_kernel, shape((NZ // 2, piece_rows, 128), f32))(piece)
    piece = exchanged(piece, "tokens", groups_z4).sum(axis=0)
    other = lax.ppermute(piece, "tokens", pairs_z4)
    piece = call(pair_kernel, shape((NYC, piece_rows, 128), f32))(piece, other)
    both = exchanged(piece, "tokens", groups_yc).reshape(-1, 128)
    query_grad = both[:query_lines].reshape(query_count, index_heads, index_width)
    weight_grad = both[query_lines : query_lines + index_heads, :query_count].T

    key_grad = call(
        lambda *refs: key_kernel(index_heads, index_scale, *refs),
        shape((key_count, index_width), f32),
        flops=2 * index_flops * NX * NZH,
        moved=3 << 20,
    )(dlogit, index_keys, *messages)
    return (query_grad, weight_grad, key_grad)


def solution(mesh):
    placed = (
        P("heads", "tokens", None),
        P("tokens", None),
        P(None, "heads", None),
        P("tokens", None),
        P(None, "heads"),
        P(),
    )
    return jax.shard_map(
        local,
        mesh=mesh,
        in_specs=placed,
        out_specs=(P(None, "heads", None), P(None, "heads"), P("tokens", None)),
        check_vma=False,
    )
```

```python
import jax
import jax.numpy as jnp
from jax import lax
from jax.experimental import pallas as pl
from jax.experimental.pallas import tpu as pltpu
from jax.sharding import PartitionSpec as P

H = 128
NX, NZH = 4, 2
NY, NZ, NC = 4, 8, 2
NYC = NY * NC
GRAD_SCALE = 8192.0
VMEM = 12 << 20

softmax_scale = 192.0 ** (-0.5)
masked_value = -1e30
f32, bf16 = jnp.float32, jnp.bfloat16


def token_at(y, z, c):
    return (y * NZ + z) * NC + c


def head_at(x, z):
    return x * NZH + z


all_y, all_z, all_c = range(NY), range(NZ), range(NC)
groups_z = [[token_at(y, z, c) for z in all_z] for y in all_y for c in all_c]
groups_z4 = [
    [token_at(y, half + z, c) for z in range(4)] for half in (0, 4) for y in all_y for c in all_c
]
groups_yc = [[token_at(y, z, c) for c in all_c for y in all_y] for z in all_z]
pairs_z4 = [(token_at(y, z, c), token_at(y, z ^ 4, c)) for y in all_y for z in all_z for c in all_c]
groups_x = [[head_at(x, z) for x in range(NX)] for z in range(NZH)]
pairs_zh = [(head_at(x, z), head_at(x, 1 - z)) for x in range(NX) for z in range(NZH)]


def pairs_x(flip):
    return [(head_at(x, z), head_at(x ^ flip, z)) for x in range(NX) for z in range(NZH)]


def exchanged(parts, axis, groups):
    return lax.all_to_all(parts, axis, 0, 0, tiled=True, axis_index_groups=groups)


def gathered(value, axis, groups):
    copies = jnp.broadcast_to(value[None], (len(groups[0]), *value.shape))
    return exchanged(copies, axis, groups)


def diagonal(rows, lanes):
    return lax.broadcasted_iota(jnp.int32, (rows, lanes), 0) == lax.broadcasted_iota(
        jnp.int32, (rows, lanes), 1
    )


def as_row(column, lanes=128):
    return jnp.sum(jnp.where(diagonal(column.shape[0], lanes), column, 0.0), axis=0, keepdims=True)


def as_column(row, rows):
    return jnp.sum(jnp.where(diagonal(rows, row.shape[1]), row, 0.0), axis=1, keepdims=True)


def call(kernel, out_shape, flops=0, moved=0):
    return pl.pallas_call(
        kernel,
        out_shape=out_shape,
        compiler_params=pltpu.CompilerParams(vmem_limit_bytes=VMEM),
        cost_estimate=pl.CostEstimate(flops=flops, bytes_accessed=moved, transcendentals=0),
    )


def score_kernel(limit_ref, q_ref, k_ref, e_ref, m_ref, l_ref):
    rows, keys = e_ref.shape
    block = rows // NYC
    key = lax.broadcasted_iota(jnp.int32, (1, keys), 1)
    k = k_ref[...]
    for b in range(NYC):
        lines = slice(b * block, (b + 1) * block)
        s = jnp.dot(q_ref[lines], k, preferred_element_type=f32) * softmax_scale
        s = jnp.where(key <= limit_ref[lines], s, masked_value)
        m = jnp.max(s, axis=1, keepdims=True)
        e = jnp.exp(s - m)
        e_ref[lines] = e
        m_ref[b : b + 1] = as_row(m)
        l_ref[b : b + 1] = as_row(jnp.sum(e, axis=1, keepdims=True))


def message_parts(ref, tokens, heads):
    block = ref[tokens * heads :, :].astype(f32)
    w = block[:, :heads] + block[:, heads : 2 * heads] + block[:, 2 * heads : 3 * heads]
    return ref[: tokens * heads, :], w


def index_dot(iq, ik):
    return lax.dot_general(iq, ik, (((1,), (1,)), ((), ())), preferred_element_type=f32)


def logits_kernel(heads, scale, message_ref, ik_ref, out_ref):
    tokens = out_ref.shape[0]
    iq, w = message_parts(message_ref, tokens, heads)
    active = index_dot(iq, ik_ref[...])
    logits = jnp.zeros(out_ref.shape, f32)
    for j in range(heads):
        here = active[j * tokens : (j + 1) * tokens] * scale
        logits = logits + w[:, j : j + 1] * jnp.maximum(here, 0.0)
    out_ref[...] = logits


def index_stats_kernel(limit_ref, one_ref, two_ref, logits_ref, stat_ref):
    key = lax.broadcasted_iota(jnp.int32, (1, logits_ref.shape[1]), 1)
    logits = jnp.where(key <= limit_ref[...], one_ref[...] + two_ref[...], masked_value)
    m = jnp.max(logits, axis=1, keepdims=True)
    l = jnp.sum(jnp.exp(logits - m), axis=1, keepdims=True)
    logits_ref[...] = logits
    stat_ref[...] = jnp.concatenate([as_row(m), as_row(l), jnp.zeros((6, 128), f32)], axis=0)


def joined(stats):
    def one(m, l):
        top = jnp.max(m, axis=0)
        return top, jnp.sum(l * jnp.exp(m - top), axis=0)

    return (*one(stats[:, 0:8], stats[:, 8:16]), *one(stats[:, 16:17], stats[:, 17:18]))


def join_kernel(stats_ref, out_ref):
    lines = jnp.concatenate([*joined(stats_ref[...]), jnp.zeros((6, 128), f32)], axis=0)
    out_ref[...] = jnp.broadcast_to(lines[None], out_ref.shape)


def target_kernel(stats_ref, m_ref, e_ref, out_ref):
    top, total, _, _ = joined(stats_ref[...])
    weights = jnp.exp(m_ref[...] - top) / total
    keys = out_ref.shape[1]
    block = e_ref.shape[0] // NYC
    for b in range(NYC):
        e = e_ref[b * block : (b + 1) * block] * as_column(weights[b : b + 1], block)
        out_ref[b * NZ : (b + 1) * NZ] = jnp.sum(e.reshape(NZ, block // NZ, keys), axis=1)


def dlogit_kernel(one_ref, two_ref, logits_ref, stats_ref, out_ref):
    rows = logits_ref.shape[0]
    _, _, top, total = joined(stats_ref[...])
    probs = jnp.exp(logits_ref[...] - as_column(top, rows)) / as_column(total, rows)
    dlogit = GRAD_SCALE * (probs - (one_ref[...] + two_ref[...]) / H)
    out_ref[...] = jnp.broadcast_to(dlogit[None], out_ref.shape)


def grad_kernel(heads, scale, d_ref, message_ref, ik_ref, out_ref):
    dlogit = d_ref[...]
    tokens = dlogit.shape[0]
    iq, w = message_parts(message_ref, tokens, heads)
    ik = ik_ref[...]
    active = index_dot(iq, ik)
    row = lax.broadcasted_iota(jnp.int32, (tokens, 128), 0)
    place = row // NZ % NY * (NC * NZ) + row % NZ * NC + row // (NY * NZ)
    places = place == lax.broadcasted_iota(jnp.int32, (tokens, 128), 1)
    out_ref[tokens * heads :, :] = jnp.zeros((out_ref.shape[0] - tokens * heads, 128), f32)
    for j in range(heads):
        here = active[j * tokens : (j + 1) * tokens]
        gate = jnp.where(here > 0.0, dlogit * w[:, j : j + 1], 0.0).astype(bf16)
        grad = jnp.dot(gate, ik, preferred_element_type=f32) * scale
        for b in range(NYC):
            first = b % NY * (NZ * NC) + b // NY
            lines = pl.ds(first * heads + j, NZ, stride=NC * heads)
            out_ref[lines, :] = grad[b * NZ : (b + 1) * NZ]
        weight_grad = jnp.sum(dlogit * jnp.maximum(here * scale, 0.0), axis=1, keepdims=True)
        out_ref[tokens * heads + j : tokens * heads + j + 1, :] = jnp.sum(
            jnp.where(places, weight_grad, 0.0), axis=0, keepdims=True
        )


def key_kernel(heads, scale, d_ref, ik_ref, *refs):
    messages, out_ref = refs[:-1], refs[-1]
    dlogit, ik = d_ref[...], ik_ref[...]
    tokens, keys = dlogit.shape
    total = jnp.zeros((ik.shape[1], keys), f32)
    for message in messages:
        for part in range(message.shape[0]):
            iq, w = message_parts(message.at[part], tokens, heads)
            active = index_dot(iq, ik)
            gates = []
            for j in range(heads):
                here = active[j * tokens : (j + 1) * tokens]
                gates.append(jnp.where(here > 0.0, dlogit * w[:, j : j + 1], 0.0).astype(bf16))
            gate = jnp.concatenate(gates, axis=0)
            total = total + jnp.dot(iq.T, gate, preferred_element_type=f32)
    out_ref[...] = total.T * scale


def sum_kernel(parts_ref, out_ref):
    out_ref[...] = jnp.broadcast_to(jnp.sum(parts_ref[...], axis=0)[None], out_ref.shape)


def pair_kernel(one_ref, two_ref, out_ref):
    out_ref[...] = jnp.broadcast_to((one_ref[...] + two_ref[...])[None], out_ref.shape)


def in_order(value):
    return jnp.moveaxis(value.reshape(NY, NZ, NC, *value.shape[1:]), 2, 0).reshape(value.shape)


def x_scatter_sum(parts, x):
    total = lax.dynamic_index_in_dim(parts, x, 0, keepdims=False)
    for flip in range(1, NX):
        piece = lax.dynamic_index_in_dim(parts, x ^ flip, 0, keepdims=False)
        total = total + lax.ppermute(piece, "heads", pairs_x(flip))
    return total


def local(queries, latent_keys, index_queries, index_keys, index_weights, positions):
    heads_here, width = queries.shape[0], queries.shape[2]
    key_count = latent_keys.shape[0]
    query_count, index_heads, index_width = index_queries.shape
    index_scale = index_width ** (-0.5)
    share_rows = query_count // NX
    shape = jax.ShapeDtypeStruct
    x = lax.axis_index("heads") // NZH
    limit = in_order(positions - lax.axis_index("tokens") * key_count)

    along_z = gathered(queries.reshape(heads_here, width), "tokens", groups_z)

    high = lax.reduce_precision(index_weights, 8, 7)
    middle = lax.reduce_precision(index_weights - high, 8, 7)
    low = index_weights - high - middle
    lines = in_order(jnp.concatenate([high, middle, low], axis=1))
    lines = jnp.pad(lines, ((0, 0), (0, 128 - 3 * index_heads)))
    by_head = in_order(index_queries).transpose(1, 0, 2)
    by_head = by_head.reshape(index_heads * query_count, index_width)
    mine = jnp.concatenate([by_head, lines.astype(bf16)])

    index_flops = 2 * query_count * index_heads * key_count * index_width
    partial = call(
        lambda *refs: logits_kernel(index_heads, index_scale, *refs),
        shape((query_count, key_count), f32),
        flops=index_flops,
        moved=1 << 20,
    )(mine, index_keys)
    over_x = x_scatter_sum(partial.reshape(NX, share_rows, key_count), x)
    along_z, over_x = lax.optimization_barrier((along_z, over_x))
    other = lax.ppermute(over_x, "heads", pairs_zh)
    rows = gathered(along_z, "tokens", groups_yc).reshape(-1, width)
    rows, other = lax.optimization_barrier((rows, other))
    share_limit = lax.dynamic_slice_in_dim(limit, x * share_rows, share_rows, 0)
    logits, index_stats = call(
        index_stats_kernel,
        (shape((share_rows, key_count), f32), shape((8, 128), f32)),
    )(share_limit[:, None], over_x, other)

    row_count = rows.shape[0]
    lines_shape = shape((NYC, row_count // NYC), f32)
    exponent, local_max, local_total = call(
        score_kernel,
        (shape((row_count, key_count), f32), lines_shape, lines_shape),
        flops=2 * row_count * key_count * width,
        moved=4 << 20,
    )(jnp.repeat(limit, heads_here)[:, None], rows, latent_keys.T)

    stats = jnp.concatenate([local_max, local_total, index_stats])
    stats = gathered(stats, "tokens", groups_z)
    stats = call(join_kernel, shape((NYC, *stats.shape[1:]), f32))(stats)
    stats, sent = lax.optimization_barrier((stats, mine))
    swapped = lax.ppermute(sent, "heads", pairs_zh)
    stats = exchanged(stats, "tokens", groups_yc)

    partial = call(target_kernel, shape((query_count, key_count), f32), moved=5 << 20)(
        stats, local_max, exponent
    )
    over_x = exchanged(partial.reshape(NX, share_rows, key_count), "heads", groups_x).sum(axis=0)
    other = lax.ppermute(over_x, "heads", pairs_zh)
    other, swapped = lax.optimization_barrier((other, swapped))
    pair = jnp.stack([mine, swapped])
    messages = [pair] + [lax.ppermute(pair, "heads", pairs_x(flip)) for flip in range(1, NX)]
    dlogit = call(dlogit_kernel, shape((NX, share_rows, key_count), f32))(
        over_x, other, logits, stats
    )
    dlogit = exchanged(dlogit, "heads", groups_x).reshape(query_count, key_count)
    dlogit, messages[1] = lax.optimization_barrier((dlogit, messages[1]))

    query_lines = query_count * index_heads
    piece_rows = -(-(query_lines + index_heads) // (NYC * 8)) * 8
    both = call(
        lambda *refs: grad_kernel(index_heads, index_scale, *refs),
        shape((piece_rows * NYC, 128), f32),
        flops=2 * index_flops,
        moved=2 << 20,
    )(dlogit, mine, index_keys)

    piece = exchanged(both.reshape(NYC, piece_rows, 128), "tokens", groups_yc)
    piece, messages[2] = lax.optimization_barrier((piece, messages[2]))
    piece = call(sum_kernel, shape((NZ // 2, piece_rows, 128), f32))(piece)
    piece = exchanged(piece, "tokens", groups_z4).sum(axis=0)
    other = lax.ppermute(piece, "tokens", pairs_z4)
    piece = call(pair_kernel, shape((NYC, piece_rows, 128), f32))(piece, other)
    both = exchanged(piece, "tokens", groups_yc).reshape(-1, 128)
    query_grad = both[:query_lines].reshape(query_count, index_heads, index_width)
    weight_grad = both[query_lines : query_lines + index_heads, :query_count].T

    key_grad = call(
        lambda *refs: key_kernel(index_heads, index_scale, *refs),
        shape((key_count, index_width), f32),
        flops=2 * index_flops * NX * NZH,
        moved=3 << 20,
    )(dlogit, index_keys, *messages)
    return (query_grad, weight_grad, key_grad)


def solution(mesh):
    placed = (
        P("heads", "tokens", None),
        P("tokens", None),
        P(None, "heads", None),
        P("tokens", None),
        P(None, "heads"),
        P(),
    )
    return jax.shard_map(
        local,
        mesh=mesh,
        in_specs=placed,
        out_specs=(P(None, "heads", None), P(None, "heads"), P("tokens", None)),
        check_vma=False,
    )
```

```python
import jax
import jax.numpy as jnp
from jax import lax
from jax.experimental import pallas as pl
from jax.experimental.pallas import tpu as pltpu
from jax.sharding import PartitionSpec as P

H = 128
NX, NZH = 4, 2
NY, NZ, NC = 4, 8, 2
NYC = NY * NC
GRAD_SCALE = 8192.0
VMEM = 12 << 20

softmax_scale = 192.0 ** (-0.5)
masked_value = -1e30
f32, bf16 = jnp.float32, jnp.bfloat16


def token_at(y, z, c):
    return (y * NZ + z) * NC + c


def head_at(x, z):
    return x * NZH + z


all_y, all_z, all_c = range(NY), range(NZ), range(NC)
groups_z = [[token_at(y, z, c) for z in all_z] for y in all_y for c in all_c]
groups_z4 = [
    [token_at(y, half + z, c) for z in range(4)] for half in (0, 4) for y in all_y for c in all_c
]
pairs_c = [(token_at(y, z, c), token_at(y, z, 1 - c)) for y in all_y for z in all_z for c in all_c]
groups_yc = [[token_at(y, z, c) for c in all_c for y in all_y] for z in all_z]
pairs_z4 = [(token_at(y, z, c), token_at(y, z ^ 4, c)) for y in all_y for z in all_z for c in all_c]
groups_x = [[head_at(x, z) for x in range(NX)] for z in range(NZH)]
pairs_zh = [(head_at(x, z), head_at(x, 1 - z)) for x in range(NX) for z in range(NZH)]


def pairs_x(flip):
    return [(head_at(x, z), head_at(x ^ flip, z)) for x in range(NX) for z in range(NZH)]


def exchanged(parts, axis, groups):
    return lax.all_to_all(parts, axis, 0, 0, tiled=True, axis_index_groups=groups)


def gathered(value, axis, groups):
    copies = jnp.broadcast_to(value[None], (len(groups[0]), *value.shape))
    return exchanged(copies, axis, groups)


def diagonal(rows, lanes):
    return lax.broadcasted_iota(jnp.int32, (rows, lanes), 0) == lax.broadcasted_iota(
        jnp.int32, (rows, lanes), 1
    )


def as_row(column, lanes=128):
    return jnp.sum(jnp.where(diagonal(column.shape[0], lanes), column, 0.0), axis=0, keepdims=True)


def as_column(row, rows):
    return jnp.sum(jnp.where(diagonal(rows, row.shape[1]), row, 0.0), axis=1, keepdims=True)


def call(kernel, out_shape, flops=0, moved=0):
    return pl.pallas_call(
        kernel,
        out_shape=out_shape,
        compiler_params=pltpu.CompilerParams(vmem_limit_bytes=VMEM),
        cost_estimate=pl.CostEstimate(flops=flops, bytes_accessed=moved, transcendentals=0),
    )


def score_kernel(limit_ref, q_ref, k_ref, e_ref, m_ref, l_ref):
    rows, keys = e_ref.shape
    block = rows // NYC
    key = lax.broadcasted_iota(jnp.int32, (1, keys), 1)
    k = k_ref[...]
    for b in range(NYC):
        lines = slice(b * block, (b + 1) * block)
        s = jnp.dot(q_ref[lines], k, preferred_element_type=f32) * softmax_scale
        s = jnp.where(key <= limit_ref[lines], s, masked_value)
        m = jnp.max(s, axis=1, keepdims=True)
        e = jnp.exp(s - m)
        e_ref[lines] = e
        m_ref[b : b + 1] = as_row(m)
        l_ref[b : b + 1] = as_row(jnp.sum(e, axis=1, keepdims=True))


def message_parts(ref, tokens, heads):
    block = ref[tokens * heads :, :].astype(f32)
    w = block[:, :heads] + block[:, heads : 2 * heads] + block[:, 2 * heads : 3 * heads]
    return ref[: tokens * heads, :], w


def index_dot(iq, ik):
    return lax.dot_general(iq, ik, (((1,), (1,)), ((), ())), preferred_element_type=f32)


def logits_kernel(heads, scale, message_ref, ik_ref, *refs):
    before, out_ref = refs[:-1], refs[-1]
    tokens = out_ref.shape[0]
    ik = ik_ref[...]
    logits = before[0][...] if before else jnp.zeros(out_ref.shape, f32)
    for part in range(message_ref.shape[0]):
        iq, w = message_parts(message_ref.at[part], tokens, heads)
        active = index_dot(iq, ik)
        for j in range(heads):
            here = active[j * tokens : (j + 1) * tokens] * scale
            logits = logits + w[:, j : j + 1] * jnp.maximum(here, 0.0)
    out_ref[...] = logits


def index_stats_kernel(heads, scale, message_ref, ik_ref, before_ref, limit_ref, logits_ref, stat_ref):
    logits_kernel(heads, scale, message_ref, ik_ref, before_ref, logits_ref)
    key = lax.broadcasted_iota(jnp.int32, (1, logits_ref.shape[1]), 1)
    logits = jnp.where(key <= limit_ref[...], logits_ref[...], masked_value)
    m = jnp.max(logits, axis=1, keepdims=True)
    l = jnp.sum(jnp.exp(logits - m), axis=1, keepdims=True)
    logits_ref[...] = logits
    stat_ref[...] = jnp.concatenate([as_row(m), as_row(l), jnp.zeros((6, 128), f32)], axis=0)


def joined(stats):
    def one(m, l):
        top = jnp.max(m, axis=0)
        return top, jnp.sum(l * jnp.exp(m - top), axis=0)

    return (*one(stats[:, 0:8], stats[:, 8:16]), *one(stats[:, 16:17], stats[:, 17:18]))


def join_kernel(stats_ref, out_ref):
    lines = jnp.concatenate([*joined(stats_ref[...]), jnp.zeros((6, 128), f32)], axis=0)
    out_ref[...] = jnp.broadcast_to(lines[None], out_ref.shape)


def target_kernel(stats_ref, m_ref, e_ref, out_ref):
    top, total, _, _ = joined(stats_ref[...])
    weights = jnp.exp(m_ref[...] - top) / total
    keys = out_ref.shape[1]
    block = e_ref.shape[0] // NYC
    for b in range(NYC):
        e = e_ref[b * block : (b + 1) * block] * as_column(weights[b : b + 1], block)
        out_ref[b * NZ : (b + 1) * NZ] = jnp.sum(e.reshape(NZ, block // NZ, keys), axis=1)


def dlogit_kernel(x_ref, one_ref, two_ref, logits_ref, stats_ref, out_ref):
    rows = one_ref.shape[0]
    first = pl.multiple_of(x_ref[0] * rows, rows)
    _, _, top, total = joined(stats_ref[...])
    lane = lax.broadcasted_iota(jnp.int32, (rows, 128), 1)
    mine = lane == lax.broadcasted_iota(jnp.int32, (rows, 128), 0) + first
    top = jnp.sum(jnp.where(mine, top, 0.0), axis=1, keepdims=True)
    total = jnp.sum(jnp.where(mine, total, 0.0), axis=1, keepdims=True)
    probs = jnp.exp(logits_ref[pl.ds(first, rows), :] - top) / total
    dlogit = GRAD_SCALE * (probs - (one_ref[...] + two_ref[...]) / H)
    out_ref[...] = jnp.broadcast_to(dlogit[None], out_ref.shape)


def grad_kernel(heads, scale, d_ref, message_ref, ik_ref, out_ref):
    dlogit = d_ref[...]
    tokens = dlogit.shape[0]
    parts = message_ref.shape[0]
    ik = ik_ref[...]
    row = lax.broadcasted_iota(jnp.int32, (tokens, 128), 0)
    place = row // NZ % NY * (NC * NZ) + row % NZ * NC + row // (NY * NZ)
    places = place == lax.broadcasted_iota(jnp.int32, (tokens, 128), 1)
    weights = tokens * heads * parts
    out_ref[weights:, :] = jnp.zeros((out_ref.shape[0] - weights, 128), f32)
    for part in range(parts):
        iq, w = message_parts(message_ref.at[part], tokens, heads)
        active = index_dot(iq, ik)
        for j in range(heads):
            here = active[j * tokens : (j + 1) * tokens]
            gate = jnp.where(here > 0.0, dlogit * w[:, j : j + 1], 0.0).astype(bf16)
            grad = jnp.dot(gate, ik, preferred_element_type=f32) * scale
            head = part * heads + j
            for b in range(NYC):
                first = b % NY * (NZ * NC) + b // NY
                lines = pl.ds(first * heads * parts + head, NZ, stride=NC * heads * parts)
                out_ref[lines, :] = grad[b * NZ : (b + 1) * NZ]
            weight_grad = jnp.sum(dlogit * jnp.maximum(here * scale, 0.0), axis=1, keepdims=True)
            out_ref[weights + head : weights + head + 1, :] = jnp.sum(
                jnp.where(places, weight_grad, 0.0), axis=0, keepdims=True
            )


def key_kernel(heads, scale, d_ref, ik_ref, *refs):
    messages, out_ref = refs[:-1], refs[-1]
    dlogit, ik = d_ref[...], ik_ref[...]
    tokens, keys = dlogit.shape
    total = jnp.zeros((ik.shape[1], keys), f32)
    for message in messages:
        for part in range(message.shape[0]):
            iq, w = message_parts(message.at[part], tokens, heads)
            active = index_dot(iq, ik)
            gates = []
            for j in range(heads):
                here = active[j * tokens : (j + 1) * tokens]
                gates.append(jnp.where(here > 0.0, dlogit * w[:, j : j + 1], 0.0).astype(bf16))
            gate = jnp.concatenate(gates, axis=0)
            total = total + jnp.dot(iq.T, gate, preferred_element_type=f32)
    out_ref[...] = total.T * scale


def sum_kernel(parts_ref, out_ref):
    out_ref[...] = jnp.broadcast_to(jnp.sum(parts_ref[...], axis=0)[None], out_ref.shape)


def pair_kernel(one_ref, two_ref, out_ref):
    out_ref[...] = jnp.broadcast_to((one_ref[...] + two_ref[...])[None], out_ref.shape)


def in_order(value):
    return jnp.moveaxis(value.reshape(NY, NZ, NC, *value.shape[1:]), 2, 0).reshape(value.shape)


def local(queries, latent_keys, index_queries, index_keys, index_weights, positions):
    heads_here, width = queries.shape[0], queries.shape[2]
    key_count = latent_keys.shape[0]
    query_count, index_heads, index_width = index_queries.shape
    index_scale = index_width ** (-0.5)
    share_rows = query_count // NX
    shape = jax.ShapeDtypeStruct
    x = lax.axis_index("heads") // NZH
    core = lax.axis_index("tokens") % NC
    limit = in_order(positions - lax.axis_index("tokens") * key_count)

    along_z = gathered(queries.reshape(heads_here, width), "tokens", groups_z)

    high = lax.reduce_precision(index_weights, 8, 7)
    middle = lax.reduce_precision(index_weights - high, 8, 7)
    low = index_weights - high - middle
    half = index_heads // NC
    lines = jnp.stack([high, middle, low], axis=1).reshape(query_count, 3, NC, half)
    lines = in_order(lines.transpose(0, 2, 1, 3).reshape(query_count, NC, 3 * half))
    lines = jnp.pad(lines.transpose(1, 0, 2), ((0, 0), (0, 0), (0, 128 - 3 * half)))
    by_head = in_order(index_queries).transpose(1, 0, 2)
    by_head = by_head.reshape(NC, half * query_count, index_width)
    mine = jnp.concatenate([by_head, lines.astype(bf16)], axis=1)

    first = lax.ppermute(lax.dynamic_index_in_dim(mine, core, 0), "heads", pairs_zh)
    second = lax.ppermute(first, "tokens", pairs_c)
    four = jnp.concatenate([mine, first, second])
    messages = [four] + [lax.ppermute(four, "heads", pairs_x(flip)) for flip in range(1, NX)]

    index_flops = 2 * query_count * half * key_count * index_width
    logits = None
    for message in messages[:-1]:
        logits = call(
            lambda *refs: logits_kernel(half, index_scale, *refs),
            shape((query_count, key_count), f32),
            flops=4 * index_flops,
            moved=1 << 20,
        )(message, index_keys, *([] if logits is None else [logits]))
    logits, index_stats = call(
        lambda *refs: index_stats_kernel(half, index_scale, *refs),
        (shape((query_count, key_count), f32), shape((8, 128), f32)),
        flops=80 * index_flops,
        moved=1 << 20,
    )(messages[-1], index_keys, logits, limit[:, None])
    rows = gathered(along_z, "tokens", groups_yc).reshape(-1, width)

    row_count = rows.shape[0]
    lines_shape = shape((NYC, row_count // NYC), f32)
    exponent, local_max, local_total = call(
        score_kernel,
        (shape((row_count, key_count), f32), lines_shape, lines_shape),
        flops=2 * row_count * key_count * width,
        moved=4 << 20,
    )(jnp.repeat(limit, heads_here)[:, None], rows, latent_keys.T)

    stats = jnp.concatenate([local_max, local_total, index_stats])
    stats = gathered(stats, "tokens", groups_z)
    stats = call(join_kernel, shape((NYC, *stats.shape[1:]), f32))(stats)
    stats = exchanged(stats, "tokens", groups_yc)

    partial = call(target_kernel, shape((query_count, key_count), f32), moved=5 << 20)(
        stats, local_max, exponent
    )
    over_x = exchanged(partial.reshape(NX, share_rows, key_count), "heads", groups_x).sum(axis=0)
    other = lax.ppermute(over_x, "heads", pairs_zh)
    dlogit = call(dlogit_kernel, shape((NX, share_rows, key_count), f32))(
        x.reshape(1), over_x, other, logits, stats
    )
    dlogit = exchanged(dlogit, "heads", groups_x).reshape(query_count, key_count)

    query_lines = query_count * index_heads
    piece_rows = -(-(query_lines + index_heads) // (NYC * 8)) * 8
    both = call(
        lambda *refs: grad_kernel(half, index_scale, *refs),
        shape((piece_rows * NYC, 128), f32),
        flops=4 * index_flops,
        moved=2 << 20,
    )(dlogit, mine, index_keys)

    piece = exchanged(both.reshape(NYC, piece_rows, 128), "tokens", groups_yc)
    piece = call(sum_kernel, shape((NZ // 2, piece_rows, 128), f32))(piece)
    piece = exchanged(piece, "tokens", groups_z4).sum(axis=0)
    other = lax.ppermute(piece, "tokens", pairs_z4)
    piece = call(pair_kernel, shape((NYC, piece_rows, 128), f32))(piece, other)
    both = exchanged(piece, "tokens", groups_yc).reshape(-1, 128)
    query_grad = both[:query_lines].reshape(query_count, index_heads, index_width)
    weight_grad = both[query_lines : query_lines + index_heads, :query_count].T

    key_grad = call(
        lambda *refs: key_kernel(half, index_scale, *refs),
        shape((key_count, index_width), f32),
        flops=4 * index_flops * NX * NZH,
        moved=3 << 20,
    )(dlogit, index_keys, *messages)
    return (query_grad, weight_grad, key_grad)


def solution(mesh):
    placed = (
        P("heads", "tokens", None),
        P("tokens", None),
        P(None, "heads", None),
        P("tokens", None),
        P(None, "heads"),
        P(),
    )
    return jax.shard_map(
        local,
        mesh=mesh,
        in_specs=placed,
        out_specs=(P(None, "heads", None), P(None, "heads"), P("tokens", None)),
        check_vma=False,
    )
```

```python
import jax
import jax.numpy as jnp
from jax import lax
from jax.experimental import pallas as pl
from jax.experimental.pallas import tpu as pltpu
from jax.sharding import PartitionSpec as P

H = 128
NX, NZH = 4, 2
NY, NZ, NC = 4, 8, 2
NYC = NY * NC
GRAD_SCALE = 8192.0
VMEM = 12 << 20
WEIGHT = 160

softmax_scale = 192.0 ** (-0.5)
masked_value = -1e30
f32, bf16 = jnp.float32, jnp.bfloat16


def token_at(y, z, c):
    return (y * NZ + z) * NC + c


def head_at(x, z):
    return x * NZH + z


all_y, all_z, all_c = range(NY), range(NZ), range(NC)
groups_z = [[token_at(y, z, c) for z in all_z] for y in all_y for c in all_c]
groups_z4 = [
    [token_at(y, half + z, c) for z in range(4)] for half in (0, 4) for y in all_y for c in all_c
]
pairs_c = [(token_at(y, z, c), token_at(y, z, 1 - c)) for y in all_y for z in all_z for c in all_c]
groups_y = [[token_at(y, z, c) for y in all_y] for z in all_z for c in all_c]
groups_yc = [[token_at(y, z, c) for c in all_c for y in all_y] for z in all_z]
pairs_z4 = [(token_at(y, z, c), token_at(y, z ^ 4, c)) for y in all_y for z in all_z for c in all_c]
groups_x = [[head_at(x, z) for x in range(NX)] for z in range(NZH)]
pairs_zh = [(head_at(x, z), head_at(x, 1 - z)) for x in range(NX) for z in range(NZH)]


def pairs_x(flip):
    return [(head_at(x, z), head_at(x ^ flip, z)) for x in range(NX) for z in range(NZH)]


def exchanged(parts, axis, groups):
    return lax.all_to_all(parts, axis, 0, 0, tiled=True, axis_index_groups=groups)


def gathered(value, axis, groups):
    copies = jnp.broadcast_to(value[None], (len(groups[0]), *value.shape))
    return exchanged(copies, axis, groups)


def diagonal(rows, lanes):
    return lax.broadcasted_iota(jnp.int32, (rows, lanes), 0) == lax.broadcasted_iota(
        jnp.int32, (rows, lanes), 1
    )


def as_row(column, lanes=128):
    return jnp.sum(jnp.where(diagonal(column.shape[0], lanes), column, 0.0), axis=0, keepdims=True)


def as_column(row, rows):
    return jnp.sum(jnp.where(diagonal(rows, row.shape[1]), row, 0.0), axis=1, keepdims=True)


def call(kernel, out_shape, flops=0, moved=0, aliases={}):
    return pl.pallas_call(
        kernel,
        out_shape=out_shape,
        input_output_aliases=aliases,
        compiler_params=pltpu.CompilerParams(vmem_limit_bytes=VMEM),
        cost_estimate=pl.CostEstimate(flops=flops, bytes_accessed=moved, transcendentals=0),
    )


def score_kernel(core_ref, limit_ref, q_ref, k_ref, *refs):
    e_ref, m_ref, l_ref = refs[-3:]
    block = e_ref.shape[0] // NYC
    key = lax.broadcasted_iota(jnp.int32, (1, e_ref.shape[1]), 1)
    k = k_ref[...]
    core = core_ref[0]
    for y in range(NY):
        line = core * NY + y
        lines = pl.ds(pl.multiple_of(line * block, block), block)
        s = jnp.dot(q_ref[y * block : (y + 1) * block], k, preferred_element_type=f32)
        s = jnp.where(key <= limit_ref[lines], s * softmax_scale, masked_value)
        m = jnp.max(s, axis=1, keepdims=True)
        e = jnp.exp(s - m)
        e_ref[lines] = e
        m_ref[pl.ds(line, 1)] = as_row(m)
        l_ref[pl.ds(line, 1)] = as_row(jnp.sum(e, axis=1, keepdims=True))


def message_parts(ref, tokens, heads):
    block = ref[tokens * heads :, :].astype(f32)
    w = block[:, :heads] + block[:, heads : 2 * heads] + block[:, 2 * heads : 3 * heads]
    return ref[: tokens * heads, :], w


def index_dot(iq, ik):
    return lax.dot_general(iq, ik, (((1,), (1,)), ((), ())), preferred_element_type=f32)


def logits_kernel(heads, scale, message_ref, ik_ref, out_ref):
    tokens = out_ref.shape[0]
    iq, w = message_parts(message_ref, tokens, heads)
    active = index_dot(iq, ik_ref[...])
    logits = jnp.zeros(out_ref.shape, f32)
    for j in range(heads):
        here = active[j * tokens : (j + 1) * tokens] * scale
        logits = logits + w[:, j : j + 1] * jnp.maximum(here, 0.0)
    out_ref[...] = logits


def index_stats_kernel(limit_ref, one_ref, two_ref, logits_ref, stat_ref):
    key = lax.broadcasted_iota(jnp.int32, (1, logits_ref.shape[1]), 1)
    logits = jnp.where(key <= limit_ref[...], one_ref[...] + two_ref[...], masked_value)
    m = jnp.max(logits, axis=1, keepdims=True)
    l = jnp.sum(jnp.exp(logits - m), axis=1, keepdims=True)
    logits_ref[...] = logits
    stat_ref[...] = jnp.concatenate([as_row(m), as_row(l), jnp.zeros((6, 128), f32)], axis=0)


def joined(stats):
    def one(m, l):
        top = jnp.max(m, axis=0)
        return top, jnp.sum(l * jnp.exp(m - top), axis=0)

    return (*one(stats[:, 0:8], stats[:, 8:16]), *one(stats[:, 16:17], stats[:, 17:18]))


def join_kernel(stats_ref, out_ref):
    lines = jnp.concatenate([*joined(stats_ref[...]), jnp.zeros((6, 128), f32)], axis=0)
    out_ref[...] = jnp.broadcast_to(lines[None], out_ref.shape)


def target_kernel(stats_ref, m_ref, e_ref, out_ref):
    top, total, _, _ = joined(stats_ref[...])
    weights = jnp.exp(m_ref[...] - top) / total
    keys = out_ref.shape[1]
    block = e_ref.shape[0] // NYC
    for b in range(NYC):
        e = e_ref[b * block : (b + 1) * block] * as_column(weights[b : b + 1], block)
        out_ref[b * NZ : (b + 1) * NZ] = jnp.sum(e.reshape(NZ, block // NZ, keys), axis=1)


def dlogit_kernel(one_ref, two_ref, logits_ref, stats_ref, out_ref):
    rows = logits_ref.shape[0]
    _, _, top, total = joined(stats_ref[...])
    probs = jnp.exp(logits_ref[...] - as_column(top, rows)) / as_column(total, rows)
    dlogit = GRAD_SCALE * (probs - (one_ref[...] + two_ref[...]) / H)
    out_ref[...] = jnp.broadcast_to(dlogit[None], out_ref.shape)


def grad_kernel(heads, scale, d_ref, message_ref, ik_ref, out_ref):
    dlogit = d_ref[...]
    tokens = dlogit.shape[0]
    iq, w = message_parts(message_ref, tokens, heads)
    ik = ik_ref[...]
    active = index_dot(iq, ik)
    row = lax.broadcasted_iota(jnp.int32, (tokens, 128), 0)
    place = row // NZ % NY * (NC * NZ) + row % NZ * NC + row // (NY * NZ)
    places = place == lax.broadcasted_iota(jnp.int32, (tokens, 128), 1)
    out_ref[tokens * heads :, :] = jnp.zeros((out_ref.shape[0] - tokens * heads, 128), f32)
    for j in range(heads):
        here = active[j * tokens : (j + 1) * tokens]
        gate = jnp.where(here > 0.0, dlogit * w[:, j : j + 1], 0.0).astype(bf16)
        grad = jnp.dot(gate, ik, preferred_element_type=f32) * scale
        for b in range(NYC):
            first = b % NY * (NZ * NC) + b // NY
            lines = pl.ds(first * heads + j, NZ, stride=NC * heads)
            out_ref[lines, :] = grad[b * NZ : (b + 1) * NZ]
        weight_grad = jnp.sum(dlogit * jnp.maximum(here * scale, 0.0), axis=1, keepdims=True)
        out_ref[tokens * heads + j : tokens * heads + j + 1, :] = jnp.sum(
            jnp.where(places, weight_grad, 0.0), axis=0, keepdims=True
        )


def key_kernel(heads, scale, d_ref, ik_ref, *refs):
    messages, out_ref = refs[:-1], refs[-1]
    dlogit, ik = d_ref[...], ik_ref[...]
    tokens, keys = dlogit.shape
    total = jnp.zeros((ik.shape[1], keys), f32)
    for message in messages:
        for part in range(message.shape[0]):
            iq, w = message_parts(message.at[part], tokens, heads)
            active = index_dot(iq, ik)
            gates = []
            for j in range(heads):
                here = active[j * tokens : (j + 1) * tokens]
                gates.append(jnp.where(here > 0.0, dlogit * w[:, j : j + 1], 0.0).astype(bf16))
            gate = jnp.concatenate(gates, axis=0)
            total = total + jnp.dot(iq.T, gate, preferred_element_type=f32)
    out_ref[...] = total.T * scale


def sum_kernel(parts_ref, out_ref):
    out_ref[...] = jnp.broadcast_to(jnp.sum(parts_ref[...], axis=0)[None], out_ref.shape)


def pair_kernel(one_ref, two_ref, out_ref):
    out_ref[...] = jnp.broadcast_to((one_ref[...] + two_ref[...])[None], out_ref.shape)


def in_order(value):
    return jnp.moveaxis(value.reshape(NY, NZ, NC, *value.shape[1:]), 2, 0).reshape(value.shape)


def x_scatter_sum(parts, x):
    total = lax.dynamic_index_in_dim(parts, x, 0, keepdims=False)
    for flip in range(1, NX):
        piece = lax.dynamic_index_in_dim(parts, x ^ flip, 0, keepdims=False)
        total = total + lax.ppermute(piece, "heads", pairs_x(flip))
    return total


def local(queries, latent_keys, index_queries, index_keys, index_weights, positions):
    heads_here, width = queries.shape[0], queries.shape[2]
    key_count = latent_keys.shape[0]
    query_count, index_heads, index_width = index_queries.shape
    index_scale = index_width ** (-0.5)
    share_rows = query_count // NX
    shape = jax.ShapeDtypeStruct
    x = lax.axis_index("heads") // NZH
    core = lax.axis_index("tokens") % NC
    limit = in_order(positions - lax.axis_index("tokens") * key_count)

    along_z = gathered(queries.reshape(heads_here, width), "tokens", groups_z)

    high = lax.reduce_precision(index_weights, 8, 7)
    middle = lax.reduce_precision(index_weights - high, 8, 7)
    low = index_weights - high - middle
    lines = in_order(jnp.concatenate([high, middle, low], axis=1))
    lines = jnp.pad(lines, ((0, 0), (0, 128 - 3 * index_heads)))
    by_head = in_order(index_queries).transpose(1, 0, 2)
    by_head = by_head.reshape(index_heads * query_count, index_width)
    mine = jnp.concatenate([by_head, lines.astype(bf16)])

    index_flops = 2 * query_count * index_heads * key_count * index_width
    partial = call(
        lambda *refs: logits_kernel(index_heads, index_scale, *refs),
        shape((query_count, key_count), f32),
        flops=index_flops,
        moved=1 << 20,
    )(mine, index_keys)
    over_x = x_scatter_sum(partial.reshape(NX, share_rows, key_count), x)
    other = lax.ppermute(over_x, "heads", pairs_zh)
    share_limit = lax.dynamic_slice_in_dim(limit, x * share_rows, share_rows, 0)
    logits, index_stats = call(
        index_stats_kernel,
        (shape((share_rows, key_count), f32), shape((8, 128), f32)),
        flops=WEIGHT * index_flops,
        moved=1 << 20,
    )(share_limit[:, None], over_x, other)

    rows = gathered(along_z, "tokens", groups_y)
    other_rows = lax.ppermute(rows, "tokens", pairs_c)
    row_count = NC * rows.size // width
    row_limit = jnp.repeat(limit, heads_here)[:, None]
    lines_shape = shape((NYC, row_count // NYC), f32)
    scored = ()
    for where, part in ((core, rows), (1 - core, other_rows)):
        scored = call(
            score_kernel,
            (shape((row_count, key_count), f32), lines_shape, lines_shape),
            flops=row_count * key_count * width,
            moved=4 << 20,
            aliases={4 + i: i for i in range(len(scored))},
        )(where.reshape(1), row_limit, part.reshape(-1, width), latent_keys.T, *scored)
    exponent, local_max, local_total = scored

    stats = jnp.concatenate([local_max, local_total, index_stats])

    stats = gathered(stats, "tokens", groups_z)
    stats = call(join_kernel, shape((NYC, *stats.shape[1:]), f32))(stats)
    stats = exchanged(stats, "tokens", groups_yc)

    partial = call(target_kernel, shape((query_count, key_count), f32), moved=5 << 20)(
        stats, local_max, exponent
    )

    mine_rows = mine.shape[0] // NC
    partial, late = lax.optimization_barrier((partial, mine))
    sent = lax.dynamic_slice_in_dim(late, core * mine_rows, mine_rows, 0)
    swapped = lax.ppermute(sent, "heads", pairs_zh)
    over_x = exchanged(partial.reshape(NX, share_rows, key_count), "heads", groups_x).sum(axis=0)
    other = lax.ppermute(over_x, "heads", pairs_zh)
    other, swapped = lax.optimization_barrier((other, swapped))
    swapped_other = lax.ppermute(swapped, "tokens", pairs_c)
    dlogit = call(dlogit_kernel, shape((NX, share_rows, key_count), f32))(
        over_x, other, logits, stats
    )
    dlogit = exchanged(dlogit, "heads", groups_x).reshape(query_count, key_count)
    dlogit, swapped_other = lax.optimization_barrier((dlogit, swapped_other))
    halves = jnp.where(
        core == 0,
        jnp.concatenate([swapped, swapped_other]),
        jnp.concatenate([swapped_other, swapped]),
    )
    pair = jnp.stack([mine, halves])
    messages = [pair] + [lax.ppermute(pair, "heads", pairs_x(flip)) for flip in range(1, NX)]

    query_lines = query_count * index_heads
    piece_rows = -(-(query_lines + index_heads) // (NYC * 8)) * 8
    both = call(
        lambda *refs: grad_kernel(index_heads, index_scale, *refs),
        shape((piece_rows * NYC, 128), f32),
        flops=2 * index_flops,
        moved=2 << 20,
    )(dlogit, mine, index_keys)

    piece = exchanged(both.reshape(NYC, piece_rows, 128), "tokens", groups_yc)
    piece = call(sum_kernel, shape((NZ // 2, piece_rows, 128), f32))(piece)
    piece = exchanged(piece, "tokens", groups_z4).sum(axis=0)
    other = lax.ppermute(piece, "tokens", pairs_z4)
    piece = call(pair_kernel, shape((NYC, piece_rows, 128), f32))(piece, other)
    both = exchanged(piece, "tokens", groups_yc).reshape(-1, 128)
    query_grad = both[:query_lines].reshape(query_count, index_heads, index_width)
    weight_grad = both[query_lines : query_lines + index_heads, :query_count].T

    key_grad = call(
        lambda *refs: key_kernel(index_heads, index_scale, *refs),
        shape((key_count, index_width), f32),
        flops=2 * index_flops * NX * NZH,
        moved=3 << 20,
    )(dlogit, index_keys, *messages)
    return (query_grad, weight_grad, key_grad)


def solution(mesh):
    placed = (
        P("heads", "tokens", None),
        P("tokens", None),
        P(None, "heads", None),
        P("tokens", None),
        P(None, "heads"),
        P(),
    )
    return jax.shard_map(
        local,
        mesh=mesh,
        in_specs=placed,
        out_specs=(P(None, "heads", None), P(None, "heads"), P("tokens", None)),
        check_vma=False,
    )
```

```python
import jax
import jax.numpy as jnp
from jax import lax
from jax.experimental import pallas as pl
from jax.experimental.pallas import tpu as pltpu
from jax.sharding import PartitionSpec as P

H = 128
NX, NZH = 4, 2
NY, NZ, NC = 4, 8, 2
NYC = NY * NC
GRAD_SCALE = 8192.0
VMEM = 12 << 20
WEIGHT = 160

softmax_scale = 192.0 ** (-0.5)
masked_value = -1e30
f32, bf16 = jnp.float32, jnp.bfloat16


def token_at(y, z, c):
    return (y * NZ + z) * NC + c


def head_at(x, z):
    return x * NZH + z


all_y, all_z, all_c = range(NY), range(NZ), range(NC)
groups_z = [[token_at(y, z, c) for z in all_z] for y in all_y for c in all_c]
groups_z4 = [
    [token_at(y, half + z, c) for z in range(4)] for half in (0, 4) for y in all_y for c in all_c
]
pairs_c = [(token_at(y, z, c), token_at(y, z, 1 - c)) for y in all_y for z in all_z for c in all_c]
groups_y = [[token_at(y, z, c) for y in all_y] for z in all_z for c in all_c]
groups_yc = [[token_at(y, z, c) for c in all_c for y in all_y] for z in all_z]
pairs_z4 = [(token_at(y, z, c), token_at(y, z ^ 4, c)) for y in all_y for z in all_z for c in all_c]
groups_x = [[head_at(x, z) for x in range(NX)] for z in range(NZH)]
pairs_zh = [(head_at(x, z), head_at(x, 1 - z)) for x in range(NX) for z in range(NZH)]


def pairs_x(flip):
    return [(head_at(x, z), head_at(x ^ flip, z)) for x in range(NX) for z in range(NZH)]


def exchanged(parts, axis, groups):
    return lax.all_to_all(parts, axis, 0, 0, tiled=True, axis_index_groups=groups)


def gathered(value, axis, groups):
    copies = jnp.broadcast_to(value[None], (len(groups[0]), *value.shape))
    return exchanged(copies, axis, groups)


def diagonal(rows, lanes):
    return lax.broadcasted_iota(jnp.int32, (rows, lanes), 0) == lax.broadcasted_iota(
        jnp.int32, (rows, lanes), 1
    )


def as_row(column, lanes=128):
    return jnp.sum(jnp.where(diagonal(column.shape[0], lanes), column, 0.0), axis=0, keepdims=True)


def as_column(row, rows):
    return jnp.sum(jnp.where(diagonal(rows, row.shape[1]), row, 0.0), axis=1, keepdims=True)


def call(kernel, out_shape, flops=0, moved=0, aliases={}, vmem=VMEM, **specs):
    return pl.pallas_call(
        kernel,
        **specs,
        out_shape=out_shape,
        input_output_aliases=aliases,
        compiler_params=pltpu.CompilerParams(vmem_limit_bytes=vmem),
        cost_estimate=pl.CostEstimate(flops=flops, bytes_accessed=moved, transcendentals=0),
    )


def score_kernel(core_ref, limit_ref, q_ref, k_ref, *refs):
    e_ref, m_ref, l_ref, held, sems = refs[-5:]
    for before, after in zip(refs[1:-5], (m_ref, l_ref)):
        after[...] = before[...]
    block = held.shape[1]
    key = lax.broadcasted_iota(jnp.int32, (1, held.shape[2]), 1)
    k = k_ref[...]
    core = core_ref[0]
    copies = []
    for y in range(NY):
        line = core * NY + y
        lines = pl.ds(pl.multiple_of(line * block, block), block)
        s = jnp.dot(q_ref[y * block : (y + 1) * block], k, preferred_element_type=f32)
        s = jnp.where(key <= limit_ref[lines], s * softmax_scale, masked_value)
        m = jnp.max(s, axis=1, keepdims=True)
        e = jnp.exp(s - m)
        held[y] = e
        copies.append(pltpu.make_async_copy(held.at[y], e_ref.at[lines], sems.at[y]))
        copies[-1].start()
        m_ref[pl.ds(line, 1)] = as_row(m)
        l_ref[pl.ds(line, 1)] = as_row(jnp.sum(e, axis=1, keepdims=True))
    for copy in copies:
        copy.wait()


def message_parts(ref, tokens, heads):
    block = ref[tokens * heads :, :].astype(f32)
    w = block[:, :heads] + block[:, heads : 2 * heads] + block[:, 2 * heads : 3 * heads]
    return ref[: tokens * heads, :], w


def index_dot(iq, ik):
    return lax.dot_general(iq, ik, (((1,), (1,)), ((), ())), preferred_element_type=f32)


def logits_kernel(heads, scale, message_ref, ik_ref, out_ref):
    tokens = out_ref.shape[0]
    iq, w = message_parts(message_ref, tokens, heads)
    active = index_dot(iq, ik_ref[...])
    logits = jnp.zeros(out_ref.shape, f32)
    for j in range(heads):
        here = active[j * tokens : (j + 1) * tokens] * scale
        logits = logits + w[:, j : j + 1] * jnp.maximum(here, 0.0)
    out_ref[...] = logits


def index_stats_kernel(limit_ref, one_ref, two_ref, logits_ref, stat_ref):
    key = lax.broadcasted_iota(jnp.int32, (1, logits_ref.shape[1]), 1)
    logits = jnp.where(key <= limit_ref[...], one_ref[...] + two_ref[...], masked_value)
    m = jnp.max(logits, axis=1, keepdims=True)
    l = jnp.sum(jnp.exp(logits - m), axis=1, keepdims=True)
    logits_ref[...] = logits
    stat_ref[...] = jnp.concatenate([as_row(m), as_row(l), jnp.zeros((6, 128), f32)], axis=0)


def joined(stats):
    def one(m, l):
        top = jnp.max(m, axis=0)
        return top, jnp.sum(l * jnp.exp(m - top), axis=0)

    return (*one(stats[:, 0:8], stats[:, 8:16]), *one(stats[:, 16:17], stats[:, 17:18]))


def join_kernel(stats_ref, out_ref):
    lines = jnp.concatenate([*joined(stats_ref[...]), jnp.zeros((6, 128), f32)], axis=0)
    out_ref[...] = jnp.broadcast_to(lines[None], out_ref.shape)


def target_kernel(stats_ref, m_ref, e_ref, out_ref, held, sems):
    block = held.shape[1]
    copies = []
    for b in range(NYC):
        lines = e_ref.at[b * block : (b + 1) * block]
        copies.append(pltpu.make_async_copy(lines, held.at[b], sems.at[b]))
        copies[-1].start()
    top, total, _, _ = joined(stats_ref[...])
    weights = jnp.exp(m_ref[...] - top) / total
    keys = out_ref.shape[1]
    for b in range(NYC):
        weight = as_column(weights[b : b + 1], block)
        copies[b].wait()
        e = held[b] * weight
        out_ref[b * NZ : (b + 1) * NZ] = jnp.sum(e.reshape(NZ, block // NZ, keys), axis=1)


def dlogit_kernel(one_ref, two_ref, logits_ref, stats_ref, out_ref):
    rows = logits_ref.shape[0]
    _, _, top, total = joined(stats_ref[...])
    probs = jnp.exp(logits_ref[...] - as_column(top, rows)) / as_column(total, rows)
    dlogit = GRAD_SCALE * (probs - (one_ref[...] + two_ref[...]) / H)
    out_ref[...] = jnp.broadcast_to(dlogit[None], out_ref.shape)


def grad_kernel(heads, scale, d_ref, message_ref, ik_ref, out_ref):
    dlogit = d_ref[...]
    tokens = dlogit.shape[0]
    iq, w = message_parts(message_ref, tokens, heads)
    ik = ik_ref[...]
    active = index_dot(iq, ik)
    row = lax.broadcasted_iota(jnp.int32, (tokens, 128), 0)
    place = row // NZ % NY * (NC * NZ) + row % NZ * NC + row // (NY * NZ)
    places = place == lax.broadcasted_iota(jnp.int32, (tokens, 128), 1)
    out_ref[tokens * heads :, :] = jnp.zeros((out_ref.shape[0] - tokens * heads, 128), f32)
    for j in range(heads):
        here = active[j * tokens : (j + 1) * tokens]
        gate = jnp.where(here > 0.0, dlogit * w[:, j : j + 1], 0.0).astype(bf16)
        grad = jnp.dot(gate, ik, preferred_element_type=f32) * scale
        for b in range(NYC):
            first = b % NY * (NZ * NC) + b // NY
            lines = pl.ds(first * heads + j, NZ, stride=NC * heads)
            out_ref[lines, :] = grad[b * NZ : (b + 1) * NZ]
        weight_grad = jnp.sum(dlogit * jnp.maximum(here * scale, 0.0), axis=1, keepdims=True)
        out_ref[tokens * heads + j : tokens * heads + j + 1, :] = jnp.sum(
            jnp.where(places, weight_grad, 0.0), axis=0, keepdims=True
        )


def key_kernel(heads, scale, d_ref, ik_ref, *refs):
    messages, out_ref = refs[:-1], refs[-1]
    dlogit, ik = d_ref[...], ik_ref[...]
    tokens, keys = dlogit.shape
    total = jnp.zeros((ik.shape[1], keys), f32)
    for message in messages:
        for part in range(message.shape[0]):
            iq, w = message_parts(message.at[part], tokens, heads)
            active = index_dot(iq, ik)
            gates = []
            for j in range(heads):
                here = active[j * tokens : (j + 1) * tokens]
                gates.append(jnp.where(here > 0.0, dlogit * w[:, j : j + 1], 0.0).astype(bf16))
            gate = jnp.concatenate(gates, axis=0)
            total = total + jnp.dot(iq.T, gate, preferred_element_type=f32)
    out_ref[...] = total.T * scale


def sum_kernel(parts_ref, out_ref):
    out_ref[...] = jnp.broadcast_to(jnp.sum(parts_ref[...], axis=0)[None], out_ref.shape)


def pair_kernel(one_ref, two_ref, out_ref):
    out_ref[...] = jnp.broadcast_to((one_ref[...] + two_ref[...])[None], out_ref.shape)


def in_order(value):
    return jnp.moveaxis(value.reshape(NY, NZ, NC, *value.shape[1:]), 2, 0).reshape(value.shape)


def x_scatter_sum(parts, x):
    total = lax.dynamic_index_in_dim(parts, x, 0, keepdims=False)
    for flip in range(1, NX):
        piece = lax.dynamic_index_in_dim(parts, x ^ flip, 0, keepdims=False)
        total = total + lax.ppermute(piece, "heads", pairs_x(flip))
    return total


def local(queries, latent_keys, index_queries, index_keys, index_weights, positions):
    heads_here, width = queries.shape[0], queries.shape[2]
    key_count = latent_keys.shape[0]
    query_count, index_heads, index_width = index_queries.shape
    index_scale = index_width ** (-0.5)
    share_rows = query_count // NX
    shape = jax.ShapeDtypeStruct
    x = lax.axis_index("heads") // NZH
    core = lax.axis_index("tokens") % NC
    limit = in_order(positions - lax.axis_index("tokens") * key_count)

    along_z = gathered(queries.reshape(heads_here, width), "tokens", groups_z)

    high = lax.reduce_precision(index_weights, 8, 7)
    middle = lax.reduce_precision(index_weights - high, 8, 7)
    low = index_weights - high - middle
    lines = in_order(jnp.concatenate([high, middle, low], axis=1))
    lines = jnp.pad(lines, ((0, 0), (0, 128 - 3 * index_heads)))
    by_head = in_order(index_queries).transpose(1, 0, 2)
    by_head = by_head.reshape(index_heads * query_count, index_width)
    mine = jnp.concatenate([by_head, lines.astype(bf16)])

    index_flops = 2 * query_count * index_heads * key_count * index_width
    partial = call(
        lambda *refs: logits_kernel(index_heads, index_scale, *refs),
        shape((query_count, key_count), f32),
        flops=index_flops,
        moved=1 << 20,
    )(mine, index_keys)
    over_x = x_scatter_sum(partial.reshape(NX, share_rows, key_count), x)
    other = lax.ppermute(over_x, "heads", pairs_zh)
    share_limit = lax.dynamic_slice_in_dim(limit, x * share_rows, share_rows, 0)
    logits, index_stats = call(
        index_stats_kernel,
        (shape((share_rows, key_count), f32), shape((8, 128), f32)),
        flops=WEIGHT * index_flops,
        moved=1 << 20,
    )(share_limit[:, None], over_x, other)

    rows = gathered(along_z, "tokens", groups_y)
    other_rows = lax.ppermute(rows, "tokens", pairs_c)
    row_count = NC * rows.size // width
    row_limit = jnp.repeat(limit, heads_here)[:, None]
    lines_shape = shape((NYC, row_count // NYC), f32)
    hbm, vmem, smem = (pl.BlockSpec(memory_space=m) for m in (pltpu.HBM, pltpu.VMEM, pltpu.SMEM))
    scored = ()
    for where, part in ((core, rows), (1 - core, other_rows)):
        scored = call(
            score_kernel,
            (shape((row_count, key_count), f32), lines_shape, lines_shape),
            flops=row_count * key_count * width,
            moved=4 << 20,
            aliases={4: 0} if scored else {},
            in_specs=[smem, vmem, vmem, vmem, *[hbm, vmem, vmem][: len(scored)]],
            out_specs=(hbm, vmem, vmem),
            vmem=48 << 20,
            scratch_shapes=[
                pltpu.VMEM((NY, row_count // NYC, key_count), f32),
                pltpu.SemaphoreType.DMA((NY,)),
            ],
        )(where.reshape(1), row_limit, part.reshape(-1, width), latent_keys.T, *scored)
    exponent, local_max, local_total = scored

    stats = jnp.concatenate([local_max, local_total, index_stats])

    mine_rows = mine.shape[0] // NC
    sent = lax.dynamic_slice_in_dim(mine, core * mine_rows, mine_rows, 0)
    stats, sent = lax.optimization_barrier((stats, sent))
    swapped = lax.ppermute(sent, "heads", pairs_zh)
    stats = gathered(stats, "tokens", groups_z)
    stats = call(join_kernel, shape((NYC, *stats.shape[1:]), f32))(stats)
    stats = exchanged(stats, "tokens", groups_yc)
    swapped_other = lax.ppermute(swapped, "tokens", pairs_c)

    partial = call(
        target_kernel,
        shape((query_count, key_count), f32),
        moved=5 << 20,
        in_specs=[vmem, vmem, hbm],
        out_specs=vmem,
        vmem=52 << 20,
        scratch_shapes=[
            pltpu.VMEM((NYC, row_count // NYC, key_count), f32),
            pltpu.SemaphoreType.DMA((NYC,)),
        ],
    )(stats, local_max, exponent)
    partial, swapped_other = lax.optimization_barrier((partial, swapped_other))
    halves = jnp.where(
        core == 0,
        jnp.concatenate([swapped, swapped_other]),
        jnp.concatenate([swapped_other, swapped]),
    )
    pair = jnp.stack([mine, halves])
    messages = [pair] + [lax.ppermute(pair, "heads", pairs_x(flip)) for flip in (1, 3, 2)]
    over_x = exchanged(partial.reshape(NX, share_rows, key_count), "heads", groups_x).sum(axis=0)
    over_x, pair = lax.optimization_barrier((over_x, pair))
    other = lax.ppermute(over_x, "heads", pairs_zh)
    dlogit = call(dlogit_kernel, shape((NX, share_rows, key_count), f32))(
        over_x, other, logits, stats
    )
    dlogit = exchanged(dlogit, "heads", groups_x).reshape(query_count, key_count)
    dlogit, messages[1], messages[2] = lax.optimization_barrier((dlogit, messages[1], messages[2]))

    query_lines = query_count * index_heads
    piece_rows = -(-(query_lines + index_heads) // (NYC * 8)) * 8
    both = call(
        lambda *refs: grad_kernel(index_heads, index_scale, *refs),
        shape((piece_rows * NYC, 128), f32),
        flops=2 * index_flops,
        moved=2 << 20,
    )(dlogit, mine, index_keys)

    piece = exchanged(both.reshape(NYC, piece_rows, 128), "tokens", groups_yc)
    piece = call(sum_kernel, shape((NZ // 2, piece_rows, 128), f32))(piece)
    piece = exchanged(piece, "tokens", groups_z4).sum(axis=0)
    other = lax.ppermute(piece, "tokens", pairs_z4)
    piece = call(pair_kernel, shape((NYC, piece_rows, 128), f32))(piece, other)
    both = exchanged(piece, "tokens", groups_yc).reshape(-1, 128)
    query_grad = both[:query_lines].reshape(query_count, index_heads, index_width)
    weight_grad = both[query_lines : query_lines + index_heads, :query_count].T

    key_grad = call(
        lambda *refs: key_kernel(index_heads, index_scale, *refs),
        shape((key_count, index_width), f32),
        flops=2 * index_flops * NX * NZH,
        moved=3 << 20,
    )(dlogit, index_keys, *messages)
    return (query_grad, weight_grad, key_grad)


def solution(mesh):
    placed = (
        P("heads", "tokens", None),
        P("tokens", None),
        P(None, "heads", None),
        P("tokens", None),
        P(None, "heads"),
        P(),
    )
    return jax.shard_map(
        local,
        mesh=mesh,
        in_specs=placed,
        out_specs=(P(None, "heads", None), P(None, "heads"), P("tokens", None)),
        check_vma=False,
    )
```

```python
import jax
import jax.numpy as jnp
from jax import lax
from jax.experimental import pallas as pl
from jax.experimental.pallas import tpu as pltpu
from jax.sharding import PartitionSpec as P

H = 128
NX, NZH = 4, 2
NY, NZ, NC = 4, 8, 2
NYC = NY * NC
GRAD_SCALE = 8192.0
VMEM = 12 << 20
WEIGHT = 160

softmax_scale = 192.0 ** (-0.5)
masked_value = -1e30
f32, bf16 = jnp.float32, jnp.bfloat16


def token_at(y, z, c):
    return (y * NZ + z) * NC + c


def head_at(x, z):
    return x * NZH + z


all_y, all_z, all_c = range(NY), range(NZ), range(NC)
groups_z = [[token_at(y, z, c) for z in all_z] for y in all_y for c in all_c]
groups_z4 = [
    [token_at(y, half + z, c) for z in range(4)] for half in (0, 4) for y in all_y for c in all_c
]
pairs_c = [(token_at(y, z, c), token_at(y, z, 1 - c)) for y in all_y for z in all_z for c in all_c]
groups_y = [[token_at(y, z, c) for y in all_y] for z in all_z for c in all_c]
groups_yc = [[token_at(y, z, c) for c in all_c for y in all_y] for z in all_z]
pairs_z4 = [(token_at(y, z, c), token_at(y, z ^ 4, c)) for y in all_y for z in all_z for c in all_c]
groups_x = [[head_at(x, z) for x in range(NX)] for z in range(NZH)]
pairs_zh = [(head_at(x, z), head_at(x, 1 - z)) for x in range(NX) for z in range(NZH)]


def pairs_x(flip):
    return [(head_at(x, z), head_at(x ^ flip, z)) for x in range(NX) for z in range(NZH)]


def exchanged(parts, axis, groups):
    return lax.all_to_all(parts, axis, 0, 0, tiled=True, axis_index_groups=groups)


def gathered(value, axis, groups):
    copies = jnp.broadcast_to(value[None], (len(groups[0]), *value.shape))
    return exchanged(copies, axis, groups)


def diagonal(rows, lanes):
    return lax.broadcasted_iota(jnp.int32, (rows, lanes), 0) == lax.broadcasted_iota(
        jnp.int32, (rows, lanes), 1
    )


def as_row(column, lanes=128):
    return jnp.sum(jnp.where(diagonal(column.shape[0], lanes), column, 0.0), axis=0, keepdims=True)


def as_column(row, rows):
    return jnp.sum(jnp.where(diagonal(rows, row.shape[1]), row, 0.0), axis=1, keepdims=True)


def call(kernel, out_shape, flops=0, moved=0, aliases={}):
    return pl.pallas_call(
        kernel,
        out_shape=out_shape,
        input_output_aliases=aliases,
        compiler_params=pltpu.CompilerParams(vmem_limit_bytes=VMEM),
        cost_estimate=pl.CostEstimate(flops=flops, bytes_accessed=moved, transcendentals=0),
    )


def score_kernel(core_ref, limit_ref, q_ref, k_ref, *refs):
    e_ref, m_ref, l_ref = refs[-3:]
    block = e_ref.shape[0] // NYC
    key = lax.broadcasted_iota(jnp.int32, (1, e_ref.shape[1]), 1)
    k = k_ref[...]
    core = core_ref[0]
    for y in range(NY):
        line = core * NY + y
        lines = pl.ds(pl.multiple_of(line * block, block), block)
        s = jnp.dot(q_ref[y * block : (y + 1) * block], k, preferred_element_type=f32)
        s = jnp.where(key <= limit_ref[lines], s * softmax_scale, masked_value)
        m = jnp.max(s, axis=1, keepdims=True)
        e = jnp.exp(s - m)
        e_ref[lines] = e
        m_ref[pl.ds(line, 1)] = as_row(m)
        l_ref[pl.ds(line, 1)] = as_row(jnp.sum(e, axis=1, keepdims=True))


def message_parts(ref, tokens, heads):
    block = ref[tokens * heads :, :].astype(f32)
    w = block[:, :heads] + block[:, heads : 2 * heads] + block[:, 2 * heads : 3 * heads]
    return ref[: tokens * heads, :], w


def index_dot(iq, ik):
    return lax.dot_general(iq, ik, (((1,), (1,)), ((), ())), preferred_element_type=f32)


def logits_kernel(heads, scale, message_ref, ik_ref, out_ref):
    tokens = out_ref.shape[0]
    iq, w = message_parts(message_ref, tokens, heads)
    active = index_dot(iq, ik_ref[...])
    logits = jnp.zeros(out_ref.shape, f32)
    for j in range(heads):
        here = active[j * tokens : (j + 1) * tokens] * scale
        logits = logits + w[:, j : j + 1] * jnp.maximum(here, 0.0)
    out_ref[...] = logits


def index_stats_kernel(limit_ref, one_ref, two_ref, logits_ref, stat_ref):
    key = lax.broadcasted_iota(jnp.int32, (1, logits_ref.shape[1]), 1)
    logits = jnp.where(key <= limit_ref[...], one_ref[...] + two_ref[...], masked_value)
    m = jnp.max(logits, axis=1, keepdims=True)
    l = jnp.sum(jnp.exp(logits - m), axis=1, keepdims=True)
    logits_ref[...] = logits
    stat_ref[...] = jnp.concatenate([as_row(m), as_row(l), jnp.zeros((6, 128), f32)], axis=0)


def joined(stats):
    def one(m, l):
        top = jnp.max(m, axis=0)
        return top, jnp.sum(l * jnp.exp(m - top), axis=0)

    return (*one(stats[:, 0:8], stats[:, 8:16]), *one(stats[:, 16:17], stats[:, 17:18]))


def join_kernel(stats_ref, out_ref):
    lines = jnp.concatenate([*joined(stats_ref[...]), jnp.zeros((6, 128), f32)], axis=0)
    out_ref[...] = jnp.broadcast_to(lines[None], out_ref.shape)


def target_kernel(stats_ref, m_ref, e_ref, out_ref):
    top, total, _, _ = joined(stats_ref[...])
    weights = jnp.exp(m_ref[...] - top) / total
    keys = out_ref.shape[1]
    block = e_ref.shape[0] // NYC
    for b in range(NYC):
        e = e_ref[b * block : (b + 1) * block] * as_column(weights[b : b + 1], block)
        out_ref[b * NZ : (b + 1) * NZ] = jnp.sum(e.reshape(NZ, block // NZ, keys), axis=1)


def dlogit_kernel(one_ref, two_ref, logits_ref, stats_ref, out_ref):
    rows = logits_ref.shape[0]
    _, _, top, total = joined(stats_ref[...])
    probs = jnp.exp(logits_ref[...] - as_column(top, rows)) / as_column(total, rows)
    dlogit = GRAD_SCALE * (probs - (one_ref[...] + two_ref[...]) / H)
    out_ref[...] = jnp.broadcast_to(dlogit[None], out_ref.shape)


def grad_kernel(heads, scale, d_ref, message_ref, ik_ref, out_ref):
    dlogit = d_ref[...]
    tokens = dlogit.shape[0]
    iq, w = message_parts(message_ref, tokens, heads)
    ik = ik_ref[...]
    active = index_dot(iq, ik)
    row = lax.broadcasted_iota(jnp.int32, (tokens, 128), 0)
    place = row // NZ % NY * (NC * NZ) + row % NZ * NC + row // (NY * NZ)
    places = place == lax.broadcasted_iota(jnp.int32, (tokens, 128), 1)
    out_ref[tokens * heads :, :] = jnp.zeros((out_ref.shape[0] - tokens * heads, 128), f32)
    for j in range(heads):
        here = active[j * tokens : (j + 1) * tokens]
        gate = jnp.where(here > 0.0, dlogit * w[:, j : j + 1], 0.0).astype(bf16)
        grad = jnp.dot(gate, ik, preferred_element_type=f32) * scale
        for b in range(NYC):
            first = b % NY * (NZ * NC) + b // NY
            lines = pl.ds(first * heads + j, NZ, stride=NC * heads)
            out_ref[lines, :] = grad[b * NZ : (b + 1) * NZ]
        weight_grad = jnp.sum(dlogit * jnp.maximum(here * scale, 0.0), axis=1, keepdims=True)
        out_ref[tokens * heads + j : tokens * heads + j + 1, :] = jnp.sum(
            jnp.where(places, weight_grad, 0.0), axis=0, keepdims=True
        )


def key_kernel(heads, scale, d_ref, ik_ref, *refs):
    messages, out_ref = refs[:-1], refs[-1]
    dlogit, ik = d_ref[...], ik_ref[...]
    tokens, keys = dlogit.shape
    total = jnp.zeros((ik.shape[1], keys), f32)
    for message in messages:
        for part in range(message.shape[0]):
            iq, w = message_parts(message.at[part], tokens, heads)
            active = index_dot(iq, ik)
            gates = []
            for j in range(heads):
                here = active[j * tokens : (j + 1) * tokens]
                gates.append(jnp.where(here > 0.0, dlogit * w[:, j : j + 1], 0.0).astype(bf16))
            gate = jnp.concatenate(gates, axis=0)
            total = total + jnp.dot(iq.T, gate, preferred_element_type=f32)
    out_ref[...] = total.T * scale


def sum_kernel(parts_ref, out_ref):
    out_ref[...] = jnp.broadcast_to(jnp.sum(parts_ref[...], axis=0)[None], out_ref.shape)


def pair_kernel(one_ref, two_ref, out_ref):
    out_ref[...] = jnp.broadcast_to((one_ref[...] + two_ref[...])[None], out_ref.shape)


def in_order(value):
    return jnp.moveaxis(value.reshape(NY, NZ, NC, *value.shape[1:]), 2, 0).reshape(value.shape)


def x_scatter_sum(parts, x):
    total = lax.dynamic_index_in_dim(parts, x, 0, keepdims=False)
    for flip in range(1, NX):
        piece = lax.dynamic_index_in_dim(parts, x ^ flip, 0, keepdims=False)
        total = total + lax.ppermute(piece, "heads", pairs_x(flip))
    return total


def local(queries, latent_keys, index_queries, index_keys, index_weights, positions):
    heads_here, width = queries.shape[0], queries.shape[2]
    key_count = latent_keys.shape[0]
    query_count, index_heads, index_width = index_queries.shape
    index_scale = index_width ** (-0.5)
    share_rows = query_count // NX
    shape = jax.ShapeDtypeStruct
    x = lax.axis_index("heads") // NZH
    core = lax.axis_index("tokens") % NC
    limit = in_order(positions - lax.axis_index("tokens") * key_count)

    along_z = gathered(queries.reshape(heads_here, width), "tokens", groups_z)

    high = lax.reduce_precision(index_weights, 8, 7)
    middle = lax.reduce_precision(index_weights - high, 8, 7)
    low = index_weights - high - middle
    lines = in_order(jnp.concatenate([high, middle, low], axis=1))
    lines = jnp.pad(lines, ((0, 0), (0, 128 - 3 * index_heads)))
    by_head = in_order(index_queries).transpose(1, 0, 2)
    by_head = by_head.reshape(index_heads * query_count, index_width)
    mine = jnp.concatenate([by_head, lines.astype(bf16)])

    index_flops = 2 * query_count * index_heads * key_count * index_width
    partial = call(
        lambda *refs: logits_kernel(index_heads, index_scale, *refs),
        shape((query_count, key_count), f32),
        flops=index_flops,
        moved=1 << 20,
    )(mine, index_keys)
    over_x = x_scatter_sum(partial.reshape(NX, share_rows, key_count), x)
    other = lax.ppermute(over_x, "heads", pairs_zh)
    share_limit = lax.dynamic_slice_in_dim(limit, x * share_rows, share_rows, 0)
    logits, index_stats = call(
        index_stats_kernel,
        (shape((share_rows, key_count), f32), shape((8, 128), f32)),
        flops=WEIGHT * index_flops,
        moved=1 << 20,
    )(share_limit[:, None], over_x, other)

    rows = gathered(along_z, "tokens", groups_y)
    other_rows = lax.ppermute(rows, "tokens", pairs_c)
    row_count = NC * rows.size // width
    row_limit = jnp.repeat(limit, heads_here)[:, None]
    lines_shape = shape((NYC, row_count // NYC), f32)
    scored = ()
    for where, part in ((core, rows), (1 - core, other_rows)):
        scored = call(
            score_kernel,
            (shape((row_count, key_count), f32), lines_shape, lines_shape),
            flops=row_count * key_count * width,
            moved=4 << 20,
            aliases={4 + i: i for i in range(len(scored))},
        )(where.reshape(1), row_limit, part.reshape(-1, width), latent_keys.T, *scored)
    exponent, local_max, local_total = scored

    stats = jnp.concatenate([local_max, local_total, index_stats])

    stats = gathered(stats, "tokens", groups_z)
    stats = call(join_kernel, shape((NYC, *stats.shape[1:]), f32))(stats)
    stats = exchanged(stats, "tokens", groups_yc)

    partial = call(target_kernel, shape((query_count, key_count), f32), moved=5 << 20)(
        stats, local_max, exponent
    )

    mine_rows = mine.shape[0] // NC
    partial, late = lax.optimization_barrier((partial, mine))
    sent = lax.dynamic_slice_in_dim(late, core * mine_rows, mine_rows, 0)
    swapped = lax.ppermute(sent, "heads", pairs_zh)
    over_x = exchanged(partial.reshape(NX, share_rows, key_count), "heads", groups_x).sum(axis=0)
    other = lax.ppermute(over_x, "heads", pairs_zh)
    other, swapped = lax.optimization_barrier((other, swapped))
    dlogit = call(dlogit_kernel, shape((NX, share_rows, key_count), f32))(
        over_x, other, logits, stats
    )
    dlogit, swapped = lax.optimization_barrier((dlogit, swapped))
    swapped_other = lax.ppermute(swapped, "tokens", pairs_c)
    dlogit = exchanged(dlogit, "heads", groups_x).reshape(query_count, key_count)
    halves = jnp.where(
        core == 0,
        jnp.concatenate([swapped, swapped_other]),
        jnp.concatenate([swapped_other, swapped]),
    )
    pair = jnp.stack([mine, halves])
    nearer = jnp.concatenate([pair, lax.ppermute(pair, "heads", pairs_x(1))])
    messages = [nearer, lax.ppermute(nearer, "heads", pairs_x(2))]

    query_lines = query_count * index_heads
    piece_rows = -(-(query_lines + index_heads) // (NYC * 8)) * 8
    both = call(
        lambda *refs: grad_kernel(index_heads, index_scale, *refs),
        shape((piece_rows * NYC, 128), f32),
        flops=2 * index_flops,
        moved=2 << 20,
    )(dlogit, mine, index_keys)

    piece = exchanged(both.reshape(NYC, piece_rows, 128), "tokens", groups_yc)
    piece = call(sum_kernel, shape((NZ // 2, piece_rows, 128), f32))(piece)
    piece = exchanged(piece, "tokens", groups_z4).sum(axis=0)
    other = lax.ppermute(piece, "tokens", pairs_z4)
    piece = call(pair_kernel, shape((NYC, piece_rows, 128), f32))(piece, other)
    both = exchanged(piece, "tokens", groups_yc).reshape(-1, 128)
    query_grad = both[:query_lines].reshape(query_count, index_heads, index_width)
    weight_grad = both[query_lines : query_lines + index_heads, :query_count].T

    key_grad = call(
        lambda *refs: key_kernel(index_heads, index_scale, *refs),
        shape((key_count, index_width), f32),
        flops=2 * index_flops * NX * NZH,
        moved=3 << 20,
    )(dlogit, index_keys, *messages)
    return (query_grad, weight_grad, key_grad)


def solution(mesh):
    placed = (
        P("heads", "tokens", None),
        P("tokens", None),
        P(None, "heads", None),
        P("tokens", None),
        P(None, "heads"),
        P(),
    )
    return jax.shard_map(
        local,
        mesh=mesh,
        in_specs=placed,
        out_specs=(P(None, "heads", None), P(None, "heads"), P("tokens", None)),
        check_vma=False,
    )
```

```python
import jax
import jax.numpy as jnp
from jax import lax
from jax.experimental import pallas as pl
from jax.experimental.pallas import tpu as pltpu
from jax.sharding import PartitionSpec as P

H = 128
NX, NZH = 4, 2
NY, NZ, NC = 4, 8, 2
NYC = NY * NC
GRAD_SCALE = 8192.0
VMEM = 12 << 20
WEIGHT = 20

softmax_scale = 192.0 ** (-0.5)
masked_value = -1e30
f32, bf16 = jnp.float32, jnp.bfloat16


def token_at(y, z, c):
    return (y * NZ + z) * NC + c


def head_at(x, z):
    return x * NZH + z


all_y, all_z, all_c = range(NY), range(NZ), range(NC)
groups_z = [[token_at(y, z, c) for z in all_z] for y in all_y for c in all_c]
groups_z4 = [
    [token_at(y, half + z, c) for z in range(4)] for half in (0, 4) for y in all_y for c in all_c
]
pairs_c = [(token_at(y, z, c), token_at(y, z, 1 - c)) for y in all_y for z in all_z for c in all_c]
groups_yc = [[token_at(y, z, c) for c in all_c for y in all_y] for z in all_z]
pairs_z4 = [(token_at(y, z, c), token_at(y, z ^ 4, c)) for y in all_y for z in all_z for c in all_c]
groups_x = [[head_at(x, z) for x in range(NX)] for z in range(NZH)]
pairs_zh = [(head_at(x, z), head_at(x, 1 - z)) for x in range(NX) for z in range(NZH)]


def pairs_x(flip):
    return [(head_at(x, z), head_at(x ^ flip, z)) for x in range(NX) for z in range(NZH)]


def exchanged(parts, axis, groups):
    return lax.all_to_all(parts, axis, 0, 0, tiled=True, axis_index_groups=groups)


def gathered(value, axis, groups):
    copies = jnp.broadcast_to(value[None], (len(groups[0]), *value.shape))
    return exchanged(copies, axis, groups)


def diagonal(rows, lanes):
    return lax.broadcasted_iota(jnp.int32, (rows, lanes), 0) == lax.broadcasted_iota(
        jnp.int32, (rows, lanes), 1
    )


def as_row(column, lanes=128):
    return jnp.sum(jnp.where(diagonal(column.shape[0], lanes), column, 0.0), axis=0, keepdims=True)


def as_column(row, rows):
    return jnp.sum(jnp.where(diagonal(rows, row.shape[1]), row, 0.0), axis=1, keepdims=True)


def call(kernel, out_shape, flops=0, moved=0):
    return pl.pallas_call(
        kernel,
        out_shape=out_shape,
        compiler_params=pltpu.CompilerParams(vmem_limit_bytes=VMEM),
        cost_estimate=pl.CostEstimate(flops=flops, bytes_accessed=moved, transcendentals=0),
    )


def score_kernel(limit_ref, q_ref, k_ref, e_ref, m_ref, l_ref):
    block = e_ref.shape[0] // NYC
    key = lax.broadcasted_iota(jnp.int32, (1, e_ref.shape[1]), 1)
    k = k_ref[...]
    for b in range(NYC):
        lines = slice(b * block, (b + 1) * block)
        s = jnp.dot(q_ref[lines], k, preferred_element_type=f32) * softmax_scale
        s = jnp.where(key <= limit_ref[lines], s, masked_value)
        m = jnp.max(s, axis=1, keepdims=True)
        e = jnp.exp(s - m)
        e_ref[lines] = e
        m_ref[b : b + 1] = as_row(m)
        l_ref[b : b + 1] = as_row(jnp.sum(e, axis=1, keepdims=True))


def message_parts(one_ref, two_ref, tokens, heads):
    rows = tokens * heads

    def weights(ref):
        block = ref[rows:, :].astype(f32)
        return block[:, :heads] + block[:, heads : 2 * heads] + block[:, 2 * heads : 3 * heads]

    iq = jnp.concatenate([one_ref[:rows, :], two_ref[:rows, :]])
    return iq, [w[:, j : j + 1] for w in (weights(one_ref), weights(two_ref)) for j in range(heads)]


def index_dot(iq, ik):
    return lax.dot_general(iq, ik, (((1,), (1,)), ((), ())), preferred_element_type=f32)


def logits_kernel(heads, scale, mine_ref, one_ref, two_ref, ik_ref, out_ref):
    tokens = out_ref.shape[0]
    ik = ik_ref[...]
    logits = jnp.zeros(out_ref.shape, f32)
    for pair in ((mine_ref.at[0], mine_ref.at[1]), (one_ref.at[0], two_ref.at[0])):
        iq, weights = message_parts(*pair, tokens, heads)
        active = index_dot(iq, ik)
        for j, w in enumerate(weights):
            here = active[j * tokens : (j + 1) * tokens] * scale
            logits = logits + w * jnp.maximum(here, 0.0)
    out_ref[...] = logits


def index_stats_kernel(limit_ref, sum_ref, logits_ref, stat_ref):
    key = lax.broadcasted_iota(jnp.int32, (1, logits_ref.shape[1]), 1)
    logits = jnp.where(key <= limit_ref[...], sum_ref[...], masked_value)
    m = jnp.max(logits, axis=1, keepdims=True)
    l = jnp.sum(jnp.exp(logits - m), axis=1, keepdims=True)
    logits_ref[...] = logits
    stat_ref[...] = jnp.concatenate([as_row(m), as_row(l), jnp.zeros((6, 128), f32)], axis=0)


def joined(stats):
    def one(m, l):
        top = jnp.max(m, axis=0)
        return top, jnp.sum(l * jnp.exp(m - top), axis=0)

    return (*one(stats[:, 0:8], stats[:, 8:16]), *one(stats[:, 16:17], stats[:, 17:18]))


def join_kernel(stats_ref, out_ref):
    lines = jnp.concatenate([*joined(stats_ref[...]), jnp.zeros((6, 128), f32)], axis=0)
    out_ref[...] = jnp.broadcast_to(lines[None], out_ref.shape)


def target_kernel(stats_ref, m_ref, e_ref, out_ref):
    top, total, _, _ = joined(stats_ref[...])
    weights = jnp.exp(m_ref[...] - top) / total
    keys = out_ref.shape[1]
    block = e_ref.shape[0] // NYC
    for b in range(NYC):
        e = e_ref[b * block : (b + 1) * block] * as_column(weights[b : b + 1], block)
        out_ref[b * NZ : (b + 1) * NZ] = jnp.sum(e.reshape(NZ, block // NZ, keys), axis=1)


def dlogit_kernel(one_ref, two_ref, logits_ref, stats_ref, out_ref):
    rows = logits_ref.shape[0]
    _, _, top, total = joined(stats_ref[...])
    probs = jnp.exp(logits_ref[...] - as_column(top, rows)) / as_column(total, rows)
    dlogit = GRAD_SCALE * (probs - (one_ref[...] + two_ref[...]) / H)
    out_ref[...] = jnp.broadcast_to(dlogit[None], out_ref.shape)


def grad_kernel(heads, scale, d_ref, message_ref, ik_ref, out_ref):
    dlogit = d_ref[...]
    tokens = dlogit.shape[0]
    iq, weights = message_parts(message_ref.at[0], message_ref.at[1], tokens, heads)
    ik = ik_ref[...]
    active = index_dot(iq, ik)
    heads = len(weights)
    row = lax.broadcasted_iota(jnp.int32, (tokens, 128), 0)
    place = row // NZ % NY * (NC * NZ) + row % NZ * NC + row // (NY * NZ)
    places = place == lax.broadcasted_iota(jnp.int32, (tokens, 128), 1)
    out_ref[tokens * heads :, :] = jnp.zeros((out_ref.shape[0] - tokens * heads, 128), f32)
    for j, w in enumerate(weights):
        here = active[j * tokens : (j + 1) * tokens]
        gate = jnp.where(here > 0.0, dlogit * w, 0.0).astype(bf16)
        grad = jnp.dot(gate, ik, preferred_element_type=f32) * scale
        for b in range(NYC):
            first = b % NY * (NZ * NC) + b // NY
            lines = pl.ds(first * heads + j, NZ, stride=NC * heads)
            out_ref[lines, :] = grad[b * NZ : (b + 1) * NZ]
        weight_grad = jnp.sum(dlogit * jnp.maximum(here * scale, 0.0), axis=1, keepdims=True)
        out_ref[tokens * heads + j : tokens * heads + j + 1, :] = jnp.sum(
            jnp.where(places, weight_grad, 0.0), axis=0, keepdims=True
        )


def key_kernel(heads, scale, d_ref, ik_ref, *refs):
    messages, out_ref = refs[:-1], refs[-1]
    dlogit, ik = d_ref[...], ik_ref[...]
    tokens, keys = dlogit.shape
    total = jnp.zeros((ik.shape[1], keys), f32)
    for message in messages:
        for part in range(0, message.shape[0], 2):
            iq, weights = message_parts(message.at[part], message.at[part + 1], tokens, heads)
            active = index_dot(iq, ik)
            gates = []
            for j, w in enumerate(weights):
                here = active[j * tokens : (j + 1) * tokens]
                gates.append(jnp.where(here > 0.0, dlogit * w, 0.0).astype(bf16))
            gate = jnp.concatenate(gates, axis=0)
            total = total + jnp.dot(iq.T, gate, preferred_element_type=f32)
    out_ref[...] = total.T * scale


def sum_kernel(parts_ref, out_ref):
    out_ref[...] = jnp.broadcast_to(jnp.sum(parts_ref[...], axis=0)[None], out_ref.shape)


def pair_kernel(one_ref, two_ref, out_ref):
    out_ref[...] = jnp.broadcast_to((one_ref[...] + two_ref[...])[None], out_ref.shape)


def in_order(value):
    return jnp.moveaxis(value.reshape(NY, NZ, NC, *value.shape[1:]), 2, 0).reshape(value.shape)


def x_scatter_sum(parts, x):
    total = lax.dynamic_index_in_dim(parts, x, 0, keepdims=False)
    for flip in range(1, NX):
        piece = lax.dynamic_index_in_dim(parts, x ^ flip, 0, keepdims=False)
        total = total + lax.ppermute(piece, "heads", pairs_x(flip))
    return total


def local(queries, latent_keys, index_queries, index_keys, index_weights, positions):
    heads_here, width = queries.shape[0], queries.shape[2]
    key_count = latent_keys.shape[0]
    query_count, index_heads, index_width = index_queries.shape
    index_scale = index_width ** (-0.5)
    share_rows = query_count // NX
    shape = jax.ShapeDtypeStruct
    x = lax.axis_index("heads") // NZH
    core = lax.axis_index("tokens") % NC
    limit = in_order(positions - lax.axis_index("tokens") * key_count)

    along_z = gathered(queries.reshape(heads_here, width), "tokens", groups_z)

    high = lax.reduce_precision(index_weights, 8, 7)
    middle = lax.reduce_precision(index_weights - high, 8, 7)
    low = index_weights - high - middle
    half = index_heads // NC
    lines = jnp.stack([high, middle, low], axis=1).reshape(query_count, 3, NC, half)
    lines = in_order(lines.transpose(0, 2, 1, 3).reshape(query_count, NC, 3 * half))
    lines = jnp.pad(lines.transpose(1, 0, 2), ((0, 0), (0, 0), (0, 128 - 3 * half)))
    by_head = in_order(index_queries).transpose(1, 0, 2)
    by_head = by_head.reshape(NC, half * query_count, index_width)
    mine = jnp.concatenate([by_head, lines.astype(bf16)], axis=1)

    first = lax.ppermute(lax.dynamic_index_in_dim(mine, core, 0), "heads", pairs_zh)
    second = lax.ppermute(first, "tokens", pairs_c)

    index_flops = 2 * query_count * index_heads * key_count * index_width
    partial = call(
        lambda *refs: logits_kernel(half, index_scale, *refs),
        shape((query_count, key_count), f32),
        flops=2 * index_flops,
        moved=1 << 20,
    )(mine, first, second, index_keys)
    over_x = x_scatter_sum(partial.reshape(NX, share_rows, key_count), x)
    share_limit = lax.dynamic_slice_in_dim(limit, x * share_rows, share_rows, 0)
    logits, index_stats = call(
        index_stats_kernel,
        (shape((share_rows, key_count), f32), shape((8, 128), f32)),
        flops=WEIGHT * index_flops,
        moved=1 << 20,
    )(share_limit[:, None], over_x)

    rows = gathered(along_z, "tokens", groups_yc).reshape(-1, width)
    row_count = rows.shape[0]
    lines_shape = shape((NYC, row_count // NYC), f32)
    exponent, local_max, local_total = call(
        score_kernel,
        (shape((row_count, key_count), f32), lines_shape, lines_shape),
        flops=2 * row_count * key_count * width,
        moved=4 << 20,
    )(jnp.repeat(limit, heads_here)[:, None], rows, latent_keys.T)

    stats = jnp.concatenate([local_max, local_total, index_stats])

    stats = gathered(stats, "tokens", groups_z)
    stats = call(join_kernel, shape((NYC, *stats.shape[1:]), f32))(stats)
    stats = exchanged(stats, "tokens", groups_yc)

    partial = call(target_kernel, shape((query_count, key_count), f32), moved=5 << 20)(
        stats, local_max, exponent
    )

    over_x = exchanged(partial.reshape(NX, share_rows, key_count), "heads", groups_x).sum(axis=0)
    other = lax.ppermute(over_x, "heads", pairs_zh)
    dlogit = call(dlogit_kernel, shape((NX, share_rows, key_count), f32))(
        over_x, other, logits, stats
    )
    dlogit = exchanged(dlogit, "heads", groups_x).reshape(query_count, key_count)
    four = jnp.concatenate([mine, first, second])
    nearer = jnp.concatenate([four, lax.ppermute(four, "heads", pairs_x(1))])
    messages = [nearer, lax.ppermute(nearer, "heads", pairs_x(2))]

    query_lines = query_count * index_heads
    piece_rows = -(-(query_lines + index_heads) // (NYC * 8)) * 8
    both = call(
        lambda *refs: grad_kernel(half, index_scale, *refs),
        shape((piece_rows * NYC, 128), f32),
        flops=2 * index_flops,
        moved=2 << 20,
    )(dlogit, mine, index_keys)

    piece = exchanged(both.reshape(NYC, piece_rows, 128), "tokens", groups_yc)
    piece = call(sum_kernel, shape((NZ // 2, piece_rows, 128), f32))(piece)
    piece = exchanged(piece, "tokens", groups_z4).sum(axis=0)
    other = lax.ppermute(piece, "tokens", pairs_z4)
    piece = call(pair_kernel, shape((NYC, piece_rows, 128), f32))(piece, other)
    both = exchanged(piece, "tokens", groups_yc).reshape(-1, 128)
    query_grad = both[:query_lines].reshape(query_count, index_heads, index_width)
    weight_grad = both[query_lines : query_lines + index_heads, :query_count].T

    key_grad = call(
        lambda *refs: key_kernel(half, index_scale, *refs),
        shape((key_count, index_width), f32),
        flops=2 * index_flops * NX * NZH,
        moved=3 << 20,
    )(dlogit, index_keys, *messages)
    return (query_grad, weight_grad, key_grad)


def solution(mesh):
    placed = (
        P("heads", "tokens", None),
        P("tokens", None),
        P(None, "heads", None),
        P("tokens", None),
        P(None, "heads"),
        P(),
    )
    return jax.shard_map(
        local,
        mesh=mesh,
        in_specs=placed,
        out_specs=(P(None, "heads", None), P(None, "heads"), P("tokens", None)),
        check_vma=False,
    )
```

```python
import jax
import jax.numpy as jnp
from jax import lax
from jax.experimental import pallas as pl
from jax.experimental.pallas import tpu as pltpu
from jax.sharding import PartitionSpec as P

H = 128
NX, NZH = 4, 2
NY, NZ, NC = 4, 8, 2
NYC = NY * NC
GRAD_SCALE = 8192.0
VMEM = 12 << 20
WEIGHT = 20

softmax_scale = 192.0 ** (-0.5)
masked_value = -1e30
f32, bf16 = jnp.float32, jnp.bfloat16


def token_at(y, z, c):
    return (y * NZ + z) * NC + c


def head_at(x, z):
    return x * NZH + z


all_y, all_z, all_c = range(NY), range(NZ), range(NC)
groups_z = [[token_at(y, z, c) for z in all_z] for y in all_y for c in all_c]
groups_z4 = [
    [token_at(y, half + z, c) for z in range(4)] for half in (0, 4) for y in all_y for c in all_c
]
pairs_c = [(token_at(y, z, c), token_at(y, z, 1 - c)) for y in all_y for z in all_z for c in all_c]
groups_yc = [[token_at(y, z, c) for c in all_c for y in all_y] for z in all_z]
pairs_z4 = [(token_at(y, z, c), token_at(y, z ^ 4, c)) for y in all_y for z in all_z for c in all_c]
groups_x = [[head_at(x, z) for x in range(NX)] for z in range(NZH)]
pairs_zh = [(head_at(x, z), head_at(x, 1 - z)) for x in range(NX) for z in range(NZH)]


def pairs_x(flip):
    return [(head_at(x, z), head_at(x ^ flip, z)) for x in range(NX) for z in range(NZH)]


def exchanged(parts, axis, groups):
    return lax.all_to_all(parts, axis, 0, 0, tiled=True, axis_index_groups=groups)


def gathered(value, axis, groups):
    copies = jnp.broadcast_to(value[None], (len(groups[0]), *value.shape))
    return exchanged(copies, axis, groups)


def diagonal(rows, lanes):
    return lax.broadcasted_iota(jnp.int32, (rows, lanes), 0) == lax.broadcasted_iota(
        jnp.int32, (rows, lanes), 1
    )


def as_row(column, lanes=128):
    return jnp.sum(jnp.where(diagonal(column.shape[0], lanes), column, 0.0), axis=0, keepdims=True)


def as_column(row, rows):
    return jnp.sum(jnp.where(diagonal(rows, row.shape[1]), row, 0.0), axis=1, keepdims=True)


def call(kernel, out_shape, flops=0, moved=0):
    return pl.pallas_call(
        kernel,
        out_shape=out_shape,
        compiler_params=pltpu.CompilerParams(vmem_limit_bytes=VMEM),
        cost_estimate=pl.CostEstimate(flops=flops, bytes_accessed=moved, transcendentals=0),
    )


def score_kernel(limit_ref, q_ref, k_ref, e_ref, m_ref, l_ref):
    block = e_ref.shape[0] // NYC
    key = lax.broadcasted_iota(jnp.int32, (1, e_ref.shape[1]), 1)
    k = k_ref[...]
    for b in range(NYC):
        lines = slice(b * block, (b + 1) * block)
        s = jnp.dot(q_ref[lines], k, preferred_element_type=f32) * softmax_scale
        s = jnp.where(key <= limit_ref[lines], s, masked_value)
        m = jnp.max(s, axis=1, keepdims=True)
        e = jnp.exp(s - m)
        e_ref[lines] = e
        m_ref[b : b + 1] = as_row(m)
        l_ref[b : b + 1] = as_row(jnp.sum(e, axis=1, keepdims=True))


def message_parts(one_ref, two_ref, tokens, heads):
    rows = tokens * heads

    def weights(ref):
        block = ref[rows:, :].astype(f32)
        return block[:, :heads] + block[:, heads : 2 * heads] + block[:, 2 * heads : 3 * heads]

    iq = jnp.concatenate([one_ref[:rows, :], two_ref[:rows, :]])
    return iq, [w[:, j : j + 1] for w in (weights(one_ref), weights(two_ref)) for j in range(heads)]


def index_dot(iq, ik):
    return lax.dot_general(iq, ik, (((1,), (1,)), ((), ())), preferred_element_type=f32)


def logits_kernel(heads, scale, mine_ref, one_ref, two_ref, ik_ref, out_ref):
    tokens = out_ref.shape[0]
    ik = ik_ref[...]
    logits = jnp.zeros(out_ref.shape, f32)
    for pair in ((mine_ref.at[0], mine_ref.at[1]), (one_ref.at[0], two_ref.at[0])):
        iq, weights = message_parts(*pair, tokens, heads)
        active = index_dot(iq, ik)
        for j, w in enumerate(weights):
            here = active[j * tokens : (j + 1) * tokens] * scale
            logits = logits + w * jnp.maximum(here, 0.0)
    out_ref[...] = logits


def index_stats_kernel(limit_ref, sum_ref, logits_ref, stat_ref):
    key = lax.broadcasted_iota(jnp.int32, (1, logits_ref.shape[1]), 1)
    logits = jnp.where(key <= limit_ref[...], sum_ref[...], masked_value)
    m = jnp.max(logits, axis=1, keepdims=True)
    l = jnp.sum(jnp.exp(logits - m), axis=1, keepdims=True)
    logits_ref[...] = logits
    stat_ref[...] = jnp.concatenate([as_row(m), as_row(l), jnp.zeros((6, 128), f32)], axis=0)


def joined(stats):
    def one(m, l):
        top = jnp.max(m, axis=0)
        return top, jnp.sum(l * jnp.exp(m - top), axis=0)

    return (*one(stats[:, 0:8], stats[:, 8:16]), *one(stats[:, 16:17], stats[:, 17:18]))


def join_kernel(stats_ref, out_ref):
    lines = jnp.concatenate([*joined(stats_ref[...]), jnp.zeros((6, 128), f32)], axis=0)
    out_ref[...] = jnp.broadcast_to(lines[None], out_ref.shape)


def target_kernel(stats_ref, m_ref, e_ref, out_ref):
    top, total, _, _ = joined(stats_ref[...])
    weights = jnp.exp(m_ref[...] - top) / total
    keys = out_ref.shape[1]
    block = e_ref.shape[0] // NYC
    for b in range(NYC):
        e = e_ref[b * block : (b + 1) * block] * as_column(weights[b : b + 1], block)
        out_ref[b * NZ : (b + 1) * NZ] = jnp.sum(e.reshape(NZ, block // NZ, keys), axis=1)


def dlogit_kernel(one_ref, two_ref, logits_ref, stats_ref, out_ref):
    rows = logits_ref.shape[0]
    _, _, top, total = joined(stats_ref[...])
    probs = jnp.exp(logits_ref[...] - as_column(top, rows)) / as_column(total, rows)
    dlogit = GRAD_SCALE * (probs - (one_ref[...] + two_ref[...]) / H)
    out_ref[...] = jnp.broadcast_to(dlogit[None], out_ref.shape)


def grad_kernel(heads, scale, d_ref, message_ref, ik_ref, out_ref):
    dlogit = d_ref[...]
    tokens = dlogit.shape[0]
    iq, weights = message_parts(message_ref.at[0], message_ref.at[1], tokens, heads)
    ik = ik_ref[...]
    active = index_dot(iq, ik)
    heads = len(weights)
    row = lax.broadcasted_iota(jnp.int32, (tokens, 128), 0)
    place = row // NZ % NY * (NC * NZ) + row % NZ * NC + row // (NY * NZ)
    places = place == lax.broadcasted_iota(jnp.int32, (tokens, 128), 1)
    out_ref[tokens * heads :, :] = jnp.zeros((out_ref.shape[0] - tokens * heads, 128), f32)
    for j, w in enumerate(weights):
        here = active[j * tokens : (j + 1) * tokens]
        gate = jnp.where(here > 0.0, dlogit * w, 0.0).astype(bf16)
        grad = jnp.dot(gate, ik, preferred_element_type=f32) * scale
        for b in range(NYC):
            first = b % NY * (NZ * NC) + b // NY
            lines = pl.ds(first * heads + j, NZ, stride=NC * heads)
            out_ref[lines, :] = grad[b * NZ : (b + 1) * NZ]
        weight_grad = jnp.sum(dlogit * jnp.maximum(here * scale, 0.0), axis=1, keepdims=True)
        out_ref[tokens * heads + j : tokens * heads + j + 1, :] = jnp.sum(
            jnp.where(places, weight_grad, 0.0), axis=0, keepdims=True
        )


def key_kernel(heads, scale, d_ref, ik_ref, message, *refs):
    before, out_ref = refs[:-1], refs[-1]
    dlogit, ik = d_ref[...], ik_ref[...]
    tokens, keys = dlogit.shape
    total = jnp.zeros((ik.shape[1], keys), f32)
    for part in range(0, message.shape[0], 2):
        iq, weights = message_parts(message.at[part], message.at[part + 1], tokens, heads)
        active = index_dot(iq, ik)
        gates = []
        for j, w in enumerate(weights):
            here = active[j * tokens : (j + 1) * tokens]
            gates.append(jnp.where(here > 0.0, dlogit * w, 0.0).astype(bf16))
        gate = jnp.concatenate(gates, axis=0)
        total = total + jnp.dot(iq.T, gate, preferred_element_type=f32)
    grad = total.T * scale
    out_ref[...] = before[0][...] + grad if before else grad


def sum_kernel(parts_ref, out_ref):
    out_ref[...] = jnp.broadcast_to(jnp.sum(parts_ref[...], axis=0)[None], out_ref.shape)


def pair_kernel(one_ref, two_ref, out_ref):
    out_ref[...] = jnp.broadcast_to((one_ref[...] + two_ref[...])[None], out_ref.shape)


def in_order(value):
    return jnp.moveaxis(value.reshape(NY, NZ, NC, *value.shape[1:]), 2, 0).reshape(value.shape)


def x_scatter_sum(parts, x):
    total = lax.dynamic_index_in_dim(parts, x, 0, keepdims=False)
    for flip in range(1, NX):
        piece = lax.dynamic_index_in_dim(parts, x ^ flip, 0, keepdims=False)
        total = total + lax.ppermute(piece, "heads", pairs_x(flip))
    return total


def local(queries, latent_keys, index_queries, index_keys, index_weights, positions):
    heads_here, width = queries.shape[0], queries.shape[2]
    key_count = latent_keys.shape[0]
    query_count, index_heads, index_width = index_queries.shape
    index_scale = index_width ** (-0.5)
    share_rows = query_count // NX
    shape = jax.ShapeDtypeStruct
    x = lax.axis_index("heads") // NZH
    core = lax.axis_index("tokens") % NC
    limit = in_order(positions - lax.axis_index("tokens") * key_count)

    along_z = gathered(queries.reshape(heads_here, width), "tokens", groups_z)

    high = lax.reduce_precision(index_weights, 8, 7)
    middle = lax.reduce_precision(index_weights - high, 8, 7)
    low = index_weights - high - middle
    half = index_heads // NC
    lines = jnp.stack([high, middle, low], axis=1).reshape(query_count, 3, NC, half)
    lines = in_order(lines.transpose(0, 2, 1, 3).reshape(query_count, NC, 3 * half))
    lines = jnp.pad(lines.transpose(1, 0, 2), ((0, 0), (0, 0), (0, 128 - 3 * half)))
    by_head = in_order(index_queries).transpose(1, 0, 2)
    by_head = by_head.reshape(NC, half * query_count, index_width)
    mine = jnp.concatenate([by_head, lines.astype(bf16)], axis=1)

    first = lax.ppermute(lax.dynamic_index_in_dim(mine, core, 0), "heads", pairs_zh)
    second = lax.ppermute(first, "tokens", pairs_c)

    index_flops = 2 * query_count * index_heads * key_count * index_width
    partial = call(
        lambda *refs: logits_kernel(half, index_scale, *refs),
        shape((query_count, key_count), f32),
        flops=2 * index_flops,
        moved=1 << 20,
    )(mine, first, second, index_keys)
    over_x = x_scatter_sum(partial.reshape(NX, share_rows, key_count), x)
    share_limit = lax.dynamic_slice_in_dim(limit, x * share_rows, share_rows, 0)
    logits, index_stats = call(
        index_stats_kernel,
        (shape((share_rows, key_count), f32), shape((8, 128), f32)),
        flops=WEIGHT * index_flops,
        moved=1 << 20,
    )(share_limit[:, None], over_x)

    rows = gathered(along_z, "tokens", groups_yc).reshape(-1, width)
    row_count = rows.shape[0]
    lines_shape = shape((NYC, row_count // NYC), f32)
    exponent, local_max, local_total = call(
        score_kernel,
        (shape((row_count, key_count), f32), lines_shape, lines_shape),
        flops=2 * row_count * key_count * width,
        moved=4 << 20,
    )(jnp.repeat(limit, heads_here)[:, None], rows, latent_keys.T)

    stats = jnp.concatenate([local_max, local_total, index_stats])

    stats = gathered(stats, "tokens", groups_z)
    stats = call(join_kernel, shape((NYC, *stats.shape[1:]), f32))(stats)
    stats = exchanged(stats, "tokens", groups_yc)

    partial = call(target_kernel, shape((query_count, key_count), f32), moved=5 << 20)(
        stats, local_max, exponent
    )

    over_x = exchanged(partial.reshape(NX, share_rows, key_count), "heads", groups_x).sum(axis=0)
    other = lax.ppermute(over_x, "heads", pairs_zh)
    dlogit = call(dlogit_kernel, shape((NX, share_rows, key_count), f32))(
        over_x, other, logits, stats
    )
    dlogit, *three = lax.optimization_barrier((dlogit, mine, first, second))
    four = jnp.concatenate(three)
    near = lax.ppermute(four, "heads", pairs_x(1))
    dlogit = exchanged(dlogit, "heads", groups_x).reshape(query_count, key_count)
    query_lines = query_count * index_heads
    piece_rows = -(-(query_lines + index_heads) // (NYC * 8)) * 8
    both = call(
        lambda *refs: grad_kernel(half, index_scale, *refs),
        shape((piece_rows * NYC, 128), f32),
        flops=2 * index_flops,
        moved=2 << 20,
    )(dlogit, mine, index_keys)

    piece = exchanged(both.reshape(NYC, piece_rows, 128), "tokens", groups_yc)
    eight = jnp.concatenate([four, near])
    far = lax.ppermute(eight, "heads", pairs_x(2))
    piece = call(sum_kernel, shape((NZ // 2, piece_rows, 128), f32))(piece)
    piece = exchanged(piece, "tokens", groups_z4).sum(axis=0)
    other = lax.ppermute(piece, "tokens", pairs_z4)
    piece = call(pair_kernel, shape((NYC, piece_rows, 128), f32))(piece, other)
    both = exchanged(piece, "tokens", groups_yc).reshape(-1, 128)
    query_grad = both[:query_lines].reshape(query_count, index_heads, index_width)
    weight_grad = both[query_lines : query_lines + index_heads, :query_count].T

    key_flops = index_flops * NX * NZH
    key_grad = ()
    for message in (eight, far):
        key_grad = call(
            lambda *refs: key_kernel(half, index_scale, *refs),
            shape((key_count, index_width), f32),
            flops=key_flops,
            moved=2 << 20,
        )(dlogit, index_keys, message, *key_grad),
    return (query_grad, weight_grad, *key_grad)


def solution(mesh):
    placed = (
        P("heads", "tokens", None),
        P("tokens", None),
        P(None, "heads", None),
        P("tokens", None),
        P(None, "heads"),
        P(),
    )
    return jax.shard_map(
        local,
        mesh=mesh,
        in_specs=placed,
        out_specs=(P(None, "heads", None), P(None, "heads"), P("tokens", None)),
        check_vma=False,
    )
```

```python
import jax
import jax.numpy as jnp
from jax import lax
from jax.experimental import pallas as pl
from jax.experimental.pallas import tpu as pltpu
from jax.sharding import PartitionSpec as P

H = 128
NX, NZH = 4, 2
NY, NZ, NC = 4, 8, 2
NYC = NY * NC
GRAD_SCALE = 8192.0
VMEM = 12 << 20
WEIGHT = 48

softmax_scale = 192.0 ** (-0.5)
masked_value = -1e30
f32, bf16 = jnp.float32, jnp.bfloat16


def token_at(y, z, c):
    return (y * NZ + z) * NC + c


def head_at(x, z):
    return x * NZH + z


all_y, all_z, all_c = range(NY), range(NZ), range(NC)
groups_z = [[token_at(y, z, c) for z in all_z] for y in all_y for c in all_c]
groups_z4 = [
    [token_at(y, half + z, c) for z in range(4)] for half in (0, 4) for y in all_y for c in all_c
]
pairs_c = [(token_at(y, z, c), token_at(y, z, 1 - c)) for y in all_y for z in all_z for c in all_c]
groups_yc = [[token_at(y, z, c) for c in all_c for y in all_y] for z in all_z]
pairs_z4 = [(token_at(y, z, c), token_at(y, z ^ 4, c)) for y in all_y for z in all_z for c in all_c]
groups_x = [[head_at(x, z) for x in range(NX)] for z in range(NZH)]
pairs_zh = [(head_at(x, z), head_at(x, 1 - z)) for x in range(NX) for z in range(NZH)]


def pairs_x(flip):
    return [(head_at(x, z), head_at(x ^ flip, z)) for x in range(NX) for z in range(NZH)]


def exchanged(parts, axis, groups):
    return lax.all_to_all(parts, axis, 0, 0, tiled=True, axis_index_groups=groups)


def gathered(value, axis, groups):
    copies = jnp.broadcast_to(value[None], (len(groups[0]), *value.shape))
    return exchanged(copies, axis, groups)


def diagonal(rows, lanes):
    return lax.broadcasted_iota(jnp.int32, (rows, lanes), 0) == lax.broadcasted_iota(
        jnp.int32, (rows, lanes), 1
    )


def as_row(column, lanes=128):
    return jnp.sum(jnp.where(diagonal(column.shape[0], lanes), column, 0.0), axis=0, keepdims=True)


def as_column(row, rows):
    return jnp.sum(jnp.where(diagonal(rows, row.shape[1]), row, 0.0), axis=1, keepdims=True)


def call(kernel, out_shape, flops=0, moved=0):
    return pl.pallas_call(
        kernel,
        out_shape=out_shape,
        compiler_params=pltpu.CompilerParams(vmem_limit_bytes=VMEM),
        cost_estimate=pl.CostEstimate(flops=flops, bytes_accessed=moved, transcendentals=0),
    )


def score_kernel(limit_ref, q_ref, k_ref, e_ref, m_ref, l_ref):
    block = e_ref.shape[0] // NYC
    key = lax.broadcasted_iota(jnp.int32, (1, e_ref.shape[1]), 1)
    k = k_ref[...]
    for b in range(NYC):
        lines = slice(b * block, (b + 1) * block)
        s = jnp.dot(q_ref[lines], k, preferred_element_type=f32) * softmax_scale
        s = jnp.where(key <= limit_ref[lines], s, masked_value)
        m = jnp.max(s, axis=1, keepdims=True)
        e = jnp.exp(s - m)
        e_ref[lines] = e
        m_ref[b : b + 1] = as_row(m)
        l_ref[b : b + 1] = as_row(jnp.sum(e, axis=1, keepdims=True))


def message_parts(one_ref, two_ref, tokens, heads):
    rows = tokens * heads

    def weights(ref):
        block = ref[rows:, :].astype(f32)
        return block[:, :heads] + block[:, heads : 2 * heads] + block[:, 2 * heads : 3 * heads]

    iq = jnp.concatenate([one_ref[:rows, :], two_ref[:rows, :]])
    return iq, [w[:, j : j + 1] for w in (weights(one_ref), weights(two_ref)) for j in range(heads)]


def index_dot(iq, ik):
    return lax.dot_general(iq, ik, (((1,), (1,)), ((), ())), preferred_element_type=f32)


def logits_kernel(heads, scale, mine_ref, one_ref, two_ref, ik_ref, out_ref):
    tokens = out_ref.shape[0]
    ik = ik_ref[...]
    logits = jnp.zeros(out_ref.shape, f32)
    for pair in ((mine_ref.at[0], mine_ref.at[1]), (one_ref.at[0], two_ref.at[0])):
        iq, weights = message_parts(*pair, tokens, heads)
        active = index_dot(iq, ik)
        for j, w in enumerate(weights):
            here = active[j * tokens : (j + 1) * tokens] * scale
            logits = logits + w * jnp.maximum(here, 0.0)
    out_ref[...] = logits


def index_stats_kernel(limit_ref, *refs):
    pieces, (logits_ref, stat_ref) = refs[:-2], refs[-2:]
    logits = sum(piece[...] for piece in pieces)
    key = lax.broadcasted_iota(jnp.int32, (1, logits.shape[1]), 1)
    logits = jnp.where(key <= limit_ref[...], logits, masked_value)
    m = jnp.max(logits, axis=1, keepdims=True)
    l = jnp.sum(jnp.exp(logits - m), axis=1, keepdims=True)
    logits_ref[...] = logits
    stat_ref[...] = jnp.concatenate([as_row(m), as_row(l), jnp.zeros((6, 128), f32)], axis=0)


def joined(stats):
    def one(m, l):
        top = jnp.max(m, axis=0)
        return top, jnp.sum(l * jnp.exp(m - top), axis=0)

    return (*one(stats[:, 0:8], stats[:, 8:16]), *one(stats[:, 16:17], stats[:, 17:18]))


def join_kernel(stats_ref, out_ref):
    lines = jnp.concatenate([*joined(stats_ref[...]), jnp.zeros((6, 128), f32)], axis=0)
    out_ref[...] = jnp.broadcast_to(lines[None], out_ref.shape)


def target_kernel(stats_ref, m_ref, e_ref, out_ref):
    top, total, _, _ = joined(stats_ref[...])
    weights = jnp.exp(m_ref[...] - top) / total
    keys = out_ref.shape[1]
    block = e_ref.shape[0] // NYC
    for b in range(NYC):
        e = e_ref[b * block : (b + 1) * block] * as_column(weights[b : b + 1], block)
        out_ref[b * NZ : (b + 1) * NZ] = jnp.sum(e.reshape(NZ, block // NZ, keys), axis=1)


def dlogit_kernel(one_ref, two_ref, logits_ref, stats_ref, out_ref):
    rows = logits_ref.shape[0]
    _, _, top, total = joined(stats_ref[...])
    probs = jnp.exp(logits_ref[...] - as_column(top, rows)) / as_column(total, rows)
    dlogit = GRAD_SCALE * (probs - (one_ref[...] + two_ref[...]) / H)
    out_ref[...] = jnp.broadcast_to(dlogit[None], out_ref.shape)


def grad_kernel(heads, scale, d_ref, message_ref, ik_ref, out_ref):
    dlogit = d_ref[...]
    tokens = dlogit.shape[0]
    iq, weights = message_parts(message_ref.at[0], message_ref.at[1], tokens, heads)
    ik = ik_ref[...]
    active = index_dot(iq, ik)
    heads = len(weights)
    row = lax.broadcasted_iota(jnp.int32, (tokens, 128), 0)
    place = row // NZ % NY * (NC * NZ) + row % NZ * NC + row // (NY * NZ)
    places = place == lax.broadcasted_iota(jnp.int32, (tokens, 128), 1)
    out_ref[tokens * heads :, :] = jnp.zeros((out_ref.shape[0] - tokens * heads, 128), f32)
    for j, w in enumerate(weights):
        here = active[j * tokens : (j + 1) * tokens]
        gate = jnp.where(here > 0.0, dlogit * w, 0.0).astype(bf16)
        grad = jnp.dot(gate, ik, preferred_element_type=f32) * scale
        for b in range(NYC):
            first = b % NY * (NZ * NC) + b // NY
            lines = pl.ds(first * heads + j, NZ, stride=NC * heads)
            out_ref[lines, :] = grad[b * NZ : (b + 1) * NZ]
        weight_grad = jnp.sum(dlogit * jnp.maximum(here * scale, 0.0), axis=1, keepdims=True)
        out_ref[tokens * heads + j : tokens * heads + j + 1, :] = jnp.sum(
            jnp.where(places, weight_grad, 0.0), axis=0, keepdims=True
        )


def key_kernel(heads, scale, d_ref, ik_ref, message, *refs):
    before, out_ref = refs[:-1], refs[-1]
    dlogit, ik = d_ref[...], ik_ref[...]
    tokens, keys = dlogit.shape
    total = jnp.zeros((ik.shape[1], keys), f32)
    for part in range(0, message.shape[0], 2):
        iq, weights = message_parts(message.at[part], message.at[part + 1], tokens, heads)
        active = index_dot(iq, ik)
        gates = []
        for j, w in enumerate(weights):
            here = active[j * tokens : (j + 1) * tokens]
            gates.append(jnp.where(here > 0.0, dlogit * w, 0.0).astype(bf16))
        gate = jnp.concatenate(gates, axis=0)
        total = total + jnp.dot(iq.T, gate, preferred_element_type=f32)
    grad = total.T * scale
    out_ref[...] = before[0][...] + grad if before else grad


def sum_kernel(parts_ref, out_ref):
    out_ref[...] = jnp.broadcast_to(jnp.sum(parts_ref[...], axis=0)[None], out_ref.shape)


def pair_kernel(one_ref, two_ref, out_ref):
    out_ref[...] = jnp.broadcast_to((one_ref[...] + two_ref[...])[None], out_ref.shape)


def cut_kernel(both_ref, query_ref, weight_ref):
    lines, (rows, lanes) = query_ref.shape[0], weight_ref.shape
    query_ref[...] = both_ref[:lines]
    weight_ref[...] = both_ref[lines : lines + rows, :lanes]


def in_order(value):
    return jnp.moveaxis(value.reshape(NY, NZ, NC, *value.shape[1:]), 2, 0).reshape(value.shape)


def x_scatter(parts, x):
    pieces = [lax.dynamic_index_in_dim(parts, x ^ flip, 0, keepdims=False) for flip in range(NX)]
    return pieces[:1] + [
        lax.ppermute(pieces[flip], "heads", pairs_x(flip)) for flip in range(1, NX)
    ]


def local(queries, latent_keys, index_queries, index_keys, index_weights, positions):
    heads_here, width = queries.shape[0], queries.shape[2]
    key_count = latent_keys.shape[0]
    query_count, index_heads, index_width = index_queries.shape
    index_scale = index_width ** (-0.5)
    share_rows = query_count // NX
    shape = jax.ShapeDtypeStruct
    x = lax.axis_index("heads") // NZH
    core = lax.axis_index("tokens") % NC
    limit = in_order(positions - lax.axis_index("tokens") * key_count)

    along_z = gathered(queries.reshape(heads_here, width), "tokens", groups_z)

    high = lax.reduce_precision(index_weights, 8, 7)
    middle = lax.reduce_precision(index_weights - high, 8, 7)
    low = index_weights - high - middle
    half = index_heads // NC
    lines = jnp.stack([high, middle, low], axis=1).reshape(query_count, 3, NC, half)
    lines = in_order(lines.transpose(0, 2, 1, 3).reshape(query_count, NC, 3 * half))
    lines = jnp.pad(lines.transpose(1, 0, 2), ((0, 0), (0, 0), (0, 128 - 3 * half)))
    by_head = in_order(index_queries).transpose(1, 0, 2)
    by_head = by_head.reshape(NC, half * query_count, index_width)
    mine = jnp.concatenate([by_head, lines.astype(bf16)], axis=1)

    first = lax.ppermute(lax.dynamic_index_in_dim(mine, core, 0), "heads", pairs_zh)
    second = lax.ppermute(first, "tokens", pairs_c)

    index_flops = 2 * query_count * index_heads * key_count * index_width
    partial = call(
        lambda *refs: logits_kernel(half, index_scale, *refs),
        shape((query_count, key_count), f32),
        flops=WEIGHT * index_flops,
        moved=1 << 20,
    )(mine, first, second, index_keys)
    pieces = x_scatter(partial.reshape(NX, share_rows, key_count), x)
    rows = gathered(along_z, "tokens", groups_yc).reshape(-1, width)
    row_count = rows.shape[0]
    lines_shape = shape((NYC, row_count // NYC), f32)
    exponent, local_max, local_total = call(
        score_kernel,
        (shape((row_count, key_count), f32), lines_shape, lines_shape),
        flops=2 * row_count * key_count * width,
        moved=4 << 20,
    )(jnp.repeat(limit, heads_here)[:, None], rows, latent_keys.T)

    local_max, *pieces = lax.optimization_barrier((local_max, *pieces))
    share_limit = lax.dynamic_slice_in_dim(limit, x * share_rows, share_rows, 0)
    logits, index_stats = call(
        index_stats_kernel,
        (shape((share_rows, key_count), f32), shape((8, 128), f32)),
        flops=index_flops,
        moved=1 << 20,
    )(share_limit[:, None], *pieces)

    stats = jnp.concatenate([local_max, local_total, index_stats])

    stats = gathered(stats, "tokens", groups_z)
    stats = call(join_kernel, shape((NYC, *stats.shape[1:]), f32))(stats)
    stats = exchanged(stats, "tokens", groups_yc)

    partial = call(target_kernel, shape((query_count, key_count), f32), moved=5 << 20)(
        stats, local_max, exponent
    )

    over_x = exchanged(partial.reshape(NX, share_rows, key_count), "heads", groups_x).sum(axis=0)
    other = lax.ppermute(over_x, "heads", pairs_zh)
    dlogit = call(dlogit_kernel, shape((NX, share_rows, key_count), f32))(
        over_x, other, logits, stats
    )
    dlogit, *three = lax.optimization_barrier((dlogit, mine, first, second))
    four = jnp.concatenate(three)
    near = lax.ppermute(four, "heads", pairs_x(1))
    dlogit = exchanged(dlogit, "heads", groups_x).reshape(query_count, key_count)
    query_lines = query_count * index_heads
    piece_rows = -(-(query_lines + index_heads) // (NYC * 8)) * 8
    both = call(
        lambda *refs: grad_kernel(half, index_scale, *refs),
        shape((piece_rows * NYC, 128), f32),
        flops=2 * index_flops,
        moved=2 << 20,
    )(dlogit, mine, index_keys)

    piece = exchanged(both.reshape(NYC, piece_rows, 128), "tokens", groups_yc)
    eight = jnp.concatenate([four, near])
    far = lax.ppermute(eight, "heads", pairs_x(2))
    piece = call(sum_kernel, shape((NZ // 2, piece_rows, 128), f32))(piece)
    piece = exchanged(piece, "tokens", groups_z4).sum(axis=0)
    other = lax.ppermute(piece, "tokens", pairs_z4)
    piece = call(pair_kernel, shape((NYC, piece_rows, 128), f32))(piece, other)
    both = exchanged(piece, "tokens", groups_yc).reshape(-1, 128)
    query_grad, weight_grad = call(
        cut_kernel, (shape((query_lines, 128), f32), shape((index_heads, query_count), f32))
    )(both)
    query_grad = query_grad.reshape(query_count, index_heads, index_width)
    weight_grad = weight_grad.T

    key_flops = index_flops * NX * NZH
    key_grad = ()
    for message in (eight, far):
        key_grad = call(
            lambda *refs: key_kernel(half, index_scale, *refs),
            shape((key_count, index_width), f32),
            flops=key_flops,
            moved=2 << 20,
        )(dlogit, index_keys, message, *key_grad),
    return (query_grad, weight_grad, *key_grad)


def solution(mesh):
    placed = (
        P("heads", "tokens", None),
        P("tokens", None),
        P(None, "heads", None),
        P("tokens", None),
        P(None, "heads"),
        P(),
    )
    return jax.shard_map(
        local,
        mesh=mesh,
        in_specs=placed,
        out_specs=(P(None, "heads", None), P(None, "heads"), P("tokens", None)),
        check_vma=False,
    )
```

```python
import jax
import jax.numpy as jnp
from jax import lax
from jax.experimental import pallas as pl
from jax.experimental.pallas import tpu as pltpu
from jax.sharding import PartitionSpec as P

H = 128
NX, NZH = 4, 2
NY, NZ, NC = 4, 8, 2
NYC = NY * NC
GRAD_SCALE = 8192.0
VMEM = 12 << 20
WEIGHT = 48

softmax_scale = 192.0 ** (-0.5)
masked_value = -1e30
f32, bf16 = jnp.float32, jnp.bfloat16


def token_at(y, z, c):
    return (y * NZ + z) * NC + c


def head_at(x, z):
    return x * NZH + z


all_y, all_z, all_c = range(NY), range(NZ), range(NC)
groups_z = [[token_at(y, z, c) for z in all_z] for y in all_y for c in all_c]
pairs_c = [(token_at(y, z, c), token_at(y, z, 1 - c)) for y in all_y for z in all_z for c in all_c]
groups_yc = [[token_at(y, z, c) for c in all_c for y in all_y] for z in all_z]
groups_x = [[head_at(x, z) for x in range(NX)] for z in range(NZH)]
pairs_zh = [(head_at(x, z), head_at(x, 1 - z)) for x in range(NX) for z in range(NZH)]


def pairs_x(flip):
    return [(head_at(x, z), head_at(x ^ flip, z)) for x in range(NX) for z in range(NZH)]


def exchanged(parts, axis, groups):
    return lax.all_to_all(parts, axis, 0, 0, tiled=True, axis_index_groups=groups)


def gathered(value, axis, groups):
    copies = jnp.broadcast_to(value[None], (len(groups[0]), *value.shape))
    return exchanged(copies, axis, groups)


def diagonal(rows, lanes):
    return lax.broadcasted_iota(jnp.int32, (rows, lanes), 0) == lax.broadcasted_iota(
        jnp.int32, (rows, lanes), 1
    )


def as_row(column, lanes=128):
    return jnp.sum(jnp.where(diagonal(column.shape[0], lanes), column, 0.0), axis=0, keepdims=True)


def as_column(row, rows):
    return jnp.sum(jnp.where(diagonal(rows, row.shape[1]), row, 0.0), axis=1, keepdims=True)


def call(kernel, out_shape, flops=0, moved=0):
    return pl.pallas_call(
        kernel,
        out_shape=out_shape,
        compiler_params=pltpu.CompilerParams(vmem_limit_bytes=VMEM),
        cost_estimate=pl.CostEstimate(flops=flops, bytes_accessed=moved, transcendentals=0),
    )


def score_kernel(limit_ref, q_ref, k_ref, e_ref, m_ref, l_ref):
    block = e_ref.shape[0] // NYC
    key = lax.broadcasted_iota(jnp.int32, (1, e_ref.shape[1]), 1)
    k = k_ref[...]
    for b in range(NYC):
        lines = slice(b * block, (b + 1) * block)
        s = jnp.dot(q_ref[lines], k, preferred_element_type=f32) * softmax_scale
        s = jnp.where(key <= limit_ref[lines], s, masked_value)
        m = jnp.max(s, axis=1, keepdims=True)
        e = jnp.exp(s - m)
        e_ref[lines] = e
        m_ref[b : b + 1] = as_row(m)
        l_ref[b : b + 1] = as_row(jnp.sum(e, axis=1, keepdims=True))


def message_parts(one_ref, two_ref, tokens, heads):
    rows = tokens * heads

    def weights(ref):
        block = ref[rows:, :].astype(f32)
        return block[:, :heads] + block[:, heads : 2 * heads] + block[:, 2 * heads : 3 * heads]

    iq = jnp.concatenate([one_ref[:rows, :], two_ref[:rows, :]])
    return iq, [w[:, j : j + 1] for w in (weights(one_ref), weights(two_ref)) for j in range(heads)]


def index_dot(iq, ik):
    return lax.dot_general(iq, ik, (((1,), (1,)), ((), ())), preferred_element_type=f32)


def logits_kernel(heads, scale, mine_ref, one_ref, two_ref, ik_ref, out_ref):
    tokens = out_ref.shape[0]
    ik = ik_ref[...]
    logits = jnp.zeros(out_ref.shape, f32)
    for pair in ((mine_ref.at[0], mine_ref.at[1]), (one_ref.at[0], two_ref.at[0])):
        iq, weights = message_parts(*pair, tokens, heads)
        active = index_dot(iq, ik)
        for j, w in enumerate(weights):
            here = active[j * tokens : (j + 1) * tokens] * scale
            logits = logits + w * jnp.maximum(here, 0.0)
    out_ref[...] = logits


def index_stats_kernel(limit_ref, *refs):
    pieces, (logits_ref, stat_ref) = refs[:-2], refs[-2:]
    logits = sum(piece[...] for piece in pieces)
    key = lax.broadcasted_iota(jnp.int32, (1, logits.shape[1]), 1)
    logits = jnp.where(key <= limit_ref[...], logits, masked_value)
    m = jnp.max(logits, axis=1, keepdims=True)
    l = jnp.sum(jnp.exp(logits - m), axis=1, keepdims=True)
    logits_ref[...] = logits
    stat_ref[...] = jnp.concatenate([as_row(m), as_row(l), jnp.zeros((6, 128), f32)], axis=0)


def joined(stats):
    def one(m, l):
        top = jnp.max(m, axis=0)
        return top, jnp.sum(l * jnp.exp(m - top), axis=0)

    return (*one(stats[:, 0:8], stats[:, 8:16]), *one(stats[:, 16:17], stats[:, 17:18]))


def join_kernel(stats_ref, out_ref):
    lines = jnp.concatenate([*joined(stats_ref[...]), jnp.zeros((6, 128), f32)], axis=0)
    out_ref[...] = jnp.broadcast_to(lines[None], out_ref.shape)


def target_kernel(stats_ref, m_ref, e_ref, out_ref):
    top, total, _, _ = joined(stats_ref[...])
    weights = jnp.exp(m_ref[...] - top) / total
    keys = out_ref.shape[1]
    block = e_ref.shape[0] // NYC
    for b in range(NYC):
        e = e_ref[b * block : (b + 1) * block] * as_column(weights[b : b + 1], block)
        out_ref[b * NZ : (b + 1) * NZ] = jnp.sum(e.reshape(NZ, block // NZ, keys), axis=1)


def dlogit_kernel(one_ref, two_ref, logits_ref, stats_ref, out_ref):
    rows = logits_ref.shape[0]
    _, _, top, total = joined(stats_ref[...])
    probs = jnp.exp(logits_ref[...] - as_column(top, rows)) / as_column(total, rows)
    dlogit = GRAD_SCALE * (probs - (one_ref[...] + two_ref[...]) / H)
    out_ref[...] = jnp.broadcast_to(dlogit[None], out_ref.shape)


def grad_kernel(heads, scale, d_ref, message_ref, ik_ref, out_ref):
    dlogit = d_ref[...]
    tokens = dlogit.shape[0]
    iq, weights = message_parts(message_ref.at[0], message_ref.at[1], tokens, heads)
    ik = ik_ref[...]
    active = index_dot(iq, ik)
    heads = len(weights)
    row = lax.broadcasted_iota(jnp.int32, (tokens, 128), 0)
    place = row // NZ % NY * (NC * NZ) + row % NZ * NC + row // (NY * NZ)
    places = place == lax.broadcasted_iota(jnp.int32, (tokens, 128), 1)
    out_ref[tokens * heads :, :] = jnp.zeros((out_ref.shape[0] - tokens * heads, 128), f32)
    for j, w in enumerate(weights):
        here = active[j * tokens : (j + 1) * tokens]
        gate = jnp.where(here > 0.0, dlogit * w, 0.0).astype(bf16)
        grad = jnp.dot(gate, ik, preferred_element_type=f32) * scale
        for b in range(NYC):
            first = b % NY * (NZ * NC) + b // NY
            lines = pl.ds(first * heads + j, NZ, stride=NC * heads)
            out_ref[lines, :] = grad[b * NZ : (b + 1) * NZ]
        weight_grad = jnp.sum(dlogit * jnp.maximum(here * scale, 0.0), axis=1, keepdims=True)
        out_ref[tokens * heads + j : tokens * heads + j + 1, :] = jnp.sum(
            jnp.where(places, weight_grad, 0.0), axis=0, keepdims=True
        )


def key_kernel(heads, scale, d_ref, ik_ref, message, *refs):
    before, out_ref = refs[:-1], refs[-1]
    dlogit, ik = d_ref[...], ik_ref[...]
    tokens, keys = dlogit.shape
    total = jnp.zeros((ik.shape[1], keys), f32)
    for part in range(0, message.shape[0], 2):
        iq, weights = message_parts(message.at[part], message.at[part + 1], tokens, heads)
        active = index_dot(iq, ik)
        gates = []
        for j, w in enumerate(weights):
            here = active[j * tokens : (j + 1) * tokens]
            gates.append(jnp.where(here > 0.0, dlogit * w, 0.0).astype(bf16))
        gate = jnp.concatenate(gates, axis=0)
        total = total + jnp.dot(iq.T, gate, preferred_element_type=f32)
    grad = total.T * scale
    out_ref[...] = before[0][...] + grad if before else grad


def sum_kernel(parts_ref, out_ref):
    out_ref[...] = jnp.broadcast_to(jnp.sum(parts_ref[...], axis=0)[None], out_ref.shape)


def cut_kernel(both_ref, query_ref, weight_ref):
    lines, (rows, lanes) = query_ref.shape[0], weight_ref.shape
    query_ref[...] = both_ref[:lines]
    weight_ref[...] = both_ref[lines : lines + rows, :lanes]


def in_order(value):
    return jnp.moveaxis(value.reshape(NY, NZ, NC, *value.shape[1:]), 2, 0).reshape(value.shape)


def x_scatter(parts, x):
    pieces = [lax.dynamic_index_in_dim(parts, x ^ flip, 0, keepdims=False) for flip in range(NX)]
    return pieces[:1] + [
        lax.ppermute(pieces[flip], "heads", pairs_x(flip)) for flip in range(1, NX)
    ]


def local(queries, latent_keys, index_queries, index_keys, index_weights, positions):
    heads_here, width = queries.shape[0], queries.shape[2]
    key_count = latent_keys.shape[0]
    query_count, index_heads, index_width = index_queries.shape
    index_scale = index_width ** (-0.5)
    share_rows = query_count // NX
    shape = jax.ShapeDtypeStruct
    x = lax.axis_index("heads") // NZH
    core = lax.axis_index("tokens") % NC
    limit = in_order(positions - lax.axis_index("tokens") * key_count)

    along_z = gathered(queries.reshape(heads_here, width), "tokens", groups_z)

    high = lax.reduce_precision(index_weights, 8, 7)
    middle = lax.reduce_precision(index_weights - high, 8, 7)
    low = index_weights - high - middle
    half = index_heads // NC
    lines = jnp.stack([high, middle, low], axis=1).reshape(query_count, 3, NC, half)
    lines = in_order(lines.transpose(0, 2, 1, 3).reshape(query_count, NC, 3 * half))
    lines = jnp.pad(lines.transpose(1, 0, 2), ((0, 0), (0, 0), (0, 128 - 3 * half)))
    by_head = in_order(index_queries).transpose(1, 0, 2)
    by_head = by_head.reshape(NC, half * query_count, index_width)
    mine = jnp.concatenate([by_head, lines.astype(bf16)], axis=1)

    first = lax.ppermute(lax.dynamic_index_in_dim(mine, core, 0), "heads", pairs_zh)
    second = lax.ppermute(first, "tokens", pairs_c)

    index_flops = 2 * query_count * index_heads * key_count * index_width
    partial = call(
        lambda *refs: logits_kernel(half, index_scale, *refs),
        shape((query_count, key_count), f32),
        flops=WEIGHT * index_flops,
        moved=1 << 20,
    )(mine, first, second, index_keys)
    pieces = x_scatter(partial.reshape(NX, share_rows, key_count), x)
    rows = gathered(along_z, "tokens", groups_yc).reshape(-1, width)
    row_count = rows.shape[0]
    lines_shape = shape((NYC, row_count // NYC), f32)
    exponent, local_max, local_total = call(
        score_kernel,
        (shape((row_count, key_count), f32), lines_shape, lines_shape),
        flops=2 * row_count * key_count * width,
        moved=4 << 20,
    )(jnp.repeat(limit, heads_here)[:, None], rows, latent_keys.T)

    local_max, *pieces = lax.optimization_barrier((local_max, *pieces))
    share_limit = lax.dynamic_slice_in_dim(limit, x * share_rows, share_rows, 0)
    logits, index_stats = call(
        index_stats_kernel,
        (shape((share_rows, key_count), f32), shape((8, 128), f32)),
        flops=index_flops,
        moved=1 << 20,
    )(share_limit[:, None], *pieces)

    stats = jnp.concatenate([local_max, local_total, index_stats])

    stats = gathered(stats, "tokens", groups_z)
    stats = call(join_kernel, shape((NYC, *stats.shape[1:]), f32))(stats)
    stats = exchanged(stats, "tokens", groups_yc)

    partial = call(target_kernel, shape((query_count, key_count), f32), moved=5 << 20)(
        stats, local_max, exponent
    )

    over_x = exchanged(partial.reshape(NX, share_rows, key_count), "heads", groups_x).sum(axis=0)
    other = lax.ppermute(over_x, "heads", pairs_zh)
    dlogit = call(dlogit_kernel, shape((NX, share_rows, key_count), f32))(
        over_x, other, logits, stats
    )
    dlogit, *three = lax.optimization_barrier((dlogit, mine, first, second))
    four = jnp.concatenate(three)
    near = lax.ppermute(four, "heads", pairs_x(1))
    dlogit = exchanged(dlogit, "heads", groups_x).reshape(query_count, key_count)
    query_lines = query_count * index_heads
    piece_rows = -(-(query_lines + index_heads) // (NYC * 8)) * 8
    both = call(
        lambda *refs: grad_kernel(half, index_scale, *refs),
        shape((piece_rows * NYC, 128), f32),
        flops=2 * index_flops,
        moved=2 << 20,
    )(dlogit, mine, index_keys)

    piece = exchanged(both.reshape(NYC, piece_rows, 128), "tokens", groups_yc)
    eight = jnp.concatenate([four, near])
    far = lax.ppermute(eight, "heads", pairs_x(2))
    piece = call(sum_kernel, shape((NZ, piece_rows, 128), f32))(piece)
    piece = exchanged(piece, "tokens", groups_z)
    piece = call(sum_kernel, shape((NYC, piece_rows, 128), f32))(piece)
    both = exchanged(piece, "tokens", groups_yc).reshape(-1, 128)
    query_grad, weight_grad = call(
        cut_kernel, (shape((query_lines, 128), f32), shape((index_heads, query_count), f32))
    )(both)
    query_grad = query_grad.reshape(query_count, index_heads, index_width)
    weight_grad = weight_grad.T

    key_flops = index_flops * NX * NZH
    key_grad = ()
    for message in (eight, far):
        key_grad = call(
            lambda *refs: key_kernel(half, index_scale, *refs),
            shape((key_count, index_width), f32),
            flops=key_flops,
            moved=2 << 20,
        )(dlogit, index_keys, message, *key_grad),
    return (query_grad, weight_grad, *key_grad)


def solution(mesh):
    placed = (
        P("heads", "tokens", None),
        P("tokens", None),
        P(None, "heads", None),
        P("tokens", None),
        P(None, "heads"),
        P(),
    )
    return jax.shard_map(
        local,
        mesh=mesh,
        in_specs=placed,
        out_specs=(P(None, "heads", None), P(None, "heads"), P("tokens", None)),
        check_vma=False,
    )
```

```python
import jax
import jax.numpy as jnp
from jax import lax
from jax.experimental import pallas as pl
from jax.experimental.pallas import tpu as pltpu
from jax.sharding import PartitionSpec as P

H = 128
NX, NZH = 4, 2
NY, NZ, NC = 4, 8, 2
NYC = NY * NC
GRAD_SCALE = 8192.0
VMEM = 12 << 20
WEIGHT = 48

softmax_scale = 192.0 ** (-0.5)
masked_value = -1e30
f32, bf16 = jnp.float32, jnp.bfloat16


def token_at(y, z, c):
    return (y * NZ + z) * NC + c


def head_at(x, z):
    return x * NZH + z


all_y, all_z, all_c = range(NY), range(NZ), range(NC)
groups_z = [[token_at(y, z, c) for z in all_z] for y in all_y for c in all_c]
groups_z4 = [
    [token_at(y, half + z, c) for z in range(4)] for half in (0, 4) for y in all_y for c in all_c
]
pairs_c = [(token_at(y, z, c), token_at(y, z, 1 - c)) for y in all_y for z in all_z for c in all_c]
groups_yc = [[token_at(y, z, c) for c in all_c for y in all_y] for z in all_z]
pairs_z4 = [(token_at(y, z, c), token_at(y, z ^ 4, c)) for y in all_y for z in all_z for c in all_c]
groups_x = [[head_at(x, z) for x in range(NX)] for z in range(NZH)]
pairs_zh = [(head_at(x, z), head_at(x, 1 - z)) for x in range(NX) for z in range(NZH)]


def pairs_x(flip):
    return [(head_at(x, z), head_at(x ^ flip, z)) for x in range(NX) for z in range(NZH)]


def exchanged(parts, axis, groups):
    return lax.all_to_all(parts, axis, 0, 0, tiled=True, axis_index_groups=groups)


def gathered(value, axis, groups):
    copies = jnp.broadcast_to(value[None], (len(groups[0]), *value.shape))
    return exchanged(copies, axis, groups)


def diagonal(rows, lanes):
    return lax.broadcasted_iota(jnp.int32, (rows, lanes), 0) == lax.broadcasted_iota(
        jnp.int32, (rows, lanes), 1
    )


def as_row(column, lanes=128):
    return jnp.sum(jnp.where(diagonal(column.shape[0], lanes), column, 0.0), axis=0, keepdims=True)


def as_column(row, rows):
    return jnp.sum(jnp.where(diagonal(rows, row.shape[1]), row, 0.0), axis=1, keepdims=True)


def call(kernel, out_shape, flops=0, moved=0):
    return pl.pallas_call(
        kernel,
        out_shape=out_shape,
        compiler_params=pltpu.CompilerParams(vmem_limit_bytes=VMEM),
        cost_estimate=pl.CostEstimate(flops=flops, bytes_accessed=moved, transcendentals=0),
    )


def score_kernel(limit_ref, q_ref, k_ref, e_ref, m_ref, l_ref):
    block = e_ref.shape[0] // NYC
    key = lax.broadcasted_iota(jnp.int32, (1, e_ref.shape[1]), 1)
    k = k_ref[...]
    for b in range(NYC):
        lines = slice(b * block, (b + 1) * block)
        s = jnp.dot(q_ref[lines], k, preferred_element_type=f32) * softmax_scale
        s = jnp.where(key <= limit_ref[lines], s, masked_value)
        m = jnp.max(s, axis=1, keepdims=True)
        e = jnp.exp(s - m)
        e_ref[lines] = e
        m_ref[b : b + 1] = as_row(m)
        l_ref[b : b + 1] = as_row(jnp.sum(e, axis=1, keepdims=True))


def message_parts(one_ref, two_ref, tokens, heads):
    rows = tokens * heads

    def weights(ref):
        block = ref[rows:, :].astype(f32)
        return block[:, :heads] + block[:, heads : 2 * heads] + block[:, 2 * heads : 3 * heads]

    iq = jnp.concatenate([one_ref[:rows, :], two_ref[:rows, :]])
    return iq, [w[:, j : j + 1] for w in (weights(one_ref), weights(two_ref)) for j in range(heads)]


def index_dot(iq, ik):
    return lax.dot_general(iq, ik, (((1,), (1,)), ((), ())), preferred_element_type=f32)


def logits_kernel(heads, scale, mine_ref, one_ref, two_ref, ik_ref, out_ref):
    tokens = out_ref.shape[0]
    ik = ik_ref[...]
    logits = jnp.zeros(out_ref.shape, f32)
    for pair in ((mine_ref.at[0], mine_ref.at[1]), (one_ref.at[0], two_ref.at[0])):
        iq, weights = message_parts(*pair, tokens, heads)
        active = index_dot(iq, ik)
        for j, w in enumerate(weights):
            here = active[j * tokens : (j + 1) * tokens] * scale
            logits = logits + w * jnp.maximum(here, 0.0)
    out_ref[...] = logits


def index_stats_kernel(limit_ref, max_ref, total_ref, *refs):
    pieces, (logits_ref, stat_ref) = refs[:-2], refs[-2:]
    logits = sum(piece[...] for piece in pieces)
    key = lax.broadcasted_iota(jnp.int32, (1, logits.shape[1]), 1)
    logits = jnp.where(key <= limit_ref[...], logits, masked_value)
    m = jnp.max(logits, axis=1, keepdims=True)
    l = jnp.sum(jnp.exp(logits - m), axis=1, keepdims=True)
    logits_ref[...] = logits
    index_lines = [as_row(m), as_row(l), jnp.zeros((6, 128), f32)]
    lines = jnp.concatenate([max_ref[...], total_ref[...], *index_lines], axis=0)
    stat_ref[...] = jnp.broadcast_to(lines[None], stat_ref.shape)


def joined(stats):
    def one(m, l):
        top = jnp.max(m, axis=0)
        return top, jnp.sum(l * jnp.exp(m - top), axis=0)

    return (*one(stats[:, 0:8], stats[:, 8:16]), *one(stats[:, 16:17], stats[:, 17:18]))


def join_kernel(stats_ref, out_ref):
    lines = jnp.concatenate([*joined(stats_ref[...]), jnp.zeros((6, 128), f32)], axis=0)
    out_ref[...] = jnp.broadcast_to(lines[None], out_ref.shape)


def target_kernel(stats_ref, m_ref, e_ref, out_ref):
    top, total, _, _ = joined(stats_ref[...])
    weights = jnp.exp(m_ref[...] - top) / total
    keys = out_ref.shape[1]
    block = e_ref.shape[0] // NYC
    for b in range(NYC):
        e = e_ref[b * block : (b + 1) * block] * as_column(weights[b : b + 1], block)
        out_ref[b * NZ : (b + 1) * NZ] = jnp.sum(e.reshape(NZ, block // NZ, keys), axis=1)


def dlogit_kernel(one_ref, two_ref, logits_ref, stats_ref, out_ref):
    rows = logits_ref.shape[0]
    _, _, top, total = joined(stats_ref[...])
    probs = jnp.exp(logits_ref[...] - as_column(top, rows)) / as_column(total, rows)
    dlogit = GRAD_SCALE * (probs - (one_ref[...] + two_ref[...]) / H)
    out_ref[...] = jnp.broadcast_to(dlogit[None], out_ref.shape)


def grad_kernel(heads, scale, d_ref, message_ref, ik_ref, out_ref):
    dlogit = d_ref[...]
    tokens = dlogit.shape[0]
    iq, weights = message_parts(message_ref.at[0], message_ref.at[1], tokens, heads)
    ik = ik_ref[...]
    active = index_dot(iq, ik)
    heads = len(weights)
    row = lax.broadcasted_iota(jnp.int32, (tokens, 128), 0)
    place = row // NZ % NY * (NC * NZ) + row % NZ * NC + row // (NY * NZ)
    places = place == lax.broadcasted_iota(jnp.int32, (tokens, 128), 1)
    out_ref[tokens * heads :, :] = jnp.zeros((out_ref.shape[0] - tokens * heads, 128), f32)
    for j, w in enumerate(weights):
        here = active[j * tokens : (j + 1) * tokens]
        gate = jnp.where(here > 0.0, dlogit * w, 0.0).astype(bf16)
        grad = jnp.dot(gate, ik, preferred_element_type=f32) * scale
        for b in range(NYC):
            first = b % NY * (NZ * NC) + b // NY
            lines = pl.ds(first * heads + j, NZ, stride=NC * heads)
            out_ref[lines, :] = grad[b * NZ : (b + 1) * NZ]
        weight_grad = jnp.sum(dlogit * jnp.maximum(here * scale, 0.0), axis=1, keepdims=True)
        out_ref[tokens * heads + j : tokens * heads + j + 1, :] = jnp.sum(
            jnp.where(places, weight_grad, 0.0), axis=0, keepdims=True
        )


def key_kernel(heads, scale, d_ref, ik_ref, message, *refs):
    before, out_ref = refs[:-1], refs[-1]
    dlogit, ik = d_ref[...], ik_ref[...]
    tokens, keys = dlogit.shape
    total = jnp.zeros((ik.shape[1], keys), f32)
    for part in range(0, message.shape[0], 2):
        iq, weights = message_parts(message.at[part], message.at[part + 1], tokens, heads)
        active = index_dot(iq, ik)
        gates = []
        for j, w in enumerate(weights):
            here = active[j * tokens : (j + 1) * tokens]
            gates.append(jnp.where(here > 0.0, dlogit * w, 0.0).astype(bf16))
        gate = jnp.concatenate(gates, axis=0)
        total = total + jnp.dot(iq.T, gate, preferred_element_type=f32)
    grad = total.T * scale
    out_ref[...] = before[0][...] + grad if before else grad


def sum_kernel(parts_ref, out_ref):
    out_ref[...] = jnp.broadcast_to(jnp.sum(parts_ref[...], axis=0)[None], out_ref.shape)


def pair_kernel(one_ref, two_ref, out_ref):
    out_ref[...] = jnp.broadcast_to((one_ref[...] + two_ref[...])[None], out_ref.shape)


def cut_kernel(both_ref, query_ref, weight_ref):
    lines, (rows, lanes) = query_ref.shape[0], weight_ref.shape
    query_ref[...] = both_ref[:lines]
    weight_ref[...] = both_ref[lines : lines + rows, :lanes]


def in_order(value):
    return jnp.moveaxis(value.reshape(NY, NZ, NC, *value.shape[1:]), 2, 0).reshape(value.shape)


def x_scatter(parts, x):
    pieces = [lax.dynamic_index_in_dim(parts, x ^ flip, 0, keepdims=False) for flip in range(NX)]
    return pieces[:1] + [
        lax.ppermute(pieces[flip], "heads", pairs_x(flip)) for flip in range(1, NX)
    ]


def local(queries, latent_keys, index_queries, index_keys, index_weights, positions):
    heads_here, width = queries.shape[0], queries.shape[2]
    key_count = latent_keys.shape[0]
    query_count, index_heads, index_width = index_queries.shape
    index_scale = index_width ** (-0.5)
    share_rows = query_count // NX
    shape = jax.ShapeDtypeStruct
    x = lax.axis_index("heads") // NZH
    core = lax.axis_index("tokens") % NC
    limit = in_order(positions - lax.axis_index("tokens") * key_count)

    along_z = gathered(queries.reshape(heads_here, width), "tokens", groups_z)

    high = lax.reduce_precision(index_weights, 8, 7)
    middle = lax.reduce_precision(index_weights - high, 8, 7)
    low = index_weights - high - middle
    half = index_heads // NC
    lines = jnp.stack([high, middle, low], axis=1).reshape(query_count, 3, NC, half)
    lines = in_order(lines.transpose(0, 2, 1, 3).reshape(query_count, NC, 3 * half))
    lines = jnp.pad(lines.transpose(1, 0, 2), ((0, 0), (0, 0), (0, 128 - 3 * half)))
    by_head = in_order(index_queries).transpose(1, 0, 2)
    by_head = by_head.reshape(NC, half * query_count, index_width)
    mine = jnp.concatenate([by_head, lines.astype(bf16)], axis=1)

    first = lax.ppermute(lax.dynamic_index_in_dim(mine, core, 0), "heads", pairs_zh)
    second = lax.ppermute(first, "tokens", pairs_c)

    index_flops = 2 * query_count * index_heads * key_count * index_width
    partial = call(
        lambda *refs: logits_kernel(half, index_scale, *refs),
        shape((query_count, key_count), f32),
        flops=WEIGHT * index_flops,
        moved=1 << 20,
    )(mine, first, second, index_keys)
    pieces = x_scatter(partial.reshape(NX, share_rows, key_count), x)
    rows = gathered(along_z, "tokens", groups_yc).reshape(-1, width)
    row_count = rows.shape[0]
    lines_shape = shape((NYC, row_count // NYC), f32)
    exponent, local_max, local_total = call(
        score_kernel,
        (shape((row_count, key_count), f32), lines_shape, lines_shape),
        flops=2 * row_count * key_count * width,
        moved=4 << 20,
    )(jnp.repeat(limit, heads_here)[:, None], rows, latent_keys.T)

    local_max, *pieces = lax.optimization_barrier((local_max, *pieces))
    share_limit = lax.dynamic_slice_in_dim(limit, x * share_rows, share_rows, 0)
    logits, stats = call(
        index_stats_kernel,
        (shape((share_rows, key_count), f32), shape((NZ, 2 * NYC + 8, 128), f32)),
        flops=index_flops,
        moved=1 << 20,
    )(share_limit[:, None], local_max, local_total, *pieces)

    stats = exchanged(stats, "tokens", groups_z)
    stats = call(join_kernel, shape((NYC, *stats.shape[1:]), f32))(stats)
    stats = exchanged(stats, "tokens", groups_yc)

    partial = call(target_kernel, shape((query_count, key_count), f32), moved=5 << 20)(
        stats, local_max, exponent
    )

    over_x = exchanged(partial.reshape(NX, share_rows, key_count), "heads", groups_x).sum(axis=0)
    other = lax.ppermute(over_x, "heads", pairs_zh)
    dlogit = call(dlogit_kernel, shape((NX, share_rows, key_count), f32))(
        over_x, other, logits, stats
    )
    dlogit, *three = lax.optimization_barrier((dlogit, mine, first, second))
    four = jnp.concatenate(three)
    near = lax.ppermute(four, "heads", pairs_x(1))
    dlogit = exchanged(dlogit, "heads", groups_x).reshape(query_count, key_count)
    query_lines = query_count * index_heads
    piece_rows = -(-(query_lines + index_heads) // (NYC * 8)) * 8
    both = call(
        lambda *refs: grad_kernel(half, index_scale, *refs),
        shape((piece_rows * NYC, 128), f32),
        flops=2 * index_flops,
        moved=2 << 20,
    )(dlogit, mine, index_keys)

    piece = exchanged(both.reshape(NYC, piece_rows, 128), "tokens", groups_yc)
    eight = jnp.concatenate([four, near])
    far = lax.ppermute(eight, "heads", pairs_x(2))
    piece = call(sum_kernel, shape((NZ // 2, piece_rows, 128), f32))(piece)
    piece = exchanged(piece, "tokens", groups_z4).sum(axis=0)
    other = lax.ppermute(piece, "tokens", pairs_z4)
    piece = call(pair_kernel, shape((NYC, piece_rows, 128), f32))(piece, other)
    both = exchanged(piece, "tokens", groups_yc).reshape(-1, 128)
    query_grad, weight_grad = call(
        cut_kernel, (shape((query_lines, 128), f32), shape((index_heads, query_count), f32))
    )(both)
    query_grad = query_grad.reshape(query_count, index_heads, index_width)
    weight_grad = weight_grad.T

    key_flops = index_flops * NX * NZH
    key_grad = ()
    for message in (eight, far):
        key_grad = call(
            lambda *refs: key_kernel(half, index_scale, *refs),
            shape((key_count, index_width), f32),
            flops=key_flops,
            moved=2 << 20,
        )(dlogit, index_keys, message, *key_grad),
    return (query_grad, weight_grad, *key_grad)


def solution(mesh):
    placed = (
        P("heads", "tokens", None),
        P("tokens", None),
        P(None, "heads", None),
        P("tokens", None),
        P(None, "heads"),
        P(),
    )
    return jax.shard_map(
        local,
        mesh=mesh,
        in_specs=placed,
        out_specs=(P(None, "heads", None), P(None, "heads"), P("tokens", None)),
        check_vma=False,
    )
```

```python
import jax
import jax.numpy as jnp
from jax import lax
from jax.experimental import pallas as pl
from jax.experimental.pallas import tpu as pltpu
from jax.sharding import PartitionSpec as P

H = 128
NX, NZH = 4, 2
NY, NZ, NC = 4, 8, 2
NYC = NY * NC
GRAD_SCALE = 8192.0
VMEM = 12 << 20
WEIGHT = 48

softmax_scale = 192.0 ** (-0.5)
masked_value = -1e30
f32, bf16 = jnp.float32, jnp.bfloat16


def token_at(y, z, c):
    return (y * NZ + z) * NC + c


def head_at(x, z):
    return x * NZH + z


all_y, all_z, all_c = range(NY), range(NZ), range(NC)
groups_z = [[token_at(y, z, c) for z in all_z] for y in all_y for c in all_c]
groups_z4 = [
    [token_at(y, half + z, c) for z in range(4)] for half in (0, 4) for y in all_y for c in all_c
]
pairs_c = [(token_at(y, z, c), token_at(y, z, 1 - c)) for y in all_y for z in all_z for c in all_c]
groups_yc = [[token_at(y, z, c) for c in all_c for y in all_y] for z in all_z]
pairs_z4 = [(token_at(y, z, c), token_at(y, z ^ 4, c)) for y in all_y for z in all_z for c in all_c]
groups_x = [[head_at(x, z) for x in range(NX)] for z in range(NZH)]
pairs_zh = [(head_at(x, z), head_at(x, 1 - z)) for x in range(NX) for z in range(NZH)]


def pairs_x(flip):
    return [(head_at(x, z), head_at(x ^ flip, z)) for x in range(NX) for z in range(NZH)]


def exchanged(parts, axis, groups):
    return lax.all_to_all(parts, axis, 0, 0, tiled=True, axis_index_groups=groups)


def gathered(value, axis, groups):
    copies = jnp.broadcast_to(value[None], (len(groups[0]), *value.shape))
    return exchanged(copies, axis, groups)


def diagonal(rows, lanes):
    return lax.broadcasted_iota(jnp.int32, (rows, lanes), 0) == lax.broadcasted_iota(
        jnp.int32, (rows, lanes), 1
    )


def as_row(column, lanes=128):
    return jnp.sum(jnp.where(diagonal(column.shape[0], lanes), column, 0.0), axis=0, keepdims=True)


def as_column(row, rows):
    return jnp.sum(jnp.where(diagonal(rows, row.shape[1]), row, 0.0), axis=1, keepdims=True)


def call(kernel, out_shape, flops=0, moved=0):
    return pl.pallas_call(
        kernel,
        out_shape=out_shape,
        compiler_params=pltpu.CompilerParams(vmem_limit_bytes=VMEM),
        cost_estimate=pl.CostEstimate(flops=flops, bytes_accessed=moved, transcendentals=0),
    )


def score_kernel(limit_ref, q_ref, k_ref, e_ref, m_ref, l_ref):
    block = e_ref.shape[0] // NYC
    key = lax.broadcasted_iota(jnp.int32, (1, e_ref.shape[1]), 1)
    k = k_ref[...]
    for b in range(NYC):
        lines = slice(b * block, (b + 1) * block)
        s = jnp.dot(q_ref[lines], k, preferred_element_type=f32) * softmax_scale
        s = jnp.where(key <= limit_ref[lines], s, masked_value)
        m = jnp.max(s, axis=1, keepdims=True)
        e = jnp.exp(s - m)
        e_ref[lines] = e
        m_ref[b : b + 1] = as_row(m)
        l_ref[b : b + 1] = as_row(jnp.sum(e, axis=1, keepdims=True))


def message_parts(one_ref, two_ref, tokens, heads):
    rows = tokens * heads

    def weights(ref):
        block = ref[rows:, :].astype(f32)
        return block[:, :heads] + block[:, heads : 2 * heads] + block[:, 2 * heads : 3 * heads]

    iq = jnp.concatenate([one_ref[:rows, :], two_ref[:rows, :]])
    return iq, [w[:, j : j + 1] for w in (weights(one_ref), weights(two_ref)) for j in range(heads)]


def index_dot(iq, ik):
    return lax.dot_general(iq, ik, (((1,), (1,)), ((), ())), preferred_element_type=f32)


def logits_kernel(heads, scale, one_ref, two_ref, ik_ref, *refs):
    before, out_ref = refs[:-1], refs[-1]
    tokens = out_ref.shape[0]
    logits = before[0][...] if before else jnp.zeros(out_ref.shape, f32)
    iq, weights = message_parts(one_ref.at[0], two_ref.at[0], tokens, heads)
    active = index_dot(iq, ik_ref[...])
    for j, w in enumerate(weights):
        here = active[j * tokens : (j + 1) * tokens] * scale
        logits = logits + w * jnp.maximum(here, 0.0)
    out_ref[...] = logits


def index_stats_kernel(limit_ref, max_ref, total_ref, *refs):
    pieces, (logits_ref, stat_ref) = refs[:-2], refs[-2:]
    logits = sum(piece[...] for piece in pieces)
    key = lax.broadcasted_iota(jnp.int32, (1, logits.shape[1]), 1)
    logits = jnp.where(key <= limit_ref[...], logits, masked_value)
    m = jnp.max(logits, axis=1, keepdims=True)
    l = jnp.sum(jnp.exp(logits - m), axis=1, keepdims=True)
    logits_ref[...] = logits
    index_lines = [as_row(m), as_row(l), jnp.zeros((6, 128), f32)]
    lines = jnp.concatenate([max_ref[...], total_ref[...], *index_lines], axis=0)
    stat_ref[...] = jnp.broadcast_to(lines[None], stat_ref.shape)


def joined(stats):
    def one(m, l):
        top = jnp.max(m, axis=0)
        return top, jnp.sum(l * jnp.exp(m - top), axis=0)

    return (*one(stats[:, 0:8], stats[:, 8:16]), *one(stats[:, 16:17], stats[:, 17:18]))


def join_kernel(stats_ref, out_ref):
    lines = jnp.concatenate([*joined(stats_ref[...]), jnp.zeros((6, 128), f32)], axis=0)
    out_ref[...] = jnp.broadcast_to(lines[None], out_ref.shape)


def target_kernel(stats_ref, m_ref, e_ref, out_ref):
    top, total, _, _ = joined(stats_ref[...])
    weights = jnp.exp(m_ref[...] - top) / total
    keys = out_ref.shape[1]
    block = e_ref.shape[0] // NYC
    for b in range(NYC):
        e = e_ref[b * block : (b + 1) * block] * as_column(weights[b : b + 1], block)
        out_ref[b * NZ : (b + 1) * NZ] = jnp.sum(e.reshape(NZ, block // NZ, keys), axis=1)


def dlogit_kernel(one_ref, two_ref, logits_ref, stats_ref, out_ref):
    rows = logits_ref.shape[0]
    _, _, top, total = joined(stats_ref[...])
    probs = jnp.exp(logits_ref[...] - as_column(top, rows)) / as_column(total, rows)
    dlogit = GRAD_SCALE * (probs - (one_ref[...] + two_ref[...]) / H)
    out_ref[...] = jnp.broadcast_to(dlogit[None], out_ref.shape)


def grad_kernel(heads, scale, d_ref, message_ref, ik_ref, out_ref):
    dlogit = d_ref[...]
    tokens = dlogit.shape[0]
    iq, weights = message_parts(message_ref.at[0], message_ref.at[1], tokens, heads)
    ik = ik_ref[...]
    active = index_dot(iq, ik)
    heads = len(weights)
    row = lax.broadcasted_iota(jnp.int32, (tokens, 128), 0)
    place = row // NZ % NY * (NC * NZ) + row % NZ * NC + row // (NY * NZ)
    places = place == lax.broadcasted_iota(jnp.int32, (tokens, 128), 1)
    out_ref[tokens * heads :, :] = jnp.zeros((out_ref.shape[0] - tokens * heads, 128), f32)
    for j, w in enumerate(weights):
        here = active[j * tokens : (j + 1) * tokens]
        gate = jnp.where(here > 0.0, dlogit * w, 0.0).astype(bf16)
        grad = jnp.dot(gate, ik, preferred_element_type=f32) * scale
        for b in range(NYC):
            first = b % NY * (NZ * NC) + b // NY
            lines = pl.ds(first * heads + j, NZ, stride=NC * heads)
            out_ref[lines, :] = grad[b * NZ : (b + 1) * NZ]
        weight_grad = jnp.sum(dlogit * jnp.maximum(here * scale, 0.0), axis=1, keepdims=True)
        out_ref[tokens * heads + j : tokens * heads + j + 1, :] = jnp.sum(
            jnp.where(places, weight_grad, 0.0), axis=0, keepdims=True
        )


def key_kernel(heads, scale, d_ref, ik_ref, message, *refs):
    before, out_ref = refs[:-1], refs[-1]
    dlogit, ik = d_ref[...], ik_ref[...]
    tokens, keys = dlogit.shape
    total = jnp.zeros((ik.shape[1], keys), f32)
    for part in range(0, message.shape[0], 2):
        iq, weights = message_parts(message.at[part], message.at[part + 1], tokens, heads)
        active = index_dot(iq, ik)
        gates = []
        for j, w in enumerate(weights):
            here = active[j * tokens : (j + 1) * tokens]
            gates.append(jnp.where(here > 0.0, dlogit * w, 0.0).astype(bf16))
        gate = jnp.concatenate(gates, axis=0)
        total = total + jnp.dot(iq.T, gate, preferred_element_type=f32)
    grad = total.T * scale
    out_ref[...] = before[0][...] + grad if before else grad


def sum_kernel(parts_ref, out_ref):
    out_ref[...] = jnp.broadcast_to(jnp.sum(parts_ref[...], axis=0)[None], out_ref.shape)


def pair_kernel(one_ref, two_ref, out_ref):
    out_ref[...] = jnp.broadcast_to((one_ref[...] + two_ref[...])[None], out_ref.shape)


def cut_kernel(both_ref, query_ref, weight_ref):
    lines, (rows, lanes) = query_ref.shape[0], weight_ref.shape
    query_ref[...] = both_ref[:lines]
    weight_ref[...] = both_ref[lines : lines + rows, :lanes]


def in_order(value):
    return jnp.moveaxis(value.reshape(NY, NZ, NC, *value.shape[1:]), 2, 0).reshape(value.shape)


def x_scatter(parts, x):
    pieces = [lax.dynamic_index_in_dim(parts, x ^ flip, 0, keepdims=False) for flip in range(NX)]
    return pieces[:1] + [
        lax.ppermute(pieces[flip], "heads", pairs_x(flip)) for flip in range(1, NX)
    ]


def local(queries, latent_keys, index_queries, index_keys, index_weights, positions):
    heads_here, width = queries.shape[0], queries.shape[2]
    key_count = latent_keys.shape[0]
    query_count, index_heads, index_width = index_queries.shape
    index_scale = index_width ** (-0.5)
    share_rows = query_count // NX
    shape = jax.ShapeDtypeStruct
    x = lax.axis_index("heads") // NZH
    core = lax.axis_index("tokens") % NC
    limit = in_order(positions - lax.axis_index("tokens") * key_count)

    along_z = gathered(queries.reshape(heads_here, width), "tokens", groups_z)

    high = lax.reduce_precision(index_weights, 8, 7)
    middle = lax.reduce_precision(index_weights - high, 8, 7)
    low = index_weights - high - middle
    half = index_heads // NC
    lines = jnp.stack([high, middle, low], axis=1).reshape(query_count, 3, NC, half)
    lines = in_order(lines.transpose(0, 2, 1, 3).reshape(query_count, NC, 3 * half))
    lines = jnp.pad(lines.transpose(1, 0, 2), ((0, 0), (0, 0), (0, 128 - 3 * half)))
    by_head = in_order(index_queries).transpose(1, 0, 2)
    by_head = by_head.reshape(NC, half * query_count, index_width)
    mine = jnp.concatenate([by_head, lines.astype(bf16)], axis=1)

    first = lax.ppermute(lax.dynamic_index_in_dim(mine, core, 0), "heads", pairs_zh)
    index_flops = 2 * query_count * index_heads * key_count * index_width
    own = call(
        lambda *refs: logits_kernel(half, index_scale, *refs),
        shape((query_count, key_count), f32),
        flops=index_flops,
        moved=1 << 20,
    )(mine[:1], mine[1:], index_keys)
    first, own = lax.optimization_barrier((first, own))
    second = lax.ppermute(first, "tokens", pairs_c)

    partial = call(
        lambda *refs: logits_kernel(half, index_scale, *refs),
        shape((query_count, key_count), f32),
        flops=WEIGHT * index_flops,
        moved=1 << 20,
    )(first, second, index_keys, own)
    pieces = x_scatter(partial.reshape(NX, share_rows, key_count), x)
    rows = gathered(along_z, "tokens", groups_yc).reshape(-1, width)
    row_count = rows.shape[0]
    lines_shape = shape((NYC, row_count // NYC), f32)
    exponent, local_max, local_total = call(
        score_kernel,
        (shape((row_count, key_count), f32), lines_shape, lines_shape),
        flops=2 * row_count * key_count * width,
        moved=4 << 20,
    )(jnp.repeat(limit, heads_here)[:, None], rows, latent_keys.T)

    local_max, *pieces = lax.optimization_barrier((local_max, *pieces))
    share_limit = lax.dynamic_slice_in_dim(limit, x * share_rows, share_rows, 0)
    logits, stats = call(
        index_stats_kernel,
        (shape((share_rows, key_count), f32), shape((NZ, 2 * NYC + 8, 128), f32)),
        flops=index_flops,
        moved=1 << 20,
    )(share_limit[:, None], local_max, local_total, *pieces)

    stats = exchanged(stats, "tokens", groups_z)
    stats = call(join_kernel, shape((NYC, *stats.shape[1:]), f32))(stats)
    stats = exchanged(stats, "tokens", groups_yc)

    partial = call(target_kernel, shape((query_count, key_count), f32), moved=5 << 20)(
        stats, local_max, exponent
    )

    over_x = exchanged(partial.reshape(NX, share_rows, key_count), "heads", groups_x).sum(axis=0)
    other = lax.ppermute(over_x, "heads", pairs_zh)
    dlogit = call(dlogit_kernel, shape((NX, share_rows, key_count), f32))(
        over_x, other, logits, stats
    )
    dlogit, *three = lax.optimization_barrier((dlogit, mine, first, second))
    four = jnp.concatenate(three)
    near = lax.ppermute(four, "heads", pairs_x(1))
    dlogit = exchanged(dlogit, "heads", groups_x).reshape(query_count, key_count)
    query_lines = query_count * index_heads
    piece_rows = -(-(query_lines + index_heads) // (NYC * 8)) * 8
    both = call(
        lambda *refs: grad_kernel(half, index_scale, *refs),
        shape((piece_rows * NYC, 128), f32),
        flops=2 * index_flops,
        moved=2 << 20,
    )(dlogit, mine, index_keys)

    piece = exchanged(both.reshape(NYC, piece_rows, 128), "tokens", groups_yc)
    eight = jnp.concatenate([four, near])
    far = lax.ppermute(eight, "heads", pairs_x(2))
    piece = call(sum_kernel, shape((NZ // 2, piece_rows, 128), f32))(piece)
    piece = exchanged(piece, "tokens", groups_z4).sum(axis=0)
    other = lax.ppermute(piece, "tokens", pairs_z4)
    piece = call(pair_kernel, shape((NYC, piece_rows, 128), f32))(piece, other)
    both = exchanged(piece, "tokens", groups_yc).reshape(-1, 128)
    query_grad, weight_grad = call(
        cut_kernel, (shape((query_lines, 128), f32), shape((index_heads, query_count), f32))
    )(both)
    query_grad = query_grad.reshape(query_count, index_heads, index_width)
    weight_grad = weight_grad.T

    key_flops = index_flops * NX * NZH
    key_grad = ()
    for message in (eight, far):
        key_grad = call(
            lambda *refs: key_kernel(half, index_scale, *refs),
            shape((key_count, index_width), f32),
            flops=key_flops,
            moved=2 << 20,
        )(dlogit, index_keys, message, *key_grad),
    return (query_grad, weight_grad, *key_grad)


def solution(mesh):
    placed = (
        P("heads", "tokens", None),
        P("tokens", None),
        P(None, "heads", None),
        P("tokens", None),
        P(None, "heads"),
        P(),
    )
    return jax.shard_map(
        local,
        mesh=mesh,
        in_specs=placed,
        out_specs=(P(None, "heads", None), P(None, "heads"), P("tokens", None)),
        check_vma=False,
    )
```
